32 devices in a mesh: seq: 4 (over z), tok: 8 (over y, x, core).
Axes of the slice: x: 2, y: 2, z: 4, core: 2. Of those that a mesh axis runs over, the one named last changes fastest.
Arguments:
- layer_input: bfloat16 [32, 1024, 768], P('seq', 'tok'), may hold values from -6 to 6
- norm_gain: float32 [768], replicated, may hold values from 0.25 to 1.75
- weight_in: bfloat16 [768, 5376], replicated, may hold values from -0.21875 to 0.21875
- bias_in: float32 [3072], replicated, may hold values from -3 to 3
- query_gain: float32 [768], replicated, may hold values from 0.25 to 1.75
- key_gain: float32 [768], replicated, may hold values from 0.25 to 1.75
- weight_attn: bfloat16 [768, 768], replicated, may hold values from -2.5 to 2.5
- weight_down: bfloat16 [3072, 768], replicated, may hold values from -0.109375 to 0.109375
- bias_down: float32 [768], replicated, may hold values from -2 to 2
- image_ids: int32 [32, 1024], P('seq', 'tok'), may hold values from -1 to 15, as said below
- cotangent: bfloat16 [32, 1024, 768], P('seq', 'tok'), may hold values from -6 to 6
Outputs:
- layer_output: bfloat16 [32, 1024, 768], P('seq', 'tok')
- grad_input: float32 [32, 1024, 768], P('seq', 'tok')
- grad_weights: float32 [7084032], P(('seq', 'tok'))
The draws below stay inside these ranges and needn't reach their ends.
Inputs may be any that keep to these rules, and one draw needn't show every extreme that they name: `image_ids`: within a sequence an image's slots are contiguous and ids count its images from 0 upward; padding slots, at its end, hold -1.
All inputs are finite; a program needn't handle non-finite values.
Results may differ from the reference program's by a relative error of at most 0.0096.
Values may be sent and summed in bfloat16 or wider, within the bound.
No kernel may reach another device: no remote copies, remote signals or barrier semaphores. Data moves between devices by JAX's collectives and lax.ppermute only.
A program may use at most 256 MiB of HBM per device.

```python
import math
import jax
import jax.numpy as jnp
from jax import lax

D = 768
HEADS = 12
HD = 64
FF = 3072
SEQS_DEV = 8
LEN = 1024
SEQS = 32


def draw_image_ids(key, part):
    key = jax.random.fold_in(key, 7)
    key_start, key_pad, key_whole, key_many = jax.random.split(key, 4)
    positions = jnp.arange(LEN, dtype=jnp.int32)[None, :]
    new_image = (jax.random.randint(key_start, (SEQS, LEN), 0, LEN) < 8).astype(jnp.int32)
    seq_index = jnp.arange(SEQS, dtype=jnp.int32)[:, None]
    chosen = jnp.repeat(jax.random.randint(key_whole, (SEQS // SEQS_DEV, 1), 0, SEQS_DEV), SEQS_DEV, axis=0)
    offset = jnp.repeat(jax.random.randint(key_many, (SEQS // SEQS_DEV, 1), 1, SEQS_DEV), SEQS_DEV, axis=0)
    many_seq = seq_index % SEQS_DEV == (chosen + offset) % SEQS_DEV
    forced = (positions % (LEN // 32) == 0).astype(jnp.int32)
    new_image = jnp.where(many_seq, jnp.maximum(new_image, forced), new_image)
    new_image = jnp.where(positions == 0, 0, new_image)
    slot_ids = jnp.minimum(jnp.cumsum(new_image, axis=1), 15).astype(jnp.int32)
    padding = jax.random.randint(key_pad, (SEQS, 1), 1, LEN // 8 + 1)
    slot_ids = jnp.where(positions >= LEN - padding, -1, slot_ids)
    whole_seq = seq_index % SEQS_DEV == chosen
    return jnp.where(whole_seq, 0, slot_ids).astype(jnp.int32)


def levels(rng, extent, shards, low, top_value):
    factor_of = 1.0
    for position, shards_of in shards:
        steps = jax.random.uniform(jax.random.fold_in(jax.random.fold_in(rng, 6), position), (shards_of,), jnp.float32, low / len(shards), top_value / len(shards))
        factor_of = factor_of * jnp.repeat(jnp.exp(steps), extent[position] // shards_of).reshape((-1,) + (1,) * (len(extent) - 1 - position))
    return factor_of


def centred(rng, dims, width, limit, cuts=(), held_as=jnp.bfloat16):
    values = width * jax.random.normal(rng, dims, jnp.float32)
    if cuts:
        values = values * levels(rng, dims, cuts, -0.22, 0.18)
    return jnp.clip(values, -limit, limit).astype(held_as)


def setup_inputs(seed: int = 0) -> dict:
    streams_of = jax.random.split(jax.random.key(seed), 12)
    return {
        "layer_input": centred(streams_of[0], (SEQS, LEN, D), 1.0, 6.0, ((0, 4), (1, 8))),
        "norm_gain": jnp.clip(1.0 + 0.15 * jax.random.normal(streams_of[1], (D,), jnp.float32), 0.25, 1.75),
        "weight_in": centred(streams_of[2], (D, 3 * D + FF), D ** -0.5, 0.21875),
        "bias_in": centred(streams_of[3], (FF,), 0.5, 3.0, (), jnp.float32),
        "query_gain": jnp.clip(1.0 + 0.15 * jax.random.normal(streams_of[4], (D,), jnp.float32), 0.25, 1.75),
        "key_gain": jnp.clip(1.0 + 0.15 * jax.random.normal(streams_of[5], (D,), jnp.float32), 0.25, 1.75),
        "weight_attn": centred(streams_of[6], (D, D), (max(D // 128, 2)) ** -0.5, 2.5),
        "weight_down": centred(streams_of[7], (FF, D), FF ** -0.5, 0.109375),
        "bias_down": centred(streams_of[8], (D,), 0.3, 2.0, (), jnp.float32),
        "image_ids": draw_image_ids(jax.random.fold_in(streams_of[11], 71), 0),
        "cotangent": centred(streams_of[10], (SEQS, LEN, D), 1.0, 6.0, ((0, 4), (1, 8))),
    }


EPS = 1e-06
NEG = -1e+30

@jax.custom_vjp
def low(v):
    return lax.optimization_barrier(v.astype(jnp.bfloat16)).astype(jnp.float32)

@jax.custom_vjp
def low_back(v):
    return v

def low_keep(v):
    return (low(v), None)

def low_pass(kept, grad):
    return (grad,)

def back_keep(v):
    return (v, None)

def back_low(kept, grad):
    return (low(grad),)
low.defvjp(low_keep, low_pass)
low_back.defvjp(back_keep, back_low)

def layer_norm(values, scaling):
    average = lax.optimization_barrier(jnp.mean(values, axis=-1, keepdims=True))
    shifted = values - average
    spread = lax.optimization_barrier(jnp.mean(shifted * shifted, axis=-1, keepdims=True))
    return shifted * lax.rsqrt(spread + EPS) * scaling

def attend_group(packed):
    query_heads, key_heads, value_heads, slot_ids = packed
    highest_precision = lax.Precision.HIGHEST
    scores = jnp.einsum('glhc,gmhc->ghlm', query_heads, key_heads, precision=highest_precision) * HD ** (-0.5)
    scores = low_back(scores)
    allowed = slot_ids[:, None, :, None] == slot_ids[:, None, None, :]
    scores = jnp.where(allowed, scores, NEG)
    row_max = lax.optimization_barrier(jnp.max(scores, axis=-1, keepdims=True))
    shifted = jnp.exp(scores - row_max)
    weights = low(shifted / lax.optimization_barrier(jnp.sum(shifted, axis=-1, keepdims=True)))
    return jnp.einsum('ghlm,gmhc->glhc', weights, value_heads, precision=highest_precision)

def attention(query_heads, key_heads, value_heads, image_ids):
    group_size = math.gcd(SEQS, max(1, 4096 // LEN))
    step_count = SEQS // group_size
    packed = tuple((tensor.reshape((step_count, group_size) + tensor.shape[1:]) for tensor in (query_heads, key_heads, value_heads, image_ids)))
    result = lax.map(jax.checkpoint(attend_group), packed)
    return result.reshape(query_heads.shape)

def reference(layer_input, norm_gain, weight_in, bias_in, query_gain, key_gain, weight_attn, weight_down, bias_down, image_ids, cotangent):
    highest_precision = lax.Precision.HIGHEST

    def forward(input_full, norm_scaling, input_projection, bias_hidden, query_scaling, key_scaling, attention_projection, proj_down, bias_out):
        normalized_rows = low(layer_norm(input_full, norm_scaling))
        projected_rows = low_back(jnp.einsum('gcn,ni->gci', normalized_rows, input_projection, precision=highest_precision))
        query_raw = projected_rows[..., :D].reshape(SEQS, LEN, HEADS, HD)
        key_raw = projected_rows[..., D:2 * D].reshape(SEQS, LEN, HEADS, HD)
        value_heads = low(low_back(projected_rows[..., 2 * D:3 * D])).reshape(SEQS, LEN, HEADS, HD)
        hidden_in = projected_rows[..., 3 * D:] + bias_hidden
        query_heads = low(low_back(layer_norm(query_raw, query_scaling.reshape(HEADS, HD))))
        key_heads = low(low_back(layer_norm(key_raw, key_scaling.reshape(HEADS, HD))))
        attention_output = attention(query_heads, key_heads, value_heads, image_ids).reshape(SEQS, LEN, D)
        attention_output = low(low_back(attention_output))
        activation = low(jax.nn.gelu(hidden_in, approximate=False))
        attention_partial = jnp.einsum('gcn,ni->gci', attention_output, attention_projection, precision=highest_precision)
        down_part = jnp.einsum('slf,fe->sle', activation, proj_down, precision=highest_precision)
        return input_full + attention_partial + down_part + bias_out
    primals = (layer_input.astype(jnp.float32), norm_gain, weight_in.astype(jnp.float32), bias_in, query_gain, key_gain, weight_attn.astype(jnp.float32), weight_down.astype(jnp.float32), bias_down)
    result, pullback = jax.vjp(forward, *primals)
    gradients = pullback(cotangent.astype(jnp.float32))
    grad_weights = jnp.concatenate([tensor.reshape(-1) for tensor in gradients[1:]])
    return (result.astype(jnp.bfloat16), gradients[0], grad_weights)
```

```python
from functools import partial

import jax
import jax.numpy as jnp
from jax import lax
from jax.experimental import pallas as pl
from jax.experimental.pallas import tpu as pltpu
from jax.sharding import PartitionSpec as P

HEADS = 12


EPS = 1e-06
NEG = -1e30

F32 = jnp.float32
BF16 = jnp.bfloat16
ROWS = 256
HEAD_DIM = 64
PAIR = 2 * HEAD_DIM
FAR = 192.0
VMEM_LIMIT = 60 * 1024 * 1024


def layer_norm(values, scaling):
    average = jnp.mean(values, axis=-1, keepdims=True)
    shifted = values - average
    spread = jnp.mean(shifted * shifted, axis=-1, keepdims=True)
    return shifted * lax.rsqrt(spread + EPS) * scaling


def head_norms(query_raw, key_raw, gain_query, gain_key):
    return (layer_norm(query_raw, gain_query), layer_norm(key_raw, gain_key))


def to_units(row_values, seq_count, head_count):
    part_len = row_values.shape[0] // seq_count
    shaped = row_values.reshape(seq_count, part_len, head_count, -1).transpose(0, 2, 3, 1)
    return shaped.reshape(seq_count * head_count, -1, part_len)


def from_units(unit_values, seq_count, head_count):
    part_len = unit_values.shape[2]
    shaped = unit_values.reshape(seq_count, head_count, -1, part_len).transpose(0, 3, 1, 2)
    return shaped.reshape(seq_count * part_len, -1)


def block_scores(query_block, key_unit, image_block, slot_ids, score_scale):
    scores = (
        lax.dot_general(
            query_block, key_unit, (((0,), (0,)), ((), ())), preferred_element_type=jnp.float32
        )
        * score_scale
    )
    allowed = image_block[:, None] == slot_ids[None, :]
    return (scores, allowed)


def split_blocks(unit_values, block_len):
    head_dim, length = unit_values.shape
    return unit_values.reshape(head_dim, length // block_len, block_len).transpose(1, 0, 2)


def attend_unit(packed, score_scale):
    query_unit, key_unit, value_unit, slot_ids = packed
    head_dim, length = query_unit.shape
    block_len = min(512, length)
    query_blocks = split_blocks(query_unit, block_len)
    image_blocks = slot_ids.reshape(length // block_len, block_len)

    def one_block(inputs):
        query_block, image_block = inputs
        scores, allowed = block_scores(query_block, key_unit, image_block, slot_ids, score_scale)
        scores = jnp.where(allowed, scores, NEG)
        row_max = jnp.max(scores, axis=-1, keepdims=True)
        shifted = jnp.exp(scores - row_max)
        row_total = jnp.sum(shifted, axis=-1, keepdims=True)
        weights = (shifted / row_total).astype(jnp.bfloat16)
        outputs = lax.dot_general(
            value_unit, weights, (((1,), (1,)), ((), ())), preferred_element_type=jnp.float32
        )
        return (outputs, row_max[:, 0] + jnp.log(row_total[:, 0]))

    outputs, log_total = lax.map(one_block, (query_blocks, image_blocks))
    return (outputs.transpose(1, 0, 2).reshape(head_dim, length), log_total.reshape(length))


def attend_back(packed, score_scale):
    query_unit, key_unit, value_unit, grad_unit, log_total, slot_ids = packed
    head_dim, length = query_unit.shape
    block_len = min(512, length)
    query_blocks = split_blocks(query_unit, block_len)
    grad_blocks = split_blocks(grad_unit, block_len)
    total_blocks = log_total.reshape(length // block_len, block_len)
    image_blocks = slot_ids.reshape(length // block_len, block_len)

    def one_block(carried, inputs):
        grad_key, grad_value = carried
        query_block, grad_block, total_block, image_block = inputs
        scores, allowed = block_scores(query_block, key_unit, image_block, slot_ids, score_scale)
        weights = jnp.where(allowed, jnp.exp(scores - total_block[:, None]), 0.0)
        weights_low = weights.astype(jnp.bfloat16)
        grad_weights = lax.dot_general(
            grad_block, value_unit, (((0,), (0,)), ((), ())), preferred_element_type=jnp.float32
        )
        inner = jnp.sum(weights * grad_weights, axis=-1, keepdims=True)
        grad_scores = (weights * (grad_weights - inner)).astype(jnp.bfloat16)
        grad_query = score_scale * lax.dot_general(
            key_unit, grad_scores, (((1,), (1,)), ((), ())), preferred_element_type=jnp.float32
        )
        grad_key = grad_key + score_scale * lax.dot_general(
            query_block, grad_scores, (((1,), (0,)), ((), ())), preferred_element_type=jnp.float32
        )
        grad_value = grad_value + lax.dot_general(
            grad_block, weights_low, (((1,), (0,)), ((), ())), preferred_element_type=jnp.float32
        )
        return ((grad_key, grad_value), grad_query)

    blank = jnp.zeros((head_dim, length), jnp.float32)
    (grad_key, grad_value), grad_query = lax.scan(
        one_block, (blank, blank), (query_blocks, grad_blocks, total_blocks, image_blocks)
    )
    return (grad_query.transpose(1, 0, 2).reshape(head_dim, length), grad_key, grad_value)


def reduce_grads(flat_grad):
    return lax.psum_scatter(flat_grad, ("seq", "tok"), scatter_dimension=0, tiled=True)


def units_device(
    layer_input,
    norm_gain,
    weight_in,
    bias_in,
    query_gain,
    key_gain,
    weight_attn,
    weight_down,
    bias_down,
    image_ids,
    cotangent,
):
    seq_count, part_len, model_width = layer_input.shape
    row_count = seq_count * part_len
    head_count = HEADS
    head_dim = model_width // head_count
    score_scale = head_dim ** (-0.5)
    whole_ids = lax.all_gather(image_ids, "tok", axis=1, tiled=True)
    unit_count = seq_count * head_count // lax.axis_size("tok")
    first_unit = lax.axis_index("tok") * unit_count
    unit_seq = (first_unit + jnp.arange(unit_count, dtype=jnp.int32)) // head_count
    unit_ids = jnp.take(whole_ids, unit_seq, axis=0)
    input_rows = layer_input.reshape(row_count, model_width).astype(jnp.float32)
    normalized_rows, input_back = jax.vjp(layer_norm, input_rows, norm_gain)
    normed_low = normalized_rows.astype(jnp.bfloat16)
    projected_rows = jnp.dot(normed_low, weight_in, preferred_element_type=jnp.float32)
    query_raw = projected_rows[:, :model_width].reshape(row_count, head_count, head_dim)
    key_raw = projected_rows[:, model_width : 2 * model_width].reshape(
        row_count, head_count, head_dim
    )
    value_low = projected_rows[:, 2 * model_width : 3 * model_width].astype(jnp.bfloat16)
    hidden_in = projected_rows[:, 3 * model_width :] + bias_in
    gain_query = query_gain.reshape(head_count, head_dim)
    gain_key = key_gain.reshape(head_count, head_dim)
    (query_normed, key_normed), heads_back = jax.vjp(
        head_norms, query_raw, key_raw, gain_query, gain_key
    )
    outgoing = (
        to_units(
            query_normed.reshape(row_count, model_width).astype(jnp.bfloat16), seq_count, head_count
        ),
        to_units(
            key_normed.reshape(row_count, model_width).astype(jnp.bfloat16), seq_count, head_count
        ),
        to_units(value_low, seq_count, head_count),
    )
    query_units, key_units, value_units = (
        lax.all_to_all(outgoing[0], "tok", split_axis=0, concat_axis=2, tiled=True),
        lax.all_to_all(outgoing[1], "tok", split_axis=0, concat_axis=2, tiled=True),
        lax.all_to_all(outgoing[2], "tok", split_axis=0, concat_axis=2, tiled=True),
    )
    attention_output, log_total = lax.map(
        partial(attend_unit, score_scale=score_scale),
        (query_units, key_units, value_units, unit_ids),
    )
    returned = lax.all_to_all(
        attention_output.astype(jnp.bfloat16), "tok", split_axis=2, concat_axis=0, tiled=True
    )
    attn_rows = from_units(returned, seq_count, head_count)
    activation, gelu_back = jax.vjp(partial(jax.nn.gelu, approximate=False), hidden_in)
    act_low = activation.astype(jnp.bfloat16)
    result_rows = input_rows + jnp.dot(attn_rows, weight_attn, preferred_element_type=jnp.float32)
    result_rows = (
        result_rows + jnp.dot(act_low, weight_down, preferred_element_type=jnp.float32) + bias_down
    )
    layer_output = result_rows.astype(jnp.bfloat16).reshape(seq_count, part_len, model_width)
    grad_rows = cotangent.reshape(row_count, model_width)
    grad_full = grad_rows.astype(jnp.float32)
    contract_rows = (((0,), (0,)), ((), ()))
    contract_cols = (((1,), (1,)), ((), ()))
    grad_bias_down = jnp.sum(grad_full, axis=0)
    grad_weight_down = lax.dot_general(
        act_low, grad_rows, contract_rows, preferred_element_type=jnp.float32
    )
    grad_weight_attn = lax.dot_general(
        attn_rows, grad_rows, contract_rows, preferred_element_type=jnp.float32
    )
    grad_activation = lax.dot_general(
        grad_rows, weight_down, contract_cols, preferred_element_type=jnp.float32
    )
    grad_hidden = gelu_back(grad_activation)[0]
    grad_bias_in = jnp.sum(grad_hidden, axis=0)
    grad_attended = lax.dot_general(
        grad_rows, weight_attn, contract_cols, preferred_element_type=jnp.float32
    )
    grad_units = lax.all_to_all(
        to_units(grad_attended.astype(jnp.bfloat16), seq_count, head_count),
        "tok",
        split_axis=0,
        concat_axis=2,
        tiled=True,
    )
    grad_query_u, grad_key_u, grad_value_u = lax.map(
        partial(attend_back, score_scale=score_scale),
        (query_units, key_units, value_units, grad_units, log_total, unit_ids),
    )
    back_query, back_key, back_value = (
        lax.all_to_all(
            grad_query_u.astype(jnp.bfloat16), "tok", split_axis=2, concat_axis=0, tiled=True
        ),
        lax.all_to_all(
            grad_key_u.astype(jnp.bfloat16), "tok", split_axis=2, concat_axis=0, tiled=True
        ),
        lax.all_to_all(
            grad_value_u.astype(jnp.bfloat16), "tok", split_axis=2, concat_axis=0, tiled=True
        ),
    )
    grad_query_n = (
        from_units(back_query, seq_count, head_count)
        .astype(jnp.float32)
        .reshape(row_count, head_count, head_dim)
    )
    grad_key_n = (
        from_units(back_key, seq_count, head_count)
        .astype(jnp.float32)
        .reshape(row_count, head_count, head_dim)
    )
    grad_value_rows = from_units(back_value, seq_count, head_count).astype(jnp.float32)
    grad_query_raw, grad_key_raw, grad_gain_query, grad_gain_key = heads_back(
        (grad_query_n, grad_key_n)
    )
    grad_projected = jnp.concatenate(
        [
            grad_query_raw.reshape(row_count, model_width),
            grad_key_raw.reshape(row_count, model_width),
            grad_value_rows,
            grad_hidden,
        ],
        axis=1,
    ).astype(jnp.bfloat16)
    grad_weight_in = lax.dot_general(
        normed_low, grad_projected, contract_rows, preferred_element_type=jnp.float32
    )
    grad_normed = lax.dot_general(
        grad_projected, weight_in, contract_cols, preferred_element_type=jnp.float32
    )
    grad_input_rows, grad_norm_gain = input_back(grad_normed)
    grad_input = (grad_full + grad_input_rows).reshape(seq_count, part_len, model_width)
    pieces = [
        grad_norm_gain,
        grad_weight_in,
        grad_bias_in,
        grad_gain_query,
        grad_gain_key,
        grad_weight_attn,
        grad_weight_down,
        grad_bias_down,
    ]
    flat_grad = jnp.concatenate([tensor.reshape(-1) for tensor in pieces])
    grad_weights = reduce_grads(flat_grad)
    return (layer_output, grad_input, grad_weights)


def dot(left, right):
    return jnp.dot(left, right, preferred_element_type=F32)


def dot_nt(left, right):
    return lax.dot_general(left, right, (((1,), (1,)), ((), ())), preferred_element_type=F32)


def dot_tn(left, right):
    return lax.dot_general(left, right, (((0,), (0,)), ((), ())), preferred_element_type=F32)


def standardize(rows):
    shifted = rows - jnp.mean(rows, axis=-1, keepdims=True)
    scale = lax.rsqrt(jnp.mean(shifted * shifted, axis=-1, keepdims=True) + EPS)
    return shifted * scale, scale


def head_means(values):
    width = 4 * HEAD_DIM
    row = lax.broadcasted_iota(jnp.int32, (width, width), 0)
    column = lax.broadcasted_iota(jnp.int32, (width, width), 1)
    ones = jnp.where((row >> 6) == (column >> 6), 1.0, 0.0).astype(BF16)
    high = values.astype(BF16)
    rest = (values - high.astype(F32)).astype(BF16)
    parts = []
    for start in range(0, values.shape[1], width):
        part = slice(start, start + width)
        parts.append(dot(high[:, part], ones) + dot(rest[:, part], ones))
    return jnp.concatenate(parts, axis=1) * (1.0 / HEAD_DIM)


def head_standardize(raw):
    shifted = raw - head_means(raw)
    scale = lax.rsqrt(head_means(shifted * shifted) + EPS)
    return shifted * scale, scale


def gelu_pair(pre):
    phi = 0.5 + 0.5 * lax.erf(pre * (0.5**0.5))
    density = jnp.exp(-0.5 * pre * pre) * 0.3989422804014327
    return pre * phi, phi + pre * density


def mlp_kernel(
    x_ref, g_ref, gain_ref, wh_ref, bias_ref, wd_ref,
    out_ref, dn_ref, gwh_ref, gwd_ref, gb_ref, gbd_ref, gng_ref,
    norm_ref, flip_ref, act_ref, dh_ref,
):
    step = pl.program_id(0)
    count = x_ref.shape[0] // ROWS

    @pl.when(step == 0)
    def _():
        gbd_ref[...] = jnp.zeros_like(gbd_ref)

        def block(i, carry):
            rows = pl.ds(pl.multiple_of(i * ROWS, ROWS), ROWS)
            hat, _ = standardize(x_ref[rows].astype(F32))
            normed = (hat * gain_ref[...]).astype(BF16)
            norm_ref[rows] = normed
            out_ref[rows] = jnp.zeros_like(out_ref[rows])
            dn_ref[rows] = jnp.zeros_like(dn_ref[rows])
            gbd_ref[...] += jnp.sum(g_ref[rows].astype(F32), axis=0, keepdims=True)
            return carry

        lax.fori_loop(0, count, block, 0)
        flip_ref[...] = norm_ref[...].T

    def block(i, total):
        rows = pl.ds(pl.multiple_of(i * ROWS, ROWS), ROWS)
        pre = dot(norm_ref[rows], wh_ref[...]) + bias_ref[...]
        act, slope = gelu_pair(pre)
        act_low = act.astype(BF16)
        dh = dot_nt(g_ref[rows], wd_ref[...]) * slope
        dh_low = dh.astype(BF16)
        act_ref[rows] = act_low
        dh_ref[rows] = dh_low
        out_ref[rows] += dot(act_low, wd_ref[...])
        dn_ref[rows] += dot_nt(dh_low, wh_ref[...])
        return total + jnp.sum(dh, axis=0, keepdims=True)

    gb_ref[...] = lax.fori_loop(0, count, block, jnp.zeros(gb_ref.shape, F32))
    gwd_ref[...] = dot_tn(act_ref[...], g_ref[...]).astype(BF16)
    gwh_ref[...] = dot(flip_ref[...], dh_ref[...]).astype(BF16)

    @pl.when(step == pl.num_programs(0) - 1)
    def _():
        gng_ref[...] = jnp.zeros_like(gng_ref)

        def block(i, carry):
            rows = pl.ds(pl.multiple_of(i * ROWS, ROWS), ROWS)
            hat, _ = standardize(x_ref[rows].astype(F32))
            gng_ref[...] += jnp.sum(dn_ref[rows] * hat, axis=0, keepdims=True)
            return carry

        lax.fori_loop(0, count, block, 0)


def mlp(rows, grads, norm_gain, weight_in, bias_in, weight_down):
    count, width = rows.shape
    hidden = weight_down.shape[0]
    chunk = width
    skip = (weight_in.shape[1] - hidden) // chunk
    whole = lambda i: (0, 0)
    vec = jax.ShapeDtypeStruct((1, width), F32)
    return pl.pallas_call(
        mlp_kernel,
        grid=(hidden // chunk,),
        in_specs=[
            pl.BlockSpec((count, width), whole),
            pl.BlockSpec((count, width), whole),
            pl.BlockSpec((1, width), whole),
            pl.BlockSpec((width, chunk), lambda i: (0, i + skip)),
            pl.BlockSpec((1, chunk), lambda i: (0, i)),
            pl.BlockSpec((chunk, width), lambda i: (i, 0)),
        ],
        out_specs=[
            pl.BlockSpec((count, width), whole),
            pl.BlockSpec((count, width), whole),
            pl.BlockSpec((width, chunk), lambda i: (0, i)),
            pl.BlockSpec((chunk, width), lambda i: (i, 0)),
            pl.BlockSpec((1, chunk), lambda i: (0, i)),
            pl.BlockSpec((1, width), whole),
            pl.BlockSpec((1, width), whole),
        ],
        out_shape=[
            jax.ShapeDtypeStruct((count, width), F32),
            jax.ShapeDtypeStruct((count, width), F32),
            jax.ShapeDtypeStruct((width, hidden), BF16),
            jax.ShapeDtypeStruct((hidden, width), BF16),
            jax.ShapeDtypeStruct((1, hidden), F32),
            vec,
            vec,
        ],
        scratch_shapes=[
            pltpu.VMEM((count, width), BF16),
            pltpu.VMEM((width, count), BF16),
            pltpu.VMEM((count, chunk), BF16),
            pltpu.VMEM((count, chunk), BF16),
        ],
        compiler_params=pltpu.CompilerParams(vmem_limit_bytes=VMEM_LIMIT),
        cost_estimate=pl.CostEstimate(
            flops=12 * count * width * hidden, bytes_accessed=32 * 2**20, transcendentals=0
        ),
        name="mlp",
    )(rows, grads, norm_gain, weight_in, bias_in, weight_down)


def heads_kernel(
    x_ref, g_ref, gain_ref, wqkv_ref, wattn_ref, qgain_ref, kgain_ref,
    q_ref, k_ref, v_ref, do_ref, norm_ref, raw_ref,
):
    width = x_ref.shape[1]
    hat, _ = standardize(x_ref[...].astype(F32))
    normed = (hat * gain_ref[...]).astype(BF16)
    norm_ref[...] = normed
    q_raw = dot(normed, wqkv_ref[:, :width])
    raw_ref[:, :width] = q_raw
    q_ref[...] = (head_standardize(q_raw)[0] * qgain_ref[...]).astype(BF16)
    k_raw = dot(normed, wqkv_ref[:, width : 2 * width])
    raw_ref[:, width:] = k_raw
    k_ref[...] = (head_standardize(k_raw)[0] * kgain_ref[...]).astype(BF16)
    v_ref[...] = dot(normed, wqkv_ref[:, 2 * width :]).astype(BF16)
    do_ref[...] = dot_nt(g_ref[...], wattn_ref[...]).astype(BF16)


def heads(rows, grads, norm_gain, weight_in, weight_attn, query_gain, key_gain):
    count, width = rows.shape
    whole = lambda i: (0, 0)
    block = pl.BlockSpec((ROWS, width), lambda i: (i, 0))
    vec = pl.BlockSpec((1, width), whole)
    low = jax.ShapeDtypeStruct((count, width), BF16)
    return pl.pallas_call(
        heads_kernel,
        grid=(count // ROWS,),
        in_specs=[
            block,
            block,
            vec,
            pl.BlockSpec((width, 3 * width), whole),
            pl.BlockSpec((width, width), whole),
            vec,
            vec,
        ],
        out_specs=[block] * 5 + [pl.BlockSpec((ROWS, 2 * width), lambda i: (i, 0))],
        out_shape=[low] * 5 + [jax.ShapeDtypeStruct((count, 2 * width), F32)],
        compiler_params=pltpu.CompilerParams(vmem_limit_bytes=VMEM_LIMIT),
        cost_estimate=pl.CostEstimate(
            flops=8 * count * width * width, bytes_accessed=22 * 2**20, transcendentals=0
        ),
        name="heads",
    )(rows, grads, norm_gain, weight_in, weight_attn, query_gain, key_gain)


def attend_kernel(
    q_ref, k_ref, v_ref, do_ref, ids_ref,
    o_ref, dq_ref, dk_ref, dv_ref,
    ka_ref, va_ref, dka_ref, dva_ref,
):
    length = q_ref.shape[0]

    def lanes(count, head):
        lane = lax.broadcasted_iota(jnp.int32, (count, PAIR), 1)
        mine = (lane >> 6) == head
        return mine, lane - (1 - head) * HEAD_DIM

    ids = ids_ref[...] + 1
    for head in range(2):
        mine, spare = lanes(length, head)
        marks = jnp.where(spare == ids, 1.0, jnp.where(spare == 17, -FAR, 0.0))
        ka_ref[head] = jnp.where(mine, k_ref[...].astype(F32), marks).astype(BF16)
        marks = jnp.where((spare == 0) | (spare == 1), 1.0, 0.0)
        va_ref[head] = jnp.where(mine, v_ref[...].astype(F32), marks).astype(BF16)
        dka_ref[head] = jnp.zeros_like(dka_ref[head])
        dva_ref[head] = jnp.zeros_like(dva_ref[head])

    def block(i, carry):
        rows = pl.ds(pl.multiple_of(i * ROWS, ROWS), ROWS)
        query = q_ref[rows].astype(F32) * (HEAD_DIM**-0.5)
        grad = do_ref[rows].astype(F32)
        block_ids = ids_ref[rows] + 1
        outs, grads = [], []
        for head in range(2):
            mine, spare = lanes(ROWS, head)
            marks = jnp.where(spare == block_ids, FAR, jnp.where(spare == 17, 1.0, 0.0))
            qa = jnp.where(mine, query, marks).astype(BF16)
            ka = ka_ref[head]
            va = va_ref[head]
            grown = jnp.exp(dot_nt(qa, ka))
            grown_low = grown.astype(BF16)
            sums = dot(grown_low, va)
            first = (1 - head) * HEAD_DIM
            inverse = 1.0 / sums[:, first : first + 1]
            out = sums * inverse
            inner = jnp.sum(jnp.where(mine, grad * out, 0.0), axis=-1, keepdims=True)
            offset = -inner * inverse
            high = offset.astype(BF16).astype(F32)
            marks = jnp.where(spare == 0, high, jnp.where(spare == 1, offset - high, 0.0))
            grad_a = jnp.where(mine, grad * inverse, marks).astype(BF16)
            ds = (grown * dot_nt(grad_a, va)).astype(BF16)
            outs.append(out)
            grads.append(dot(ds, ka) * (HEAD_DIM**-0.5))
            dka_ref[head] += dot_tn(ds, qa)
            dva_ref[head] += dot_tn(grown_low, grad_a)
        mine, _ = lanes(ROWS, 0)
        o_ref[rows] = jnp.where(mine, outs[0], outs[1]).astype(BF16)
        dq_ref[rows] = jnp.where(mine, grads[0], grads[1]).astype(BF16)
        return carry

    lax.fori_loop(0, length // ROWS, block, 0)
    mine, _ = lanes(length, 0)
    dk_ref[...] = jnp.where(mine, dka_ref[0], dka_ref[1]).astype(BF16)
    dv_ref[...] = jnp.where(mine, dva_ref[0], dva_ref[1]).astype(BF16)


def attend(query, key, value, grads, ids):
    length, width = query.shape
    block = pl.BlockSpec((length, PAIR), lambda j: (0, j))
    low = jax.ShapeDtypeStruct((length, width), BF16)
    return pl.pallas_call(
        attend_kernel,
        grid=(width // PAIR,),
        in_specs=[block] * 4 + [pl.BlockSpec((length, 1), lambda j: (0, 0))],
        out_specs=[block] * 4,
        out_shape=[low] * 4,
        scratch_shapes=[
            pltpu.VMEM((2, length, PAIR), BF16),
            pltpu.VMEM((2, length, PAIR), BF16),
            pltpu.VMEM((2, length, PAIR), F32),
            pltpu.VMEM((2, length, PAIR), F32),
        ],
        compiler_params=pltpu.CompilerParams(vmem_limit_bytes=VMEM_LIMIT),
        cost_estimate=pl.CostEstimate(
            flops=48 * length * length * width, bytes_accessed=14 * 2**20, transcendentals=0
        ),
        name="attend",
    )(query, key, value, grads, ids)


def back_kernel(
    raw_ref, dq_ref, dk_ref, dv_ref, qgain_ref, kgain_ref, wqkv_ref, gain_ref, x_ref,
    norm_ref, att_ref, g_ref,
    dn_ref, gw_ref, gattn_ref, gqg_ref, gkg_ref, gng_ref,
    dp_ref,
):
    step = pl.program_id(0)
    width = norm_ref.shape[1]
    count = norm_ref.shape[0] // ROWS

    @pl.when(step == 0)
    def _():
        gqg_ref[...] = jnp.zeros_like(gqg_ref)
        gkg_ref[...] = jnp.zeros_like(gkg_ref)
        gng_ref[...] = jnp.zeros_like(gng_ref)

    @pl.when(step < count)
    def _():
        rows = pl.ds(pl.multiple_of(step * ROWS, ROWS), ROWS)
        sides = ((dq_ref, qgain_ref, gqg_ref), (dk_ref, kgain_ref, gkg_ref))
        for side, (d_ref, hgain_ref, total_ref) in enumerate(sides):
            part = slice(side * width, (side + 1) * width)
            hat, scale = head_standardize(raw_ref[:, part])
            grad = d_ref[...].astype(F32)
            total_ref[...] += jnp.sum(grad * hat, axis=0, keepdims=True)
            grad = grad * hgain_ref[...]
            grad = scale * (grad - head_means(grad) - hat * head_means(grad * hat))
            dp_ref[rows, part] = grad.astype(BF16)
        dp_ref[rows, 2 * width :] = dv_ref[...]
        dn = dot_nt(dp_ref[rows], wqkv_ref[...])
        hat, _ = standardize(x_ref[...].astype(F32))
        gng_ref[...] += jnp.sum(dn * hat, axis=0, keepdims=True)
        dn_ref[...] = dn.astype(BF16)

    for part in range(3):

        @pl.when(step == count + part)
        def _():
            columns = slice(part * width, (part + 1) * width)
            gw_ref[...] = dot_tn(norm_ref[...], dp_ref[:, columns]).astype(BF16)

    @pl.when(step == count + 3)
    def _():
        gattn_ref[...] = dot_tn(att_ref[...], g_ref[...]).astype(BF16)


def back(raw, dq, dk, dv, query_gain, key_gain, weight_in, norm_gain, rows, normed, attended, grads):
    length, width = rows.shape
    count = length // ROWS
    whole = lambda i: (0, 0)
    now = lambda i: (jnp.minimum(i, count - 1), 0)
    vec = pl.BlockSpec((1, width), whole)
    block = pl.BlockSpec((ROWS, width), now)
    full = pl.BlockSpec((length, width), whole)
    one = jax.ShapeDtypeStruct((1, width), F32)
    return pl.pallas_call(
        back_kernel,
        grid=(count + 4,),
        in_specs=[
            pl.BlockSpec((ROWS, 2 * width), now),
            block,
            block,
            block,
            vec,
            vec,
            pl.BlockSpec((width, 3 * width), whole),
            vec,
            block,
            full,
            full,
            full,
        ],
        out_specs=[
            block,
            pl.BlockSpec((width, width), lambda i: (0, jnp.clip(i - count, 0, 2))),
            pl.BlockSpec((width, width), whole),
            vec,
            vec,
            vec,
        ],
        out_shape=[
            jax.ShapeDtypeStruct((length, width), BF16),
            jax.ShapeDtypeStruct((width, 3 * width), BF16),
            jax.ShapeDtypeStruct((width, width), BF16),
            one,
            one,
            one,
        ],
        scratch_shapes=[pltpu.VMEM((length, 3 * width), BF16)],
        compiler_params=pltpu.CompilerParams(vmem_limit_bytes=VMEM_LIMIT),
        cost_estimate=pl.CostEstimate(
            flops=14 * length * width * width, bytes_accessed=28 * 2**20, transcendentals=0
        ),
        name="back",
    )(raw, dq, dk, dv, query_gain, key_gain, weight_in, norm_gain, rows, normed, attended, grads)


def close_kernel(
    x_ref, g_ref, gain_ref, att_ref, wattn_ref, part_ref, bias_ref, dn_ref, dnq_ref,
    out_ref, gin_ref,
):
    rows = x_ref[...].astype(F32)
    out = rows + dot(att_ref[...], wattn_ref[...]) + part_ref[...] + bias_ref[...]
    out_ref[...] = out.astype(BF16)
    hat, scale = standardize(rows)
    grad = (dn_ref[...] + dnq_ref[...].astype(F32)) * gain_ref[...]
    mean = jnp.mean(grad, axis=-1, keepdims=True)
    along = jnp.mean(grad * hat, axis=-1, keepdims=True)
    gin_ref[...] = g_ref[...].astype(F32) + scale * (grad - mean - hat * along)


def close(rows, grads, norm_gain, attended, weight_attn, partial_out, bias_down, dn, dn_heads):
    count, width = rows.shape
    whole = lambda i: (0, 0)
    block = pl.BlockSpec((ROWS, width), lambda i: (i, 0))
    vec = pl.BlockSpec((1, width), whole)
    return pl.pallas_call(
        close_kernel,
        grid=(count // ROWS,),
        in_specs=[
            block, block, vec, block, pl.BlockSpec((width, width), whole), block, vec, block, block,
        ],
        out_specs=[block, block],
        out_shape=[
            jax.ShapeDtypeStruct((count, width), BF16),
            jax.ShapeDtypeStruct((count, width), F32),
        ],
        compiler_params=pltpu.CompilerParams(vmem_limit_bytes=VMEM_LIMIT),
        cost_estimate=pl.CostEstimate(
            flops=2 * count * width * width, bytes_accessed=18 * 2**20, transcendentals=0
        ),
        name="close",
    )(rows, grads, norm_gain, attended, weight_attn, partial_out, bias_down, dn, dn_heads)


def swap_halves(pair, bit, shift):
    kept = lax.dynamic_index_in_dim(pair, bit, 0, keepdims=False)
    sent = lax.dynamic_index_in_dim(pair, 1 - bit, 0, keepdims=False)
    size = lax.axis_size("tok")
    came = lax.ppermute(sent, "tok", [(i, i ^ shift) for i in range(size)])
    return (kept.astype(F32) + came.astype(F32)).astype(BF16)


def plane_sums(by_place, shifts):
    tok = lax.axis_index("tok")
    for shift in shifts:
        by_place = swap_halves(by_place, (tok // shift) % 2, shift)
    return by_place


def seq_sums(parts):
    came = lax.all_to_all(parts, "seq", split_axis=0, concat_axis=0, tiled=True)
    return jnp.sum(came.astype(F32), axis=0)


def places(order):
    found = [0]
    for shift in order:
        found = [base + bit * shift for base in found for bit in range(2)]
    return found


def share_grads(grad_hidden, grad_heads, grad_attn, grad_down, small):
    width, hidden = grad_hidden.shape
    per_row = (hidden + grad_heads.shape[1]) // width
    bias_rows = hidden // width
    tok_size, seq_size = lax.axis_size("tok"), lax.axis_size("seq")
    devices = tok_size * seq_size
    attn_at = 1 + per_row * width + bias_rows + 2
    down_at = attn_at + width
    total = down_at + hidden + 1
    piece = total * width // devices
    first_row = lambda d: d * total // devices
    held = -(-(total // devices + 1) // 16) * 16
    input_rows = lambda d: max(0, (first_row(d) - 1) // per_row)
    input_held = 48

    order_a, order_b = (1, 2, 4), (1, 4, 2)
    sent_a, sent_b = [], []
    for place in places(order_a):
        for z in (0, 1):
            start = input_rows(z * tok_size + place)
            sent_a.append(grad_hidden[start : start + input_held])
    early_a = jnp.stack(sent_a).reshape((2, 2, 2, 2, input_held, hidden))
    down_pad = jnp.pad(grad_down, ((0, held), (0, 0)))
    for place in places(order_b):
        start = first_row(3 * tok_size + place) - down_at
        sent_b.append(down_pad[start : start + held])
    early_b = jnp.stack(sent_b).reshape((2, 2, 2, held, width))
    early_a = plane_sums(early_a, order_a)
    early_b = plane_sums(early_b, order_b)
    early_a = early_a.reshape(2, input_held * hidden // width, width)
    fill = held - early_a.shape[1]
    early_a = jnp.pad(early_a, ((0, 0), (0, fill), (0, 0)))
    early = jnp.concatenate([early_a, jnp.zeros((1, held, width), BF16), early_b[None]])
    early = seq_sums(early)

    late_a = []
    for place in places(order_a):
        for z in (0, 1):
            start = input_rows(z * tok_size + place)
            late_a.append(grad_heads[start : start + input_held])
    late_a = jnp.stack(late_a).reshape((2, 2, 2, 2, input_held, grad_heads.shape[1]))
    from_row = input_rows(2 * tok_size)
    base = 1 + from_row * per_row
    mixed = jnp.concatenate([grad_heads[from_row:], grad_hidden[from_row:]], axis=1)
    mixed = jnp.concatenate(
        [
            mixed.reshape(-1, width),
            jnp.zeros((bias_rows + 2, width), BF16),
            grad_attn,
            grad_down[: first_row(3 * tok_size) - down_at + held],
        ]
    )
    late_b = []
    for place in places(order_b):
        start = first_row(2 * tok_size + place) - base
        late_b.append(mixed[start : start + held])
    late_b = jnp.stack(late_b).reshape((2, 2, 2, held, width))
    late_a = plane_sums(late_a, order_a).reshape(2, -1, width)
    late_b = plane_sums(late_b, order_b)
    late_a = jnp.pad(late_a, ((0, 0), (0, held - late_a.shape[1]), (0, 0)))
    late = jnp.concatenate([late_a, late_b[None], jnp.zeros((1, held, width), BF16)])
    late = seq_sums(late)

    z = lax.axis_index("seq")
    device = z * tok_size + lax.axis_index("tok")
    count = input_held * hidden // width
    from_heads = late[: input_held * (per_row - bias_rows)].reshape(input_held, -1)
    joined = jnp.concatenate([from_heads, early[:count].reshape(input_held, -1)], axis=1)
    joined = jnp.concatenate([small[0:1], joined.reshape(-1, width)])
    starts = jnp.array(
        [first_row(d) - per_row * input_rows(d) if d < 2 * tok_size else 0 for d in range(devices)],
        jnp.int32,
    )
    rows = total // devices + 1
    input_part = lax.dynamic_slice_in_dim(joined, starts[device], rows, 0)
    index = lax.broadcasted_iota(jnp.int32, (rows, 1), 0) + (device * total) // devices
    middle = late[:rows]
    for k in range(bias_rows + 2):
        middle = jnp.where(index == attn_at - bias_rows - 2 + k, small[1 + k], middle)
    last = jnp.where(index == total - 1, small[bias_rows + 3], early[:rows])
    chosen = jnp.where(z < 2, input_part, jnp.where(z == 2, middle, last))
    skip = (device * total) % devices * width // devices
    return lax.dynamic_slice_in_dim(chosen.reshape(-1), skip, piece, 0)


def sequence_device(
    layer_input,
    norm_gain,
    weight_in,
    bias_in,
    query_gain,
    key_gain,
    weight_attn,
    weight_down,
    bias_down,
    image_ids,
    cotangent,
):
    seqs, slots, width = layer_input.shape

    def regroup(rows):
        return lax.all_to_all(
            rows.reshape(seqs, slots, -1), "tok", split_axis=0, concat_axis=0, tiled=True
        ).reshape(seqs * slots, -1)

    gain = norm_gain[None]
    gains = (query_gain[None], key_gain[None])
    ids = regroup(image_ids)
    seq_rows = regroup(layer_input)
    seq_grads = regroup(cotangent)
    rows = layer_input.reshape(seqs * slots, width)
    grads = cotangent.reshape(seqs * slots, width)
    part_out, dn, grad_hidden, grad_down, grad_bias_in, grad_bias_down, gain_home = mlp(
        rows, grads, gain, weight_in, bias_in[None], weight_down
    )
    query, key, value, grad_att, normed, raw = heads(
        seq_rows, seq_grads, gain, weight_in, weight_attn, *gains
    )
    attended, dq, dk, dv = attend(query, key, value, grad_att, ids)
    dn_heads, grad_heads, grad_attn, grad_qg, grad_kg, gain_seq = back(
        raw, dq, dk, dv, *gains, weight_in, gain, seq_rows, normed, attended, seq_grads
    )
    small = jnp.concatenate(
        [gain_home + gain_seq, grad_bias_in.reshape(-1, width), grad_qg, grad_kg, grad_bias_down]
    )
    small = lax.psum(small, ("seq", "tok"))
    grad_weights = share_grads(grad_hidden, grad_heads, grad_attn, grad_down, small)
    out, grad_input = close(
        rows, grads, gain, regroup(attended), weight_attn, part_out, bias_down[None], dn,
        regroup(dn_heads),
    )
    shape = (seqs, slots, width)
    return (out.reshape(shape), grad_input.reshape(shape), grad_weights)


def per_device(layer_input, *rest):
    seqs, slots, _ = layer_input.shape
    if lax.axis_size("tok") == seqs == 8 and lax.axis_size("seq") == 4 and slots % 16 == 0:
        return sequence_device(layer_input, *rest)
    return units_device(layer_input, *rest)


def solution(mesh):
    placed = (
        P("seq", "tok", None),
        P(),
        P(),
        P(),
        P(),
        P(),
        P(),
        P(),
        P(),
        P("seq", "tok"),
        P("seq", "tok", None),
    )
    return jax.shard_map(
        per_device,
        mesh=mesh,
        in_specs=placed,
        out_specs=(P("seq", "tok", None), P("seq", "tok", None), P(("seq", "tok"))),
        check_vma=False,
    )
```

```python
from functools import partial

import jax
import jax.numpy as jnp
from jax import lax
from jax.experimental import pallas as pl
from jax.experimental.pallas import tpu as pltpu
from jax.sharding import PartitionSpec as P

HEADS = 12


EPS = 1e-06
NEG = -1e30

F32 = jnp.float32
BF16 = jnp.bfloat16
ROWS = 256
HEAD_DIM = 64
PAIR = 2 * HEAD_DIM
FAR = 192.0
VMEM_LIMIT = 60 * 1024 * 1024


def layer_norm(values, scaling):
    average = jnp.mean(values, axis=-1, keepdims=True)
    shifted = values - average
    spread = jnp.mean(shifted * shifted, axis=-1, keepdims=True)
    return shifted * lax.rsqrt(spread + EPS) * scaling


def head_norms(query_raw, key_raw, gain_query, gain_key):
    return (layer_norm(query_raw, gain_query), layer_norm(key_raw, gain_key))


def to_units(row_values, seq_count, head_count):
    part_len = row_values.shape[0] // seq_count
    shaped = row_values.reshape(seq_count, part_len, head_count, -1).transpose(0, 2, 3, 1)
    return shaped.reshape(seq_count * head_count, -1, part_len)


def from_units(unit_values, seq_count, head_count):
    part_len = unit_values.shape[2]
    shaped = unit_values.reshape(seq_count, head_count, -1, part_len).transpose(0, 3, 1, 2)
    return shaped.reshape(seq_count * part_len, -1)


def block_scores(query_block, key_unit, image_block, slot_ids, score_scale):
    scores = (
        lax.dot_general(
            query_block, key_unit, (((0,), (0,)), ((), ())), preferred_element_type=jnp.float32
        )
        * score_scale
    )
    allowed = image_block[:, None] == slot_ids[None, :]
    return (scores, allowed)


def split_blocks(unit_values, block_len):
    head_dim, length = unit_values.shape
    return unit_values.reshape(head_dim, length // block_len, block_len).transpose(1, 0, 2)


def attend_unit(packed, score_scale):
    query_unit, key_unit, value_unit, slot_ids = packed
    head_dim, length = query_unit.shape
    block_len = min(512, length)
    query_blocks = split_blocks(query_unit, block_len)
    image_blocks = slot_ids.reshape(length // block_len, block_len)

    def one_block(inputs):
        query_block, image_block = inputs
        scores, allowed = block_scores(query_block, key_unit, image_block, slot_ids, score_scale)
        scores = jnp.where(allowed, scores, NEG)
        row_max = jnp.max(scores, axis=-1, keepdims=True)
        shifted = jnp.exp(scores - row_max)
        row_total = jnp.sum(shifted, axis=-1, keepdims=True)
        weights = (shifted / row_total).astype(jnp.bfloat16)
        outputs = lax.dot_general(
            value_unit, weights, (((1,), (1,)), ((), ())), preferred_element_type=jnp.float32
        )
        return (outputs, row_max[:, 0] + jnp.log(row_total[:, 0]))

    outputs, log_total = lax.map(one_block, (query_blocks, image_blocks))
    return (outputs.transpose(1, 0, 2).reshape(head_dim, length), log_total.reshape(length))


def attend_back(packed, score_scale):
    query_unit, key_unit, value_unit, grad_unit, log_total, slot_ids = packed
    head_dim, length = query_unit.shape
    block_len = min(512, length)
    query_blocks = split_blocks(query_unit, block_len)
    grad_blocks = split_blocks(grad_unit, block_len)
    total_blocks = log_total.reshape(length // block_len, block_len)
    image_blocks = slot_ids.reshape(length // block_len, block_len)

    def one_block(carried, inputs):
        grad_key, grad_value = carried
        query_block, grad_block, total_block, image_block = inputs
        scores, allowed = block_scores(query_block, key_unit, image_block, slot_ids, score_scale)
        weights = jnp.where(allowed, jnp.exp(scores - total_block[:, None]), 0.0)
        weights_low = weights.astype(jnp.bfloat16)
        grad_weights = lax.dot_general(
            grad_block, value_unit, (((0,), (0,)), ((), ())), preferred_element_type=jnp.float32
        )
        inner = jnp.sum(weights * grad_weights, axis=-1, keepdims=True)
        grad_scores = (weights * (grad_weights - inner)).astype(jnp.bfloat16)
        grad_query = score_scale * lax.dot_general(
            key_unit, grad_scores, (((1,), (1,)), ((), ())), preferred_element_type=jnp.float32
        )
        grad_key = grad_key + score_scale * lax.dot_general(
            query_block, grad_scores, (((1,), (0,)), ((), ())), preferred_element_type=jnp.float32
        )
        grad_value = grad_value + lax.dot_general(
            grad_block, weights_low, (((1,), (0,)), ((), ())), preferred_element_type=jnp.float32
        )
        return ((grad_key, grad_value), grad_query)

    blank = jnp.zeros((head_dim, length), jnp.float32)
    (grad_key, grad_value), grad_query = lax.scan(
        one_block, (blank, blank), (query_blocks, grad_blocks, total_blocks, image_blocks)
    )
    return (grad_query.transpose(1, 0, 2).reshape(head_dim, length), grad_key, grad_value)


def reduce_grads(flat_grad):
    return lax.psum_scatter(flat_grad, ("seq", "tok"), scatter_dimension=0, tiled=True)


def units_device(
    layer_input,
    norm_gain,
    weight_in,
    bias_in,
    query_gain,
    key_gain,
    weight_attn,
    weight_down,
    bias_down,
    image_ids,
    cotangent,
):
    seq_count, part_len, model_width = layer_input.shape
    row_count = seq_count * part_len
    head_count = HEADS
    head_dim = model_width // head_count
    score_scale = head_dim ** (-0.5)
    whole_ids = lax.all_gather(image_ids, "tok", axis=1, tiled=True)
    unit_count = seq_count * head_count // lax.axis_size("tok")
    first_unit = lax.axis_index("tok") * unit_count
    unit_seq = (first_unit + jnp.arange(unit_count, dtype=jnp.int32)) // head_count
    unit_ids = jnp.take(whole_ids, unit_seq, axis=0)
    input_rows = layer_input.reshape(row_count, model_width).astype(jnp.float32)
    normalized_rows, input_back = jax.vjp(layer_norm, input_rows, norm_gain)
    normed_low = normalized_rows.astype(jnp.bfloat16)
    projected_rows = jnp.dot(normed_low, weight_in, preferred_element_type=jnp.float32)
    query_raw = projected_rows[:, :model_width].reshape(row_count, head_count, head_dim)
    key_raw = projected_rows[:, model_width : 2 * model_width].reshape(
        row_count, head_count, head_dim
    )
    value_low = projected_rows[:, 2 * model_width : 3 * model_width].astype(jnp.bfloat16)
    hidden_in = projected_rows[:, 3 * model_width :] + bias_in
    gain_query = query_gain.reshape(head_count, head_dim)
    gain_key = key_gain.reshape(head_count, head_dim)
    (query_normed, key_normed), heads_back = jax.vjp(
        head_norms, query_raw, key_raw, gain_query, gain_key
    )
    outgoing = (
        to_units(
            query_normed.reshape(row_count, model_width).astype(jnp.bfloat16), seq_count, head_count
        ),
        to_units(
            key_normed.reshape(row_count, model_width).astype(jnp.bfloat16), seq_count, head_count
        ),
        to_units(value_low, seq_count, head_count),
    )
    query_units, key_units, value_units = (
        lax.all_to_all(outgoing[0], "tok", split_axis=0, concat_axis=2, tiled=True),
        lax.all_to_all(outgoing[1], "tok", split_axis=0, concat_axis=2, tiled=True),
        lax.all_to_all(outgoing[2], "tok", split_axis=0, concat_axis=2, tiled=True),
    )
    attention_output, log_total = lax.map(
        partial(attend_unit, score_scale=score_scale),
        (query_units, key_units, value_units, unit_ids),
    )
    returned = lax.all_to_all(
        attention_output.astype(jnp.bfloat16), "tok", split_axis=2, concat_axis=0, tiled=True
    )
    attn_rows = from_units(returned, seq_count, head_count)
    activation, gelu_back = jax.vjp(partial(jax.nn.gelu, approximate=False), hidden_in)
    act_low = activation.astype(jnp.bfloat16)
    result_rows = input_rows + jnp.dot(attn_rows, weight_attn, preferred_element_type=jnp.float32)
    result_rows = (
        result_rows + jnp.dot(act_low, weight_down, preferred_element_type=jnp.float32) + bias_down
    )
    layer_output = result_rows.astype(jnp.bfloat16).reshape(seq_count, part_len, model_width)
    grad_rows = cotangent.reshape(row_count, model_width)
    grad_full = grad_rows.astype(jnp.float32)
    contract_rows = (((0,), (0,)), ((), ()))
    contract_cols = (((1,), (1,)), ((), ()))
    grad_bias_down = jnp.sum(grad_full, axis=0)
    grad_weight_down = lax.dot_general(
        act_low, grad_rows, contract_rows, preferred_element_type=jnp.float32
    )
    grad_weight_attn = lax.dot_general(
        attn_rows, grad_rows, contract_rows, preferred_element_type=jnp.float32
    )
    grad_activation = lax.dot_general(
        grad_rows, weight_down, contract_cols, preferred_element_type=jnp.float32
    )
    grad_hidden = gelu_back(grad_activation)[0]
    grad_bias_in = jnp.sum(grad_hidden, axis=0)
    grad_attended = lax.dot_general(
        grad_rows, weight_attn, contract_cols, preferred_element_type=jnp.float32
    )
    grad_units = lax.all_to_all(
        to_units(grad_attended.astype(jnp.bfloat16), seq_count, head_count),
        "tok",
        split_axis=0,
        concat_axis=2,
        tiled=True,
    )
    grad_query_u, grad_key_u, grad_value_u = lax.map(
        partial(attend_back, score_scale=score_scale),
        (query_units, key_units, value_units, grad_units, log_total, unit_ids),
    )
    back_query, back_key, back_value = (
        lax.all_to_all(
            grad_query_u.astype(jnp.bfloat16), "tok", split_axis=2, concat_axis=0, tiled=True
        ),
        lax.all_to_all(
            grad_key_u.astype(jnp.bfloat16), "tok", split_axis=2, concat_axis=0, tiled=True
        ),
        lax.all_to_all(
            grad_value_u.astype(jnp.bfloat16), "tok", split_axis=2, concat_axis=0, tiled=True
        ),
    )
    grad_query_n = (
        from_units(back_query, seq_count, head_count)
        .astype(jnp.float32)
        .reshape(row_count, head_count, head_dim)
    )
    grad_key_n = (
        from_units(back_key, seq_count, head_count)
        .astype(jnp.float32)
        .reshape(row_count, head_count, head_dim)
    )
    grad_value_rows = from_units(back_value, seq_count, head_count).astype(jnp.float32)
    grad_query_raw, grad_key_raw, grad_gain_query, grad_gain_key = heads_back(
        (grad_query_n, grad_key_n)
    )
    grad_projected = jnp.concatenate(
        [
            grad_query_raw.reshape(row_count, model_width),
            grad_key_raw.reshape(row_count, model_width),
            grad_value_rows,
            grad_hidden,
        ],
        axis=1,
    ).astype(jnp.bfloat16)
    grad_weight_in = lax.dot_general(
        normed_low, grad_projected, contract_rows, preferred_element_type=jnp.float32
    )
    grad_normed = lax.dot_general(
        grad_projected, weight_in, contract_cols, preferred_element_type=jnp.float32
    )
    grad_input_rows, grad_norm_gain = input_back(grad_normed)
    grad_input = (grad_full + grad_input_rows).reshape(seq_count, part_len, model_width)
    pieces = [
        grad_norm_gain,
        grad_weight_in,
        grad_bias_in,
        grad_gain_query,
        grad_gain_key,
        grad_weight_attn,
        grad_weight_down,
        grad_bias_down,
    ]
    flat_grad = jnp.concatenate([tensor.reshape(-1) for tensor in pieces])
    grad_weights = reduce_grads(flat_grad)
    return (layer_output, grad_input, grad_weights)


SLOT = 48
HELD = 304
PARTS = ((0, 256), (256, 256), (512, 256))
TOK = 8
SEQS_IN = 3
GAINS_ROW = 28
PLACE_ROWS = 4 * SLOT * 2 + 2 * HELD
ATTN_BLOCKS = (
    ((0, 48, 6, 0), (48, 48, 7, 0), (96, 48, 3, 0), (144, 48, 4, 0), (192, 48, 5, 0), (240, 16, 2, 32)),
    ((0, 48, 3, 0), (48, 48, 5, 0), (96, 48, 7, 0), (144, 48, 4, 0), (192, 48, 6, 0), (240, 16, 2, 32)),
    ((0, 48, 4, 0), (48, 48, 6, 0), (96, 48, 7, 0), (144, 48, 5, 0), (192, 48, 3, 0), (240, 16, 2, 32)),
)


class Flat:
    def __init__(self, width, hidden, devices):
        self.width = width
        self.chunks = hidden // width
        self.per_row = 3 + self.chunks
        self.bias_at = 1 + self.per_row * width
        self.gains_at = self.bias_at + self.chunks
        self.attn_at = self.gains_at + 2
        self.down_at = self.attn_at + width
        self.total = self.down_at + hidden + 1
        self.devices = devices
        self.rows = self.total // devices + 1

    def first(self, device):
        return device * self.total // self.devices

    def skip(self, device):
        return (device * self.total) % self.devices * self.width // self.devices

    def input_row(self, device):
        return max(0, (self.first(device) - 1) // self.per_row)

    def slots(self):
        pairs = [(place, z) for place in range(TOK) for z in range(3)]
        return [(place, z) for place, z in pairs if self.first(z * TOK + place) < self.bias_at]

    def features(self):
        return [self.input_row(z * TOK + place) + i for place, z in self.slots() for i in range(SLOT)]

    def bias_place(self):
        return next(d for d in range(self.devices) if self.first(d + 1) > self.bias_at) % TOK

    def down_start(self, device):
        start = self.first(device) - self.down_at
        return None if start + self.rows <= 0 else max(0, start) // 16 * 16

    def attn_pieces(self, place):
        low = self.first(2 * TOK + place) - self.attn_at
        high = low + self.rows
        found = []
        for part, (base, _) in enumerate(PARTS):
            for start, rows, holder, at in ATTN_BLOCKS[part]:
                begin, end = max(base + start, low), min(base + start + rows, high)
                if begin < end:
                    found.append((part, holder, at + begin - base - start, end - begin))
        return found

    def attn_rounds(self):
        pairs = {(h, p) for p in range(TOK) for _, h, _, _ in self.attn_pieces(p) if h != p}
        degree = lambda pair: sum((pair[0] == h) + (pair[1] == p) for h, p in pairs)
        rounds = []
        for holder, place in sorted(pairs, key=lambda pair: (-degree(pair), pair)):
            for taken in rounds:
                if all(holder != h and place != p for h, p in taken):
                    taken.append((holder, place))
                    break
            else:
                rounds.append([(holder, place)])
        return rounds


def side_of(place, core):
    return core if place % 2 == 0 else 1 - core


def selection(features_ref, width):
    columns = lax.broadcasted_iota(jnp.int32, (features_ref.shape[0], width), 1)
    return jnp.where(columns == features_ref[...], 1.0, 0.0).astype(BF16)


def dot(left, right):
    return jnp.dot(left, right, preferred_element_type=F32)


def dot_nt(left, right):
    return lax.dot_general(left, right, (((1,), (1,)), ((), ())), preferred_element_type=F32)


def dot_tn(left, right):
    return lax.dot_general(left, right, (((0,), (0,)), ((), ())), preferred_element_type=F32)


def standardize(rows):
    shifted = rows - jnp.mean(rows, axis=-1, keepdims=True)
    scale = lax.rsqrt(jnp.mean(shifted * shifted, axis=-1, keepdims=True) + EPS)
    return shifted * scale, scale


def head_means(values):
    width = min(4 * HEAD_DIM, values.shape[1])
    row = lax.broadcasted_iota(jnp.int32, (width, width), 0)
    column = lax.broadcasted_iota(jnp.int32, (width, width), 1)
    ones = jnp.where((row >> 6) == (column >> 6), 1.0, 0.0).astype(BF16)
    high = values.astype(BF16)
    rest = (values - high.astype(F32)).astype(BF16)
    parts = []
    for start in range(0, values.shape[1], width):
        part = slice(start, start + width)
        parts.append(dot(high[:, part], ones) + dot(rest[:, part], ones))
    return jnp.concatenate(parts, axis=1) * (1.0 / HEAD_DIM)


def head_standardize(raw):
    shifted = raw - head_means(raw)
    scale = lax.rsqrt(head_means(shifted * shifted) + EPS)
    return shifted * scale, scale


def gelu_pair(pre):
    phi = 0.5 + 0.5 * lax.erf(pre * (0.5**0.5))
    density = jnp.exp(-0.5 * pre * pre) * 0.3989422804014327
    return pre * phi, phi + pre * density


def with_row(values, row, vector):
    index = lax.broadcasted_iota(jnp.int32, values.shape, 0)
    return jnp.where(index == row, vector, values)


def mlp_kernel(
    flat, x_ref, g_ref, gain_ref, wh_ref, bias_ref, wd_ref, features_ref,
    out_ref, dn_ref, payload_ref,
    norm_ref, perm_ref, act_ref, dh_ref, gbd_ref, buffer_ref, sem,
):
    step = pl.program_id(0)
    last = flat.chunks - 1
    width = flat.width
    count = x_ref.shape[0] // ROWS

    @pl.when(step == 0)
    def _():
        gbd_ref[...] = jnp.zeros_like(gbd_ref)
        buffer_ref[:, 8 * SLOT + HELD :] = jnp.zeros((TOK, HELD, width), BF16)

        def block(i, carry):
            rows = pl.ds(pl.multiple_of(i * ROWS, ROWS), ROWS)
            hat, _ = standardize(x_ref[rows].astype(F32))
            norm_ref[rows] = (hat * gain_ref[...]).astype(BF16)
            out_ref[rows] = jnp.zeros_like(out_ref[rows])
            dn_ref[rows] = jnp.zeros_like(dn_ref[rows])
            gbd_ref[...] += jnp.sum(g_ref[rows].astype(F32), axis=0, keepdims=True)
            return carry

        lax.fori_loop(0, count, block, 0)
        perm_ref[...] = dot_nt(selection(features_ref, width), norm_ref[...]).astype(BF16)

    def block(i, total):
        rows = pl.ds(pl.multiple_of(i * ROWS, ROWS), ROWS)
        pre = dot(norm_ref[rows], wh_ref[...]) + bias_ref[...]
        act, slope = gelu_pair(pre)
        act_low = act.astype(BF16)
        dh = dot_nt(g_ref[rows], wd_ref[...]) * slope
        dh_low = dh.astype(BF16)
        act_ref[rows] = act_low
        dh_ref[rows] = dh_low
        out_ref[rows] += dot(act_low, wd_ref[...])
        dn_ref[rows] += dot_nt(dh_low, wh_ref[...])
        return total + jnp.sum(dh, axis=0, keepdims=True)

    grad_bias = lax.fori_loop(0, count, block, jnp.zeros((1, width), F32))

    grad_down = dot_tn(act_ref[...], g_ref[...])
    for chunk in range(flat.chunks):

        @pl.when(step == chunk)
        def _():
            low = chunk * width
            for device in range(2 * TOK, 4 * TOK):
                start = flat.down_start(device)
                if start is None:
                    continue
                place, at = device % TOK, 8 * SLOT if device >= 3 * TOK else 8 * SLOT + HELD
                begin, end = max(start, low), min(start + HELD, low + width)
                if begin < end:
                    part = grad_down[begin - low : end - low].astype(BF16)
                    buffer_ref[place, at + begin - start : at + end - start] = part
                if chunk == last and start + HELD > low + width:
                    rows = 16
                    tail = with_row(jnp.zeros((rows, width), F32), 0, gbd_ref[...])
                    row = at + low + width - start
                    buffer_ref[place, row : row + rows] = tail.astype(BF16)

    grad_in = dot(perm_ref[...], dh_ref[...])
    shift = pl.multiple_of(step * SLOT, SLOT)
    for index, (place, z) in enumerate(flat.slots()):
        part = grad_in[index * SLOT : (index + 1) * SLOT]
        at = z * 4 * SLOT if z < 2 else 8 * SLOT + HELD
        buffer_ref[place, pl.ds(at + shift, SLOT)] = part.astype(BF16)

    for chunk in range(flat.chunks):

        @pl.when(step == chunk)
        def _():
            tail = with_row(jnp.zeros((16, width), F32), 0, grad_bias).astype(BF16)
            at = 8 * SLOT + HELD + 4 * SLOT + 16 * chunk
            buffer_ref[flat.bias_place(), at : at + 16] = tail

    @pl.when(step == last)
    def _():
        def block(i, total):
            rows = pl.ds(pl.multiple_of(i * ROWS, ROWS), ROWS)
            hat, _ = standardize(x_ref[rows].astype(F32))
            return total + jnp.sum(dn_ref[rows] * hat, axis=0, keepdims=True)

        total = lax.fori_loop(0, count, block, jnp.zeros((1, width), F32))
        kept = buffer_ref[0, SLOT - 16 : SLOT].astype(F32)
        buffer_ref[0, SLOT - 16 : SLOT] = with_row(kept, 15, total).astype(BF16)
        copy = pltpu.make_async_copy(buffer_ref, payload_ref, sem)
        copy.start()
        copy.wait()


def mlp(flat, rows, grads, norm_gain, weight_in, bias_in, weight_down, features):
    count, width = rows.shape
    chunks = flat.chunks
    whole = lambda i: (0, 0)
    once = pl.Buffered(1)
    full = pl.BlockSpec((count, width), whole, pipeline_mode=once)
    payload = jax.ShapeDtypeStruct((TOK, PLACE_ROWS, width), BF16)
    return pl.pallas_call(
        partial(mlp_kernel, flat),
        grid=(chunks,),
        in_specs=[
            full,
            full,
            pl.BlockSpec((1, width), whole),
            pl.BlockSpec((width, width), lambda i: (0, i + 3)),
            pl.BlockSpec((1, width), lambda i: (0, i)),
            pl.BlockSpec((width, width), lambda i: (i, 0)),
            pl.BlockSpec(features.shape, whole, pipeline_mode=once),
        ],
        out_specs=[
            pl.BlockSpec((count, width), whole),
            pl.BlockSpec((count, width), whole),
            pl.BlockSpec(memory_space=pl.ANY),
        ],
        out_shape=[
            jax.ShapeDtypeStruct((count, width), F32),
            jax.ShapeDtypeStruct((count, width), F32),
            payload,
        ],
        scratch_shapes=[
            pltpu.VMEM((count, width), BF16),
            pltpu.VMEM((features.shape[0], count), BF16),
            pltpu.VMEM((count, width), BF16),
            pltpu.VMEM((count, width), BF16),
            pltpu.VMEM((1, width), F32),
            pltpu.VMEM(payload.shape, BF16),
            pltpu.SemaphoreType.DMA,
        ],
        compiler_params=pltpu.CompilerParams(vmem_limit_bytes=VMEM_LIMIT),
        cost_estimate=pl.CostEstimate(
            flops=12 * count * width * width * chunks, bytes_accessed=32 * 2**20, transcendentals=0
        ),
        name="mlp",
    )(rows, grads, norm_gain, weight_in, bias_in, weight_down, features)


def heads_kernel(
    x_ref, g_ref, gain_ref, wqkv_ref, wattn_ref, qgain_ref, kgain_ref, features_ref,
    q_ref, k_ref, v_ref, do_ref, raw_ref, perm_ref, seqg_ref,
    pick_ref,
):
    width = x_ref.shape[2]

    @pl.when(pl.program_id(0) == 0)
    def _():
        pick_ref[...] = selection(features_ref, width)

    hat, _ = standardize(x_ref[...].reshape(ROWS, width).astype(F32))
    normed = (hat * gain_ref[...]).astype(BF16)
    grads = g_ref[...].reshape(ROWS, width)
    seqg_ref[...] = grads
    perm_ref[...] = dot_nt(pick_ref[...], normed).astype(BF16)
    q_raw = dot(normed, wqkv_ref[:, :width])
    raw_ref[:, :width] = q_raw
    q_ref[...] = (head_standardize(q_raw)[0] * qgain_ref[...]).astype(BF16)
    k_raw = dot(normed, wqkv_ref[:, width : 2 * width])
    raw_ref[:, width:] = k_raw
    k_ref[...] = (head_standardize(k_raw)[0] * kgain_ref[...]).astype(BF16)
    v_ref[...] = dot(normed, wqkv_ref[:, 2 * width :]).astype(BF16)
    do_ref[...] = dot_nt(grads, wattn_ref[...]).astype(BF16)


def heads(came, norm_gain, weight_in, weight_attn, query_gain, key_gain, features):
    seqs, held, width = came.shape
    slots = held // 2 // 16 * 16
    count = seqs * slots
    whole = lambda i: (0, 0)
    block = pl.BlockSpec((ROWS, width), lambda i: (i, 0))
    vec = pl.BlockSpec((1, width), whole)
    low = jax.ShapeDtypeStruct((count, width), BF16)
    group = (ROWS // slots, slots, width)
    return pl.pallas_call(
        heads_kernel,
        grid=(count // ROWS,),
        in_specs=[
            pl.BlockSpec(group, lambda i: (i, 0, 0)),
            pl.BlockSpec(group, lambda i: (i, 1, 0)),
            vec,
            pl.BlockSpec((width, 3 * width), whole),
            pl.BlockSpec((width, width), whole),
            vec,
            vec,
            pl.BlockSpec(features.shape, whole),
        ],
        out_specs=[block] * 4
        + [
            pl.BlockSpec((ROWS, 2 * width), lambda i: (i, 0)),
            pl.BlockSpec((features.shape[0], ROWS), lambda i: (0, i)),
            block,
        ],
        out_shape=[low] * 4
        + [
            jax.ShapeDtypeStruct((count, 2 * width), F32),
            jax.ShapeDtypeStruct((features.shape[0], count), BF16),
            low,
        ],
        scratch_shapes=[pltpu.VMEM((features.shape[0], width), BF16)],
        compiler_params=pltpu.CompilerParams(vmem_limit_bytes=VMEM_LIMIT),
        cost_estimate=pl.CostEstimate(
            flops=10 * count * width * width, bytes_accessed=26 * 2**20, transcendentals=0
        ),
        name="heads",
    )(came, came, norm_gain, weight_in, weight_attn, query_gain, key_gain, features)


def part_kernel(
    flat, part, q_ref, k_ref, v_ref, do_ref, ids_ref, qgain_ref, kgain_ref,
    raw_hbm, perm_hbm, g_hbm, win_hbm, dn_hbm, x_hbm,
    *rest,
):
    length, size = q_ref.shape
    width = flat.width
    base = PARTS[part][0]
    final = part == len(PARTS) - 1
    dn_out_ref, payload_hbm, *rest = rest
    ka_ref, va_ref, kat_ref, vat_ref, p_ref, plow_ref, d_ref, *rest = rest
    raw_ref, perm_ref, g_ref, w_ref, dn_ref, x_ref, att_ref, buffer_ref, sems = rest

    loads = {
        "raw": [
            pltpu.make_async_copy(
                raw_hbm.at[:, pl.ds(s * width + base, size)],
                raw_ref.at[:, pl.ds(s * size, size)],
                sems.at[s],
            )
            for s in range(2)
        ],
        "w": [
            pltpu.make_async_copy(
                win_hbm.at[:, pl.ds(s * width + base, size)],
                w_ref.at[:, pl.ds(s * size, size)],
                sems.at[2 + s],
            )
            for s in range(3)
        ],
        "perm": [pltpu.make_async_copy(perm_hbm, perm_ref, sems.at[5])],
        "g": [pltpu.make_async_copy(g_hbm, g_ref, sems.at[6])],
    }
    if part:
        loads["dn"] = [pltpu.make_async_copy(dn_hbm, dn_ref, sems.at[7])]
    if final:
        slots = x_ref.shape[1]
        loads["x"] = [pltpu.make_async_copy(x_hbm.at[:, pl.ds(0, slots)], x_ref, sems.at[8])]
    for group in loads.values():
        for copy in group:
            copy.start()

    def arrived(name):
        for copy in loads[name]:
            copy.wait()

    def lanes(count, head):
        lane = lax.broadcasted_iota(jnp.int32, (count, PAIR), 1)
        return (lane >> 6) == head, lane - (1 - head) * HEAD_DIM

    ids = ids_ref[...] + 1
    count = size // HEAD_DIM

    def widen(item):
        head, pair = item % 2, slice(item // 2 * PAIR, (item // 2 + 1) * PAIR)
        mine, spare = lanes(length, head)
        marks = jnp.where(spare == ids, 1.0, jnp.where(spare == 17, -FAR, 0.0))
        ka = jnp.where(mine, k_ref[:, pair].astype(F32), marks)
        ka_ref[item % 2] = ka.astype(BF16)
        kat_ref[item % 2] = ka.T.astype(BF16)
        marks = jnp.where((spare == 0) | (spare == 1), 1.0, 0.0)
        va = jnp.where(mine, v_ref[:, pair].astype(F32), marks)
        va_ref[item % 2] = va.astype(BF16)
        vat_ref[item % 2] = va.T.astype(BF16)
        marks = jnp.where(spare == ids, FAR, jnp.where(spare == 17, 1.0, 0.0))
        return jnp.where(mine, q_ref[:, pair].astype(F32) * (HEAD_DIM**-0.5), marks).astype(BF16)

    def score(item, qa):
        grown = jnp.exp(dot_nt(ka_ref[item % 2], qa))
        p_ref[item % 2] = grown
        low = grown.astype(BF16)
        plow_ref[item % 2] = low
        return dot(vat_ref[item % 2], low)

    def middle(item, sums):
        head, pair = item % 2, slice(item // 2 * PAIR, (item // 2 + 1) * PAIR)
        mine, spare = lanes(length, head)
        grad = do_ref[:, pair].astype(F32)
        out = sums.T
        first = (1 - head) * HEAD_DIM
        inverse = 1.0 / out[:, first : first + 1]
        out = out * inverse
        inner = jnp.sum(jnp.where(mine, grad * out, 0.0), axis=-1, keepdims=True)
        offset = -inner * inverse
        high = offset.astype(BF16).astype(F32)
        marks = jnp.where(spare == 0, high, jnp.where(spare == 1, offset - high, 0.0))
        return out, jnp.where(mine, grad * inverse, marks).astype(BF16)

    def gradients(item, qa, grad_a):
        ds = (p_ref[item % 2] * dot_nt(va_ref[item % 2], grad_a)).astype(BF16)
        dv = dot(plow_ref[item % 2], grad_a)
        dk = dot(ds, qa)
        dq = dot(kat_ref[item % 2], ds).T * (HEAD_DIM**-0.5)
        return dq, dk, dv

    qa = widen(0)
    sums = score(0, qa)
    kept = None
    for item in range(count):
        out, grad_a = middle(item, sums)
        now = gradients(item, qa, grad_a)
        if item + 1 < count:
            qa = widen(item + 1)
            sums = score(item + 1, qa)
        if item % 2 == 0:
            kept = (out, *now)
        else:
            mine, _ = lanes(length, 0)
            start = item // 2 * PAIR
            both = jnp.where(mine, kept[0], out).astype(BF16)
            att_ref[:, start : start + PAIR] = both
            both = both.reshape(TOK, length // TOK, PAIR)
            buffer_ref[:, : length // TOK, start : start + PAIR] = both
            for side in range(3):
                both = jnp.where(mine, kept[1 + side], now[side]).astype(BF16)
                d_ref[:, side * size + start : side * size + start + PAIR] = both

    arrived("raw")
    arrived("w")
    if part:
        arrived("dn")
    if final:
        arrived("x")
        group = ROWS // x_ref.shape[1]

    def block(i, totals):
        rows = pl.ds(pl.multiple_of(i * ROWS, ROWS), ROWS)
        totals = list(totals)
        for side, gain_ref in enumerate((qgain_ref, kgain_ref)):
            lane = slice(side * size, (side + 1) * size)
            hat, scale = head_standardize(raw_ref[rows, lane])
            grad = d_ref[rows, lane].astype(F32)
            totals[side] += jnp.sum(grad * hat, axis=0, keepdims=True)
            grad = grad * gain_ref[...]
            grad = scale * (grad - head_means(grad) - hat * head_means(grad * hat))
            d_ref[rows, lane] = grad.astype(BF16)
        dn = dot_nt(d_ref[rows], w_ref[...])
        if part:
            dn = dn + dn_ref[rows]
        if final:
            x = x_ref[pl.ds(i * group, group)].reshape(ROWS, width).astype(F32)
            totals[2] += jnp.sum(dn * standardize(x)[0], axis=0, keepdims=True)
        dn_out_ref[rows] = dn.astype(dn_out_ref.dtype)
        return tuple(totals)

    zero = jnp.zeros((1, size), F32)
    totals = lax.fori_loop(0, length // ROWS, block, (zero, zero, jnp.zeros((1, width), F32)))

    arrived("perm")
    arrived("g")
    def put_slot(place, z, values):
        for s in range(3):
            row = length // TOK + (3 * z + s) * SLOT
            part = values[:, s * size : (s + 1) * size].astype(BF16)
            buffer_ref[place, row : row + values.shape[0]] = part

    grad_in = dot(perm_ref[...], d_ref[...])
    grad_attn = dot_tn(att_ref[...], g_ref[...])
    gains = jnp.concatenate([totals[0], totals[1], zero], axis=1)
    for index, (place, z) in enumerate(flat.slots()):
        values = grad_in[index * SLOT : (index + 1) * SLOT]
        if (place, z) == (flat.bias_place(), 2):
            start, rows, _, at = ATTN_BLOCKS[part][-1]
            values = jnp.concatenate([values[:at], grad_attn[start : start + rows]])
            values = with_row(values, GAINS_ROW, gains)
        if final and (place, z) == (0, 0):
            values = with_row(values, SLOT - 1, totals[2])
        put_slot(place, z, values)
    for start, rows, place, at in ATTN_BLOCKS[part]:
        if at == 0:
            put_slot(place, 2, grad_attn[start : start + rows])
    store = pltpu.make_async_copy(buffer_ref, payload_hbm, sems.at[9])
    store.start()
    store.wait()


def attend_part(flat, part, query, key, value, grad_att, ids, gains, raw, perm, grads, weight_in, dn, came):
    length, width = query.shape
    base, size = PARTS[part]
    final = part == len(PARTS) - 1
    block = pl.BlockSpec((length, size), lambda i: (0, base // size))
    vec = pl.BlockSpec((1, size), lambda i: (0, base // size))
    anywhere = pl.BlockSpec(memory_space=pl.ANY)
    dn_out = jax.ShapeDtypeStruct((length, width), BF16 if final else F32)
    payload = jax.ShapeDtypeStruct((TOK, length // TOK + SEQS_IN * 3 * SLOT, size), BF16)
    slots = length // came.shape[0]
    return pl.pallas_call(
        partial(part_kernel, flat, part),
        grid=(1,),
        in_specs=[block] * 4
        + [pl.BlockSpec((length, 1), lambda i: (0, 0)), vec, vec]
        + [anywhere] * 6,
        out_specs=[pl.BlockSpec(dn_out.shape, lambda i: (0, 0)), anywhere],
        out_shape=[dn_out, payload],
        scratch_shapes=[
            pltpu.VMEM((2, length, PAIR), BF16),
            pltpu.VMEM((2, length, PAIR), BF16),
            pltpu.VMEM((2, PAIR, length), BF16),
            pltpu.VMEM((2, PAIR, length), BF16),
            pltpu.VMEM((2, length, length), F32),
            pltpu.VMEM((2, length, length), BF16),
            pltpu.VMEM((length, 3 * size), BF16),
            pltpu.VMEM((length, 2 * size), F32),
            pltpu.VMEM(perm.shape, BF16),
            pltpu.VMEM((length, width), BF16),
            pltpu.VMEM((width, 3 * size), BF16),
            pltpu.VMEM((length, width), F32),
            pltpu.VMEM((came.shape[0], slots, width), BF16),
            pltpu.VMEM((length, size), BF16),
            pltpu.VMEM(payload.shape, BF16),
            pltpu.SemaphoreType.DMA((10,)),
        ],
        compiler_params=pltpu.CompilerParams(vmem_limit_bytes=VMEM_LIMIT),
        cost_estimate=pl.CostEstimate(
            flops=48 * length * length * size, bytes_accessed=24 * 2**20, transcendentals=0
        ),
        name=f"attend{part}",
    )(query, key, value, grad_att, ids, *gains, raw, perm, grads, weight_in, dn, came)


def close_kernel(
    x_ref, g_ref, gain_ref, wattn_ref, part_ref, bias_ref, dn_ref, dnq_ref, *rest
):
    *att_refs, out_ref, gin_ref = rest
    rows = x_ref[...].astype(F32)
    attended = [ref[...].reshape(ROWS, ref.shape[2]) for ref in att_refs]
    attended = jnp.concatenate(attended, axis=1)
    out = rows + dot(attended, wattn_ref[...]) + part_ref[...] + bias_ref[...]
    out_ref[...] = out.astype(BF16)
    hat, scale = standardize(rows)
    grad = (dn_ref[...] + dnq_ref[...].astype(F32)) * gain_ref[...]
    mean = jnp.mean(grad, axis=-1, keepdims=True)
    along = jnp.mean(grad * hat, axis=-1, keepdims=True)
    gin_ref[...] = g_ref[...].astype(F32) + scale * (grad - mean - hat * along)


def close(rows, grads, norm_gain, attended, weight_attn, partial_out, bias_down, dn, dn_heads):
    count, width = rows.shape
    whole = lambda i: (0, 0)
    block = pl.BlockSpec((ROWS, width), lambda i: (i, 0))
    slots = count // TOK
    parts = [pl.BlockSpec((ROWS // slots, slots, size), lambda i: (i, 0, 0)) for _, size in PARTS]
    vec = pl.BlockSpec((1, width), whole)
    square = pl.BlockSpec((width, width), whole)
    return pl.pallas_call(
        close_kernel,
        grid=(count // ROWS,),
        in_specs=[block, block, vec, square, block, vec, block, block] + parts,
        out_specs=[block, block],
        out_shape=[
            jax.ShapeDtypeStruct((count, width), BF16),
            jax.ShapeDtypeStruct((count, width), F32),
        ],
        compiler_params=pltpu.CompilerParams(vmem_limit_bytes=VMEM_LIMIT),
        cost_estimate=pl.CostEstimate(
            flops=2 * count * width * width, bytes_accessed=18 * 2**20, transcendentals=0
        ),
        name="close",
    )(rows, grads, norm_gain, weight_attn, partial_out, bias_down, dn, dn_heads, *attended)


def total(*values):
    return sum(value.astype(F32) for value in values)


def low(*values):
    return total(*values).astype(BF16)


def pick(values, bit, axis=0):
    return lax.dynamic_index_in_dim(values, bit, axis, keepdims=False)


def across(shift):
    return ("tok", [(i, i ^ shift) for i in range(TOK)])


def share_mlp(payload):
    (place,) = yield [(payload, "sum")]
    place = place[0]
    fill = jnp.zeros((HELD - 4 * SLOT, place.shape[1]), BF16)
    parts = jnp.concatenate(
        [
            *[place[: 4 * SLOT], fill],
            *[place[4 * SLOT : 8 * SLOT], fill],
            place[8 * SLOT + HELD :],
            place[8 * SLOT : 8 * SLOT + HELD],
        ]
    )
    (own,) = yield [(parts, "sum seq")]
    return own.astype(F32)


def share_heads(payload, slots):
    (came,) = yield [(payload, "home")]
    plane = low(jnp.sum(came[:, slots:].astype(F32), axis=0))
    return came, plane.reshape(SEQS_IN, 3, SLOT, -1)


def share_heads_seq(plane):
    z = lax.axis_index("seq")
    size = lax.axis_size("seq")
    part_of = lambda index: pick(plane, jnp.minimum(index, SEQS_IN - 1))
    came = yield [
        (part_of((z + step) % size), ("seq", [(i, (i + step) % size) for i in range(size)]))
        for step in range(1, size)
    ]
    return total(part_of(z), *came)


def share_attn(flat, slots):
    packed = jnp.stack(slots).astype(BF16)
    came = [lax.ppermute(packed, "tok", pairs) for pairs in flat.attn_rounds()]
    return [values.astype(F32) for values in came]


def regroup(rows):
    (came,) = yield [(rows, "home")]
    return came


def tie(*values):
    leaves, tree = jax.tree.flatten(values)
    return jax.tree.unflatten(tree, lax.optimization_barrier(leaves))


class Moving:
    def __init__(self, chain):
        self.chain = chain
        self.result = None
        self.wanted = next(chain)

    def send(self, operands):
        moved = []
        for operand, (_, way) in zip(operands, self.wanted):
            if way in ("sum", "sum seq"):
                axis = "tok" if way == "sum" else "seq"
                moved.append(lax.psum_scatter(operand, axis, scatter_dimension=0, tiled=True))
            elif way == "home":
                moved.append(lax.all_to_all(operand, "tok", split_axis=0, concat_axis=0, tiled=True))
            else:
                moved.append(lax.ppermute(operand, *way))
        return moved

    def take(self, moved):
        try:
            self.wanted = self.chain.send(moved)
        except StopIteration as end:
            self.wanted, self.result = None, end.value

    def finish(self):
        while self.wanted is not None:
            self.take(self.send([operand for operand, _ in self.wanted]))
        return self.result


def beside(work, inputs, moving, loose=()):
    chains = [*moving, *loose]
    operands = [[operand for operand, _ in chain.wanted] for chain in chains]
    inputs, operands = tie(inputs, operands)
    moved = [chain.send(operand) for chain, operand in zip(chains, operands)]
    done = work(*inputs)
    done, moved[: len(moving)] = tie(done, moved[: len(moving)])
    for chain, values in zip(chains, moved):
        chain.take(values)
    return done


def own_slice(flat, device, early, late, passed):
    width = flat.width

    def assemble(d, early, late, passed):
        z, place = divmod(d, TOK)
        first, end = flat.first(d), flat.first(d) + flat.rows
        pieces = []
        if first < 1:
            pieces.append((early[SLOT - 1] + late[-1][:, SLOT - 1].reshape(-1))[None])
        if first < flat.bias_at:
            columns = [slots[s] for s in range(3) for slots in late]
            columns += [early[c * SLOT : (c + 1) * SLOT] for c in range(flat.chunks)]
            base = 1 + flat.per_row * flat.input_row(d)
            rows = jnp.concatenate(columns, axis=1).reshape(-1, width)
            pieces.append(rows[max(first, 1) - base : min(end, flat.bias_at) - base])
        if first < flat.attn_at and end > flat.bias_at:
            at = 4 * SLOT
            pieces += [early[at + 16 * c][None] for c in range(flat.chunks)]
            for s in range(2):
                row = [slots[s, GAINS_ROW] for slots in late]
                pieces.append(jnp.concatenate(row)[None])
        if z == 2:
            for part, holder, at, count in flat.attn_pieces(place):
                source = late
                if holder != place:
                    pairs = flat.attn_rounds()
                    source = next(c for c, p in zip(passed, pairs) if (holder, place) in p)
                rows = source[part][:, at : at + count]
                pieces.append(jnp.concatenate([rows[s] for s in range(3)], axis=1))
        if end > flat.down_at:
            low = max(first, flat.down_at)
            start = flat.down_at + flat.down_start(d)
            pieces.append(early[low - start : end - start])
        rows = jnp.concatenate(pieces)
        skip = flat.skip(d)
        return rows.reshape(-1)[skip : skip + flat.total * width // flat.devices]

    branches = [partial(assemble, d) for d in range(flat.devices)]
    return lax.switch(device, branches, early, late, passed)


def sequence_device(
    layer_input,
    norm_gain,
    weight_in,
    bias_in,
    query_gain,
    key_gain,
    weight_attn,
    weight_down,
    bias_down,
    image_ids,
    cotangent,
):
    seqs, slots, width = layer_input.shape
    tok, z = lax.axis_index("tok"), lax.axis_index("seq")
    flat = Flat(width, weight_down.shape[0], lax.axis_size("seq") * TOK)
    features = jnp.array(flat.features(), jnp.int32)[:, None]

    def homeward(rows):
        return Moving(regroup(rows.reshape(seqs, slots, -1)))

    gain = norm_gain[None]
    gains = (query_gain[None], key_gain[None])
    marks = jnp.pad(image_ids.astype(BF16)[:, None], ((0, 0), (0, 15), (0, width - slots)))
    rows = layer_input.reshape(seqs * slots, width)
    grads = cotangent.reshape(seqs * slots, width)
    moving = Moving(regroup(jnp.concatenate([layer_input, cotangent, marks], axis=1)))
    part_out, dn, payload = beside(
        partial(mlp, flat),
        (rows, grads, gain, weight_in, bias_in[None], weight_down, features),
        [moving],
    )
    came = moving.result
    early = Moving(share_mlp(payload))
    plane_sums = early.send([operand for operand, _ in early.wanted])
    query, key, value, grad_att, raw, perm, seq_grads = heads(
        came, gain, weight_in, weight_attn, *gains, features
    )
    ids = came[:, 2 * slots, :slots].astype(jnp.int32).reshape(seqs * slots, 1)
    dn_heads = jnp.zeros((8, 128), F32)
    attended, late, chains = [], [], []
    for part in range(len(PARTS)):
        dn_heads, payload = beside(
            partial(attend_part, flat, part),
            (query, key, value, grad_att, ids, gains, raw, perm, seq_grads, weight_in, dn_heads, came),
            chains,
        )
        results = [chain.result for chain in chains]
        if part == len(PARTS) - 1:
            dn_heads, payload, plane_sums = tie(dn_heads, payload, plane_sums)
            early.take(plane_sums)
        chains = [Moving(share_heads(payload, slots))]
        if part > 0:
            attended.append(results[0][0])
            chains.append(Moving(share_heads_seq(results[0][1])))
        if part > 1:
            late.append(results[1])
    (last, before) = chains
    att, plane = last.finish()
    attended.append(att)
    home = homeward(dn_heads)
    (both,) = [Moving(share_heads_seq(plane))]
    late.append(before.finish())
    late.append(both.finish())
    passed = share_attn(flat, late)
    dn_heads = home.finish().reshape(seqs * slots, width)
    out, grad_input = close(
        rows, grads, gain, attended, weight_attn, part_out, bias_down[None], dn, dn_heads
    )
    grad_weights = own_slice(flat, z * TOK + tok, early.finish(), late, passed)
    shape = (seqs, slots, width)
    return (out.reshape(shape), grad_input.reshape(shape), grad_weights)


def per_device(layer_input, *rest):
    seqs, slots, _ = layer_input.shape
    if lax.axis_size("tok") == seqs == 8 and lax.axis_size("seq") == 4 and slots % 16 == 0:
        return sequence_device(layer_input, *rest)
    return units_device(layer_input, *rest)


def solution(mesh):
    placed = (
        P("seq", "tok", None),
        P(),
        P(),
        P(),
        P(),
        P(),
        P(),
        P(),
        P(),
        P("seq", "tok"),
        P("seq", "tok", None),
    )
    return jax.shard_map(
        per_device,
        mesh=mesh,
        in_specs=placed,
        out_specs=(P("seq", "tok", None), P("seq", "tok", None), P(("seq", "tok"))),
        check_vma=False,
    )
```

```python
from functools import partial

import jax
import jax.numpy as jnp
from jax import lax
from jax.experimental import pallas as pl
from jax.experimental.pallas import tpu as pltpu
from jax.sharding import PartitionSpec as P

HEADS = 12


EPS = 1e-06
NEG = -1e30

F32 = jnp.float32
BF16 = jnp.bfloat16
ROWS = 256
HEAD_DIM = 64
PAIR = 2 * HEAD_DIM
FAR = 192.0
VMEM_LIMIT = 60 * 1024 * 1024


def layer_norm(values, scaling):
    average = jnp.mean(values, axis=-1, keepdims=True)
    shifted = values - average
    spread = jnp.mean(shifted * shifted, axis=-1, keepdims=True)
    return shifted * lax.rsqrt(spread + EPS) * scaling


def head_norms(query_raw, key_raw, gain_query, gain_key):
    return (layer_norm(query_raw, gain_query), layer_norm(key_raw, gain_key))


def to_units(row_values, seq_count, head_count):
    part_len = row_values.shape[0] // seq_count
    shaped = row_values.reshape(seq_count, part_len, head_count, -1).transpose(0, 2, 3, 1)
    return shaped.reshape(seq_count * head_count, -1, part_len)


def from_units(unit_values, seq_count, head_count):
    part_len = unit_values.shape[2]
    shaped = unit_values.reshape(seq_count, head_count, -1, part_len).transpose(0, 3, 1, 2)
    return shaped.reshape(seq_count * part_len, -1)


def block_scores(query_block, key_unit, image_block, slot_ids, score_scale):
    scores = (
        lax.dot_general(
            query_block, key_unit, (((0,), (0,)), ((), ())), preferred_element_type=jnp.float32
        )
        * score_scale
    )
    allowed = image_block[:, None] == slot_ids[None, :]
    return (scores, allowed)


def split_blocks(unit_values, block_len):
    head_dim, length = unit_values.shape
    return unit_values.reshape(head_dim, length // block_len, block_len).transpose(1, 0, 2)


def attend_unit(packed, score_scale):
    query_unit, key_unit, value_unit, slot_ids = packed
    head_dim, length = query_unit.shape
    block_len = min(512, length)
    query_blocks = split_blocks(query_unit, block_len)
    image_blocks = slot_ids.reshape(length // block_len, block_len)

    def one_block(inputs):
        query_block, image_block = inputs
        scores, allowed = block_scores(query_block, key_unit, image_block, slot_ids, score_scale)
        scores = jnp.where(allowed, scores, NEG)
        row_max = jnp.max(scores, axis=-1, keepdims=True)
        shifted = jnp.exp(scores - row_max)
        row_total = jnp.sum(shifted, axis=-1, keepdims=True)
        weights = (shifted / row_total).astype(jnp.bfloat16)
        outputs = lax.dot_general(
            value_unit, weights, (((1,), (1,)), ((), ())), preferred_element_type=jnp.float32
        )
        return (outputs, row_max[:, 0] + jnp.log(row_total[:, 0]))

    outputs, log_total = lax.map(one_block, (query_blocks, image_blocks))
    return (outputs.transpose(1, 0, 2).reshape(head_dim, length), log_total.reshape(length))


def attend_back(packed, score_scale):
    query_unit, key_unit, value_unit, grad_unit, log_total, slot_ids = packed
    head_dim, length = query_unit.shape
    block_len = min(512, length)
    query_blocks = split_blocks(query_unit, block_len)
    grad_blocks = split_blocks(grad_unit, block_len)
    total_blocks = log_total.reshape(length // block_len, block_len)
    image_blocks = slot_ids.reshape(length // block_len, block_len)

    def one_block(carried, inputs):
        grad_key, grad_value = carried
        query_block, grad_block, total_block, image_block = inputs
        scores, allowed = block_scores(query_block, key_unit, image_block, slot_ids, score_scale)
        weights = jnp.where(allowed, jnp.exp(scores - total_block[:, None]), 0.0)
        weights_low = weights.astype(jnp.bfloat16)
        grad_weights = lax.dot_general(
            grad_block, value_unit, (((0,), (0,)), ((), ())), preferred_element_type=jnp.float32
        )
        inner = jnp.sum(weights * grad_weights, axis=-1, keepdims=True)
        grad_scores = (weights * (grad_weights - inner)).astype(jnp.bfloat16)
        grad_query = score_scale * lax.dot_general(
            key_unit, grad_scores, (((1,), (1,)), ((), ())), preferred_element_type=jnp.float32
        )
        grad_key = grad_key + score_scale * lax.dot_general(
            query_block, grad_scores, (((1,), (0,)), ((), ())), preferred_element_type=jnp.float32
        )
        grad_value = grad_value + lax.dot_general(
            grad_block, weights_low, (((1,), (0,)), ((), ())), preferred_element_type=jnp.float32
        )
        return ((grad_key, grad_value), grad_query)

    blank = jnp.zeros((head_dim, length), jnp.float32)
    (grad_key, grad_value), grad_query = lax.scan(
        one_block, (blank, blank), (query_blocks, grad_blocks, total_blocks, image_blocks)
    )
    return (grad_query.transpose(1, 0, 2).reshape(head_dim, length), grad_key, grad_value)


def reduce_grads(flat_grad):
    return lax.psum_scatter(flat_grad, ("seq", "tok"), scatter_dimension=0, tiled=True)


def units_device(
    layer_input,
    norm_gain,
    weight_in,
    bias_in,
    query_gain,
    key_gain,
    weight_attn,
    weight_down,
    bias_down,
    image_ids,
    cotangent,
):
    seq_count, part_len, model_width = layer_input.shape
    row_count = seq_count * part_len
    head_count = HEADS
    head_dim = model_width // head_count
    score_scale = head_dim ** (-0.5)
    whole_ids = lax.all_gather(image_ids, "tok", axis=1, tiled=True)
    unit_count = seq_count * head_count // lax.axis_size("tok")
    first_unit = lax.axis_index("tok") * unit_count
    unit_seq = (first_unit + jnp.arange(unit_count, dtype=jnp.int32)) // head_count
    unit_ids = jnp.take(whole_ids, unit_seq, axis=0)
    input_rows = layer_input.reshape(row_count, model_width).astype(jnp.float32)
    normalized_rows, input_back = jax.vjp(layer_norm, input_rows, norm_gain)
    normed_low = normalized_rows.astype(jnp.bfloat16)
    projected_rows = jnp.dot(normed_low, weight_in, preferred_element_type=jnp.float32)
    query_raw = projected_rows[:, :model_width].reshape(row_count, head_count, head_dim)
    key_raw = projected_rows[:, model_width : 2 * model_width].reshape(
        row_count, head_count, head_dim
    )
    value_low = projected_rows[:, 2 * model_width : 3 * model_width].astype(jnp.bfloat16)
    hidden_in = projected_rows[:, 3 * model_width :] + bias_in
    gain_query = query_gain.reshape(head_count, head_dim)
    gain_key = key_gain.reshape(head_count, head_dim)
    (query_normed, key_normed), heads_back = jax.vjp(
        head_norms, query_raw, key_raw, gain_query, gain_key
    )
    outgoing = (
        to_units(
            query_normed.reshape(row_count, model_width).astype(jnp.bfloat16), seq_count, head_count
        ),
        to_units(
            key_normed.reshape(row_count, model_width).astype(jnp.bfloat16), seq_count, head_count
        ),
        to_units(value_low, seq_count, head_count),
    )
    query_units, key_units, value_units = (
        lax.all_to_all(outgoing[0], "tok", split_axis=0, concat_axis=2, tiled=True),
        lax.all_to_all(outgoing[1], "tok", split_axis=0, concat_axis=2, tiled=True),
        lax.all_to_all(outgoing[2], "tok", split_axis=0, concat_axis=2, tiled=True),
    )
    attention_output, log_total = lax.map(
        partial(attend_unit, score_scale=score_scale),
        (query_units, key_units, value_units, unit_ids),
    )
    returned = lax.all_to_all(
        attention_output.astype(jnp.bfloat16), "tok", split_axis=2, concat_axis=0, tiled=True
    )
    attn_rows = from_units(returned, seq_count, head_count)
    activation, gelu_back = jax.vjp(partial(jax.nn.gelu, approximate=False), hidden_in)
    act_low = activation.astype(jnp.bfloat16)
    result_rows = input_rows + jnp.dot(attn_rows, weight_attn, preferred_element_type=jnp.float32)
    result_rows = (
        result_rows + jnp.dot(act_low, weight_down, preferred_element_type=jnp.float32) + bias_down
    )
    layer_output = result_rows.astype(jnp.bfloat16).reshape(seq_count, part_len, model_width)
    grad_rows = cotangent.reshape(row_count, model_width)
    grad_full = grad_rows.astype(jnp.float32)
    contract_rows = (((0,), (0,)), ((), ()))
    contract_cols = (((1,), (1,)), ((), ()))
    grad_bias_down = jnp.sum(grad_full, axis=0)
    grad_weight_down = lax.dot_general(
        act_low, grad_rows, contract_rows, preferred_element_type=jnp.float32
    )
    grad_weight_attn = lax.dot_general(
        attn_rows, grad_rows, contract_rows, preferred_element_type=jnp.float32
    )
    grad_activation = lax.dot_general(
        grad_rows, weight_down, contract_cols, preferred_element_type=jnp.float32
    )
    grad_hidden = gelu_back(grad_activation)[0]
    grad_bias_in = jnp.sum(grad_hidden, axis=0)
    grad_attended = lax.dot_general(
        grad_rows, weight_attn, contract_cols, preferred_element_type=jnp.float32
    )
    grad_units = lax.all_to_all(
        to_units(grad_attended.astype(jnp.bfloat16), seq_count, head_count),
        "tok",
        split_axis=0,
        concat_axis=2,
        tiled=True,
    )
    grad_query_u, grad_key_u, grad_value_u = lax.map(
        partial(attend_back, score_scale=score_scale),
        (query_units, key_units, value_units, grad_units, log_total, unit_ids),
    )
    back_query, back_key, back_value = (
        lax.all_to_all(
            grad_query_u.astype(jnp.bfloat16), "tok", split_axis=2, concat_axis=0, tiled=True
        ),
        lax.all_to_all(
            grad_key_u.astype(jnp.bfloat16), "tok", split_axis=2, concat_axis=0, tiled=True
        ),
        lax.all_to_all(
            grad_value_u.astype(jnp.bfloat16), "tok", split_axis=2, concat_axis=0, tiled=True
        ),
    )
    grad_query_n = (
        from_units(back_query, seq_count, head_count)
        .astype(jnp.float32)
        .reshape(row_count, head_count, head_dim)
    )
    grad_key_n = (
        from_units(back_key, seq_count, head_count)
        .astype(jnp.float32)
        .reshape(row_count, head_count, head_dim)
    )
    grad_value_rows = from_units(back_value, seq_count, head_count).astype(jnp.float32)
    grad_query_raw, grad_key_raw, grad_gain_query, grad_gain_key = heads_back(
        (grad_query_n, grad_key_n)
    )
    grad_projected = jnp.concatenate(
        [
            grad_query_raw.reshape(row_count, model_width),
            grad_key_raw.reshape(row_count, model_width),
            grad_value_rows,
            grad_hidden,
        ],
        axis=1,
    ).astype(jnp.bfloat16)
    grad_weight_in = lax.dot_general(
        normed_low, grad_projected, contract_rows, preferred_element_type=jnp.float32
    )
    grad_normed = lax.dot_general(
        grad_projected, weight_in, contract_cols, preferred_element_type=jnp.float32
    )
    grad_input_rows, grad_norm_gain = input_back(grad_normed)
    grad_input = (grad_full + grad_input_rows).reshape(seq_count, part_len, model_width)
    pieces = [
        grad_norm_gain,
        grad_weight_in,
        grad_bias_in,
        grad_gain_query,
        grad_gain_key,
        grad_weight_attn,
        grad_weight_down,
        grad_bias_down,
    ]
    flat_grad = jnp.concatenate([tensor.reshape(-1) for tensor in pieces])
    grad_weights = reduce_grads(flat_grad)
    return (layer_output, grad_input, grad_weights)


SLOT = 48
HELD = 304
PARTS = ((0, 256), (256, 256), (512, 256))
TOK = 8
SEQS_IN = 3
GAINS_ROW = 28
PLACE_ROWS = 4 * SLOT * 2 + 2 * HELD
ATTN_BLOCKS = (
    ((0, 48, 6, 0), (48, 48, 7, 0), (96, 48, 3, 0), (144, 48, 4, 0), (192, 48, 5, 0), (240, 16, 2, 32)),
    ((0, 48, 3, 0), (48, 48, 5, 0), (96, 48, 7, 0), (144, 48, 4, 0), (192, 48, 6, 0), (240, 16, 2, 32)),
    ((0, 48, 4, 0), (48, 48, 6, 0), (96, 48, 7, 0), (144, 48, 5, 0), (192, 48, 3, 0), (240, 16, 2, 32)),
)


class Flat:
    def __init__(self, width, hidden, devices):
        self.width = width
        self.chunks = hidden // width
        self.per_row = 3 + self.chunks
        self.bias_at = 1 + self.per_row * width
        self.gains_at = self.bias_at + self.chunks
        self.attn_at = self.gains_at + 2
        self.down_at = self.attn_at + width
        self.total = self.down_at + hidden + 1
        self.devices = devices
        self.rows = self.total // devices + 1

    def first(self, device):
        return device * self.total // self.devices

    def skip(self, device):
        return (device * self.total) % self.devices * self.width // self.devices

    def input_row(self, device):
        return max(0, (self.first(device) - 1) // self.per_row)

    def slots(self):
        pairs = [(place, z) for place in range(TOK) for z in range(3)]
        return [(place, z) for place, z in pairs if self.first(z * TOK + place) < self.bias_at]

    def features(self):
        return [self.input_row(z * TOK + place) + i for place, z in self.slots() for i in range(SLOT)]

    def bias_place(self):
        return next(d for d in range(self.devices) if self.first(d + 1) > self.bias_at) % TOK

    def down_start(self, device):
        start = self.first(device) - self.down_at
        return None if start + self.rows <= 0 else max(0, start) // 16 * 16

    def attn_pieces(self, place):
        low = self.first(2 * TOK + place) - self.attn_at
        high = low + self.rows
        found = []
        for part, (base, _) in enumerate(PARTS):
            for start, rows, holder, at in ATTN_BLOCKS[part]:
                begin, end = max(base + start, low), min(base + start + rows, high)
                if begin < end:
                    found.append((part, holder, at + begin - base - start, end - begin))
        return found

    def attn_rounds(self):
        pairs = {(h, p) for p in range(TOK) for _, h, _, _ in self.attn_pieces(p) if h != p}
        degree = lambda pair: sum((pair[0] == h) + (pair[1] == p) for h, p in pairs)
        rounds = []
        for holder, place in sorted(pairs, key=lambda pair: (-degree(pair), pair)):
            for taken in rounds:
                if all(holder != h and place != p for h, p in taken):
                    taken.append((holder, place))
                    break
            else:
                rounds.append([(holder, place)])
        return rounds


def side_of(place, core):
    return core if place % 2 == 0 else 1 - core


def selection(features_ref, width):
    columns = lax.broadcasted_iota(jnp.int32, (features_ref.shape[0], width), 1)
    return jnp.where(columns == features_ref[...], 1.0, 0.0).astype(BF16)


def dot(left, right):
    return jnp.dot(left, right, preferred_element_type=F32)


def dot_nt(left, right):
    return lax.dot_general(left, right, (((1,), (1,)), ((), ())), preferred_element_type=F32)


def dot_tn(left, right):
    return lax.dot_general(left, right, (((0,), (0,)), ((), ())), preferred_element_type=F32)


def standardize(rows):
    shifted = rows - jnp.mean(rows, axis=-1, keepdims=True)
    scale = lax.rsqrt(jnp.mean(shifted * shifted, axis=-1, keepdims=True) + EPS)
    return shifted * scale, scale


def head_means(values):
    width = min(4 * HEAD_DIM, values.shape[1])
    row = lax.broadcasted_iota(jnp.int32, (width, width), 0)
    column = lax.broadcasted_iota(jnp.int32, (width, width), 1)
    ones = jnp.where((row >> 6) == (column >> 6), 1.0, 0.0).astype(BF16)
    values = values.astype(BF16)
    parts = [
        dot(values[:, start : start + width], ones) for start in range(0, values.shape[1], width)
    ]
    return jnp.concatenate(parts, axis=1) * (1.0 / HEAD_DIM)


def head_standardize(raw):
    shifted = raw - head_means(raw)
    scale = lax.rsqrt(head_means(shifted * shifted) + EPS)
    return shifted * scale, scale


def gelu_pair(pre):
    phi = 0.5 + 0.5 * lax.erf(pre * (0.5**0.5))
    density = jnp.exp(-0.5 * pre * pre) * 0.3989422804014327
    return pre * phi, phi + pre * density


def with_row(values, row, vector):
    index = lax.broadcasted_iota(jnp.int32, values.shape, 0)
    return jnp.where(index == row, vector, values)


def mlp_kernel(
    flat, x_ref, g_ref, gain_ref, wh_ref, bias_ref, wd_ref, features_ref,
    out_ref, dn_ref, payload_ref,
    norm_ref, perm_ref, act_ref, dh_ref, gbd_ref, buffer_ref, sems,
):
    step = pl.program_id(0)
    last = flat.chunks - 1
    width = flat.width
    count = x_ref.shape[0] // ROWS

    @pl.when(step == 0)
    def _():
        gbd_ref[...] = jnp.zeros_like(gbd_ref)
        buffer_ref[:, 8 * SLOT + HELD :] = jnp.zeros((TOK, HELD, width), BF16)

        def block(i, carry):
            rows = pl.ds(pl.multiple_of(i * ROWS, ROWS), ROWS)
            hat, _ = standardize(x_ref[rows].astype(F32))
            norm_ref[rows] = (hat * gain_ref[...]).astype(BF16)
            out_ref[rows] = jnp.zeros_like(out_ref[rows])
            dn_ref[rows] = jnp.zeros_like(dn_ref[rows])
            gbd_ref[...] += jnp.sum(g_ref[rows].astype(F32), axis=0, keepdims=True)
            return carry

        lax.fori_loop(0, count, block, 0)
        perm_ref[...] = dot_nt(selection(features_ref, width), norm_ref[...]).astype(BF16)

    def products(i):
        rows = slice(i * ROWS, (i + 1) * ROWS)
        pre = dot(norm_ref[rows], wh_ref[...]) + bias_ref[...]
        return pre, dot_nt(g_ref[rows], wd_ref[...])

    grad_bias = jnp.zeros((1, width), F32)
    ahead = products(0)
    for i in range(count):
        rows = slice(i * ROWS, (i + 1) * ROWS)
        pre, dh = ahead
        if i + 1 < count:
            ahead = products(i + 1)
        act, slope = gelu_pair(pre)
        act_low = act.astype(BF16)
        dh = dh * slope
        dh_low = dh.astype(BF16)
        act_ref[rows] = act_low
        dh_ref[rows] = dh_low
        out_ref[rows] += dot(act_low, wd_ref[...])
        dn_ref[rows] += dot_nt(dh_low, wh_ref[...])
        grad_bias += jnp.sum(dh, axis=0, keepdims=True)

    def store(index, row, rows, place=None):
        places = slice(None) if place is None else place
        return pltpu.make_async_copy(
            buffer_ref.at[places, pl.ds(row, rows)], payload_ref.at[places, pl.ds(row, rows)], sems.at[index]
        )

    mixed = 8 * SLOT + HELD
    inputs = lambda chunk: [store(2 * chunk + z, (4 * z + chunk) * SLOT, SLOT) for z in range(2)]
    done = [[] for _ in range(flat.chunks)]
    for place in range(TOK):
        start = flat.down_start(3 * TOK + place)
        chunk = min((start + HELD - 1) // width, last)
        done[chunk].append((2 * flat.chunks + place, 8 * SLOT, HELD, place))
        start = flat.down_start(2 * TOK + place)
        chunk = last if start is None else min((start + HELD - 1) // width, last)
        done[chunk].append((2 * flat.chunks + TOK + place, mixed, HELD, place))

    grad_down = dot_tn(act_ref[...], g_ref[...])
    grad_in = dot(perm_ref[...], dh_ref[...])
    shift = pl.multiple_of(step * SLOT, SLOT)
    for index, (place, z) in enumerate(flat.slots()):
        part = grad_in[index * SLOT : (index + 1) * SLOT]
        at = z * 4 * SLOT if z < 2 else mixed
        buffer_ref[place, pl.ds(at + shift, SLOT)] = part.astype(BF16)

    for chunk in range(flat.chunks):

        @pl.when(step == chunk)
        def _():
            low = chunk * width
            for device in range(2 * TOK, 4 * TOK):
                start = flat.down_start(device)
                if start is None:
                    continue
                place, at = device % TOK, 8 * SLOT if device >= 3 * TOK else mixed
                begin, end = max(start, low), min(start + HELD, low + width)
                if begin < end:
                    part = grad_down[begin - low : end - low].astype(BF16)
                    buffer_ref[place, at + begin - start : at + end - start] = part
                if chunk == last and start + HELD > low + width:
                    tail = with_row(jnp.zeros((16, width), F32), 0, gbd_ref[...])
                    row = at + low + width - start
                    buffer_ref[place, row : row + 16] = tail.astype(BF16)
            tail = with_row(jnp.zeros((16, width), F32), 0, grad_bias).astype(BF16)
            at = mixed + 4 * SLOT + 16 * chunk
            buffer_ref[flat.bias_place(), at : at + 16] = tail
            if chunk == 0:
                inputs(0)[1].start()
            else:
                for copy in inputs(chunk):
                    copy.start()
            for args in done[chunk]:
                store(*args).start()

    @pl.when(step == last)
    def _():
        def block(i, total):
            rows = pl.ds(pl.multiple_of(i * ROWS, ROWS), ROWS)
            hat, _ = standardize(x_ref[rows].astype(F32))
            return total + jnp.sum(dn_ref[rows] * hat, axis=0, keepdims=True)

        total = lax.fori_loop(0, count, block, jnp.zeros((1, width), F32))
        kept = buffer_ref[0, SLOT - 16 : SLOT].astype(F32)
        buffer_ref[0, SLOT - 16 : SLOT] = with_row(kept, 15, total).astype(BF16)
        inputs(0)[0].start()
        for chunk in range(flat.chunks):
            for copy in inputs(chunk):
                copy.wait()
            for args in done[chunk]:
                store(*args).wait()


def mlp(flat, rows, grads, norm_gain, weight_in, bias_in, weight_down, features):
    count, width = rows.shape
    chunks = flat.chunks
    whole = lambda i: (0, 0)
    once = pl.Buffered(1)
    full = pl.BlockSpec((count, width), whole, pipeline_mode=once)
    payload = jax.ShapeDtypeStruct((TOK, PLACE_ROWS, width), BF16)
    return pl.pallas_call(
        partial(mlp_kernel, flat),
        grid=(chunks,),
        in_specs=[
            full,
            full,
            pl.BlockSpec((1, width), whole),
            pl.BlockSpec((width, width), lambda i: (0, i + 3)),
            pl.BlockSpec((1, width), lambda i: (0, i)),
            pl.BlockSpec((width, width), lambda i: (i, 0)),
            pl.BlockSpec(features.shape, whole, pipeline_mode=once),
        ],
        out_specs=[
            pl.BlockSpec((count, width), whole),
            pl.BlockSpec((count, width), whole),
            pl.BlockSpec(memory_space=pl.ANY),
        ],
        out_shape=[
            jax.ShapeDtypeStruct((count, width), F32),
            jax.ShapeDtypeStruct((count, width), F32),
            payload,
        ],
        scratch_shapes=[
            pltpu.VMEM((count, width), BF16),
            pltpu.VMEM((features.shape[0], count), BF16),
            pltpu.VMEM((count, width), BF16),
            pltpu.VMEM((count, width), BF16),
            pltpu.VMEM((1, width), F32),
            pltpu.VMEM(payload.shape, BF16),
            pltpu.SemaphoreType.DMA((2 * chunks + 2 * TOK,)),
        ],
        compiler_params=pltpu.CompilerParams(vmem_limit_bytes=VMEM_LIMIT),
        cost_estimate=pl.CostEstimate(
            flops=12 * count * width * width * chunks, bytes_accessed=32 * 2**20, transcendentals=0
        ),
        name="mlp",
    )(rows, grads, norm_gain, weight_in, bias_in, weight_down, features)


def heads_kernel(
    x_ref, g_ref, gain_ref, wqkv_ref, wattn_ref, qgain_ref, kgain_ref, features_ref, marks_ref,
    q_ref, k_ref, v_ref, do_ref, raw_ref, perm_ref, ids_ref,
    pick_ref,
):
    width = x_ref.shape[2]

    @pl.when(pl.program_id(0) == 0)
    def _():
        pick_ref[...] = selection(features_ref, width)

    slots = x_ref.shape[1]
    for group in range(x_ref.shape[0]):
        ids = marks_ref[group, :1, :slots].astype(F32)
        ids_ref[group * slots : (group + 1) * slots] = jnp.broadcast_to(ids, (PAIR, slots)).T
    hat, _ = standardize(x_ref[...].reshape(ROWS, width).astype(F32))
    normed = (hat * gain_ref[...]).astype(BF16)
    grads = g_ref[...].reshape(ROWS, width)
    perm_ref[...] = dot_nt(pick_ref[...], normed).astype(BF16)
    q_raw = dot(normed, wqkv_ref[:, :width])
    raw_ref[:, :width] = q_raw
    q_ref[...] = (head_standardize(q_raw)[0] * qgain_ref[...]).astype(BF16)
    k_raw = dot(normed, wqkv_ref[:, width : 2 * width])
    raw_ref[:, width:] = k_raw
    k_ref[...] = (head_standardize(k_raw)[0] * kgain_ref[...]).astype(BF16)
    v_ref[...] = dot(normed, wqkv_ref[:, 2 * width :]).astype(BF16)
    do_ref[...] = dot_nt(grads, wattn_ref[...]).astype(BF16)


def heads(came, norm_gain, weight_in, weight_attn, query_gain, key_gain, features):
    seqs, held, width = came.shape
    slots = held // 2 // 16 * 16
    count = seqs * slots
    whole = lambda i: (0, 0)
    block = pl.BlockSpec((ROWS, width), lambda i: (i, 0))
    vec = pl.BlockSpec((1, width), whole)
    low = jax.ShapeDtypeStruct((count, width), BF16)
    group = (ROWS // slots, slots, width)
    return pl.pallas_call(
        heads_kernel,
        grid=(count // ROWS,),
        in_specs=[
            pl.BlockSpec(group, lambda i: (i, 0, 0)),
            pl.BlockSpec(group, lambda i: (i, 1, 0)),
            vec,
            pl.BlockSpec((width, 3 * width), whole),
            pl.BlockSpec((width, width), whole),
            vec,
            vec,
            pl.BlockSpec(features.shape, whole),
            pl.BlockSpec((ROWS // slots, 16, width), lambda i: (i, 2 * slots // 16, 0)),
        ],
        out_specs=[block] * 4
        + [
            pl.BlockSpec((ROWS, 2 * width), lambda i: (i, 0)),
            pl.BlockSpec((features.shape[0], ROWS), lambda i: (0, i)),
            pl.BlockSpec((ROWS, PAIR), lambda i: (i, 0)),
        ],
        out_shape=[low] * 4
        + [
            jax.ShapeDtypeStruct((count, 2 * width), F32),
            jax.ShapeDtypeStruct((features.shape[0], count), BF16),
            jax.ShapeDtypeStruct((count, PAIR), F32),
        ],
        scratch_shapes=[pltpu.VMEM((features.shape[0], width), BF16)],
        compiler_params=pltpu.CompilerParams(vmem_limit_bytes=VMEM_LIMIT),
        cost_estimate=pl.CostEstimate(
            flops=10 * count * width * width, bytes_accessed=26 * 2**20, transcendentals=0
        ),
        name="heads",
    )(came, came, norm_gain, weight_in, weight_attn, query_gain, key_gain, features, came)


def part_kernel(
    flat, part, core_ref, q_ref, k_ref, v_ref, do_ref, ids_ref, qgain_ref, kgain_ref,
    raw_hbm, perm_hbm, win_hbm, dn_hbm, came_hbm, att_hbm,
    *rest,
):
    length, size = q_ref.shape
    width = flat.width
    base = PARTS[part][0]
    final = part == len(PARTS) - 1
    if final:
        home_hbm, mine_hbm, theirs_hbm, *rest = rest
        *rest, att_ref, before_ref, dn_out_ref = rest
    else:
        dn_out_ref, att_ref, mine_hbm, theirs_hbm, *rest = rest
    ka_ref, va_ref, kat_ref, vat_ref, p_ref, plow_ref, d_ref, *rest = rest
    raw_ref, perm_ref, g_ref, w_ref, dn_ref, x_ref, buffer_ref, sems = rest

    core = core_ref[0]
    slots = length // TOK
    loads = {
        "raw": [
            pltpu.make_async_copy(
                raw_hbm.at[:, pl.ds(s * width + base, size)],
                raw_ref.at[:, pl.ds(s * size, size)],
                sems.at[s],
            )
            for s in range(2)
        ],
        "w": [
            pltpu.make_async_copy(
                win_hbm.at[:, pl.ds(s * width + base, size)],
                w_ref.at[:, pl.ds(s * size, size)],
                sems.at[2 + s],
            )
            for s in range(3)
        ],
        "perm": [pltpu.make_async_copy(perm_hbm, perm_ref, sems.at[5])],
        "g": [pltpu.make_async_copy(came_hbm.at[:, pl.ds(slots, slots)], g_ref, sems.at[6])],
    }
    if part:
        loads["dn"] = [pltpu.make_async_copy(dn_hbm, dn_ref, sems.at[7])]
    if final:
        loads["x"] = [pltpu.make_async_copy(came_hbm.at[:, pl.ds(0, slots)], x_ref, sems.at[8])]
        loads["att"] = [pltpu.make_async_copy(att_hbm, before_ref, sems.at[9])]
    for group in loads.values():
        for copy in group:
            copy.start()

    def arrived(name):
        for copy in loads[name]:
            copy.wait()

    def lanes(count, head):
        lane = lax.broadcasted_iota(jnp.int32, (count, PAIR), 1)
        return (lane >> 6) == head, lane - (1 - head) * HEAD_DIM

    ids = ids_ref[...].astype(jnp.int32) + 1
    count = size // HEAD_DIM

    def widen(item):
        head, pair = item % 2, slice(item // 2 * PAIR, (item // 2 + 1) * PAIR)
        mine, spare = lanes(length, head)
        marks = jnp.where(spare == ids, 1.0, jnp.where(spare == 17, -FAR, 0.0))
        ka = jnp.where(mine, k_ref[:, pair].astype(F32), marks)
        ka_ref[item % 2] = ka.astype(BF16)
        kat_ref[item % 2] = ka.T.astype(BF16)
        marks = jnp.where((spare == 0) | (spare == 1), 1.0, 0.0)
        va = jnp.where(mine, v_ref[:, pair].astype(F32), marks)
        va_ref[item % 2] = va.astype(BF16)
        vat_ref[item % 2] = va.T.astype(BF16)
        marks = jnp.where(spare == ids, FAR, jnp.where(spare == 17, 1.0, 0.0))
        return jnp.where(mine, q_ref[:, pair].astype(F32) * (HEAD_DIM**-0.5), marks).astype(BF16)

    def score(item, qa):
        grown = jnp.exp(dot_nt(ka_ref[item % 2], qa))
        p_ref[item % 2] = grown
        low = grown.astype(BF16)
        plow_ref[item % 2] = low
        return dot(vat_ref[item % 2], low)

    def middle(item, sums):
        head, pair = item % 2, slice(item // 2 * PAIR, (item // 2 + 1) * PAIR)
        mine, spare = lanes(length, head)
        grad = do_ref[:, pair].astype(F32)
        out = sums.T
        first = (1 - head) * HEAD_DIM
        inverse = 1.0 / out[:, first : first + 1]
        out = out * inverse
        inner = jnp.sum(jnp.where(mine, grad * out, 0.0), axis=-1, keepdims=True)
        offset = -inner * inverse
        high = offset.astype(BF16).astype(F32)
        marks = jnp.where(spare == 0, high, jnp.where(spare == 1, offset - high, 0.0))
        return out, jnp.where(mine, grad * inverse, marks).astype(BF16)

    def gradients(item, qa, grad_a):
        ds = (p_ref[item % 2] * dot_nt(va_ref[item % 2], grad_a)).astype(BF16)
        dv = dot(plow_ref[item % 2], grad_a)
        dk = dot(ds, qa)
        dq = dot(kat_ref[item % 2], ds).T * (HEAD_DIM**-0.5)
        return dq, dk, dv

    qa = widen(0)
    sums = score(0, qa)
    kept = None
    for item in range(count):
        out, grad_a = middle(item, sums)
        now = gradients(item, qa, grad_a)
        if item + 1 < count:
            qa = widen(item + 1)
            sums = score(item + 1, qa)
        if item % 2 == 0:
            kept = (out, *now)
        else:
            mine, _ = lanes(length, 0)
            start = item // 2 * PAIR
            att_ref[:, start : start + PAIR] = jnp.where(mine, kept[0], out).astype(BF16)
            for side in range(3):
                both = jnp.where(mine, kept[1 + side], now[side]).astype(BF16)
                d_ref[:, side * size + start : side * size + start + PAIR] = both

    arrived("raw")
    arrived("w")
    if part:
        arrived("dn")
    if final:
        arrived("x")
        group = ROWS // x_ref.shape[1]

    def block(i, totals):
        rows = pl.ds(pl.multiple_of(i * ROWS, ROWS), ROWS)
        totals = list(totals)
        for side, gain_ref in enumerate((qgain_ref, kgain_ref)):
            lane = slice(side * size, (side + 1) * size)
            hat, scale = head_standardize(raw_ref[rows, lane])
            grad = d_ref[rows, lane].astype(F32)
            totals[side] += jnp.sum(grad * hat, axis=0, keepdims=True)
            grad = grad * gain_ref[...]
            grad = scale * (grad - head_means(grad) - hat * head_means(grad * hat))
            d_ref[rows, lane] = grad.astype(BF16)
        dn = dot_nt(d_ref[rows], w_ref[...])
        if part:
            dn = dn + dn_ref[rows]
        if final:
            x = x_ref[pl.ds(i * group, group)].reshape(ROWS, width).astype(F32)
            totals[2] += jnp.sum(dn * standardize(x)[0], axis=0, keepdims=True)
        dn_out_ref[rows] = dn.astype(dn_out_ref.dtype)
        return tuple(totals)

    zero = jnp.zeros((1, size), F32)
    totals = lax.fori_loop(0, length // ROWS, block, (zero, zero, jnp.zeros((1, width), F32)))

    if final:
        arrived("att")
        homeward = [
            pltpu.make_async_copy(before_ref, home_hbm.at[:, pl.ds(width + size, size)], sems.at[8]),
            pltpu.make_async_copy(dn_out_ref, home_hbm.at[:, pl.ds(0, width)], sems.at[12]),
            pltpu.make_async_copy(att_ref, home_hbm.at[:, pl.ds(width, size)], sems.at[13]),
        ]
        for copy in homeward:
            copy.start()
    arrived("perm")
    arrived("g")
    def put_slot(place, z, values):
        for s in range(3):
            row = (3 * z + s) * SLOT
            part = values[:, s * size : (s + 1) * size].astype(BF16)
            buffer_ref[side_of(place, core), place // 2, row : row + values.shape[0]] = part

    grad_in = dot(perm_ref[...], d_ref[...])
    grad_attn = dot_tn(att_ref[...], g_ref[...].reshape(length, width))
    gains = jnp.concatenate([totals[0], totals[1], zero], axis=1)
    for index, (place, z) in enumerate(flat.slots()):
        values = grad_in[index * SLOT : (index + 1) * SLOT]
        if (place, z) == (flat.bias_place(), 2):
            start, rows, _, at = ATTN_BLOCKS[part][-1]
            values = jnp.concatenate([values[:at], grad_attn[start : start + rows]])
            values = with_row(values, GAINS_ROW, gains)
        if final and (place, z) == (0, 0):
            values = with_row(values, SLOT - 1, totals[2])
        put_slot(place, z, values)
    for start, rows, place, at in ATTN_BLOCKS[part]:
        if at == 0:
            put_slot(place, 2, grad_attn[start : start + rows])
    stores = [
        pltpu.make_async_copy(buffer_ref.at[side], ref, sems.at[10 + side])
        for side, ref in enumerate((mine_hbm, theirs_hbm))
    ]
    for copy in stores:
        copy.start()
    if final:
        stores += homeward
    for copy in stores:
        copy.wait()


def attend_part(
    flat, part, core, query, key, value, grad_att, ids, gains, raw, perm, weight_in, dn, came, att
):
    length, width = query.shape
    base, size = PARTS[part]
    final = part == len(PARTS) - 1
    block = pl.BlockSpec((length, size), lambda i: (0, base // size))
    vec = pl.BlockSpec((1, size), lambda i: (0, base // size))
    anywhere = pl.BlockSpec(memory_space=pl.ANY)
    payload = jax.ShapeDtypeStruct((TOK // 2, SEQS_IN * 3 * SLOT, size), BF16)
    in_vmem = lambda shape: pl.BlockSpec(shape.shape, lambda i: (0, 0))
    if final:
        results = [jax.ShapeDtypeStruct((length, width + 2 * size), BF16)]
        specs = [anywhere]
        scratch = [pltpu.VMEM((length, size), BF16)] * 2 + [pltpu.VMEM((length, width), BF16)]
    else:
        results = [
            jax.ShapeDtypeStruct((length, width), F32),
            jax.ShapeDtypeStruct((length, size), BF16),
        ]
        specs = [in_vmem(shape) for shape in results]
        scratch = []
    slots = length // came.shape[0]
    return pl.pallas_call(
        partial(part_kernel, flat, part),
        grid=(1,),
        in_specs=[pl.BlockSpec(memory_space=pltpu.SMEM)]
        + [block] * 4
        + [pl.BlockSpec((length, PAIR), lambda i: (0, 0)), vec, vec]
        + [anywhere] * 6,
        out_specs=[*specs, anywhere, anywhere],
        out_shape=[*results, payload, payload],
        scratch_shapes=[
            pltpu.VMEM((2, length, PAIR), BF16),
            pltpu.VMEM((2, length, PAIR), BF16),
            pltpu.VMEM((2, PAIR, length), BF16),
            pltpu.VMEM((2, PAIR, length), BF16),
            pltpu.VMEM((2, length, length), F32),
            pltpu.VMEM((2, length, length), BF16),
            pltpu.VMEM((length, 3 * size), BF16),
            pltpu.VMEM((length, 2 * size), F32),
            pltpu.VMEM(perm.shape, BF16),
            pltpu.VMEM((came.shape[0], slots, width), BF16),
            pltpu.VMEM((width, 3 * size), BF16),
            pltpu.VMEM((length, width), F32),
            pltpu.VMEM((came.shape[0], slots, width), BF16),
            pltpu.VMEM((2, *payload.shape), BF16),
            pltpu.SemaphoreType.DMA((14,)),
            *scratch,
        ],
        compiler_params=pltpu.CompilerParams(vmem_limit_bytes=VMEM_LIMIT),
        cost_estimate=pl.CostEstimate(
            flops=48 * length * length * size, bytes_accessed=24 * 2**20, transcendentals=0
        ),
        name=f"attend{part}",
    )(core, query, key, value, grad_att, ids, *gains, raw, perm, weight_in, dn, came, att)


def close_kernel(
    x_ref, g_ref, gain_ref, wattn_ref, part_ref, bias_ref, dn_ref, att0_ref, home_ref,
    out_ref, gin_ref,
):
    width = x_ref.shape[1]
    size = att0_ref.shape[1]
    rows = x_ref[...].astype(F32)
    this, before = home_ref[:, width : width + size], home_ref[:, width + size :]
    attended = jnp.concatenate([att0_ref[...], before, this], axis=1)
    out = rows + dot(attended, wattn_ref[...]) + part_ref[...] + bias_ref[...]
    out_ref[...] = out.astype(BF16)
    hat, scale = standardize(rows)
    grad = (dn_ref[...] + home_ref[:, :width].astype(F32)) * gain_ref[...]
    mean = jnp.mean(grad, axis=-1, keepdims=True)
    along = jnp.mean(grad * hat, axis=-1, keepdims=True)
    gin_ref[...] = g_ref[...].astype(F32) + scale * (grad - mean - hat * along)


def close(rows, grads, norm_gain, weight_attn, partial_out, bias_down, dn, first, home):
    count, width = rows.shape
    whole = lambda i: (0, 0)
    block = pl.BlockSpec((ROWS, width), lambda i: (i, 0))
    columns = lambda values: pl.BlockSpec((ROWS, values.shape[1]), lambda i: (i, 0))
    vec = pl.BlockSpec((1, width), whole)
    square = pl.BlockSpec((width, width), whole)
    return pl.pallas_call(
        close_kernel,
        grid=(count // ROWS,),
        in_specs=[block, block, vec, square, block, vec, block, columns(first), columns(home)],
        out_specs=[block, block],
        out_shape=[
            jax.ShapeDtypeStruct((count, width), BF16),
            jax.ShapeDtypeStruct((count, width), F32),
        ],
        compiler_params=pltpu.CompilerParams(vmem_limit_bytes=VMEM_LIMIT),
        cost_estimate=pl.CostEstimate(
            flops=2 * count * width * width, bytes_accessed=18 * 2**20, transcendentals=0
        ),
        name="close",
    )(rows, grads, norm_gain, weight_attn, partial_out, bias_down, dn, first, home)


def total(*values):
    return sum(value.astype(F32) for value in values)


def low(*values):
    return total(*values).astype(BF16)


def pick(values, bit, axis=0):
    return lax.dynamic_index_in_dim(values, bit, axis, keepdims=False)


def across(shift):
    return ("tok", [(i, i ^ shift) for i in range(TOK)])


def share_mlp(payload):
    (place,) = yield [(payload, "sum")]
    (own,) = yield [(by_seq(place[0]), "sum seq")]
    return own.astype(F32)


def by_seq_kernel(place_ref, out_ref):
    fill = jnp.zeros((HELD - 4 * SLOT, place_ref.shape[1]), BF16)
    for z in range(2):
        out_ref[z * HELD : z * HELD + 4 * SLOT] = place_ref[z * 4 * SLOT : (z + 1) * 4 * SLOT]
        out_ref[z * HELD + 4 * SLOT : (z + 1) * HELD] = fill
    out_ref[2 * HELD : 3 * HELD] = place_ref[8 * SLOT + HELD :]
    out_ref[3 * HELD :] = place_ref[8 * SLOT : 8 * SLOT + HELD]


def by_seq(place):
    return pl.pallas_call(
        by_seq_kernel,
        out_shape=jax.ShapeDtypeStruct((4 * HELD, place.shape[1]), BF16),
        name="by_seq",
    )(place)


def share_heads_core(mine, theirs):
    (came,) = yield [(theirs, across(1))]
    return low(mine, came)


def share_heads_plane(chips):
    (came,) = yield [(chips, "chips")]
    return low(jnp.sum(came.astype(F32), axis=0))


def share_heads_seq(plane):
    z = lax.axis_index("seq")
    size = lax.axis_size("seq")
    part_of = lambda index: pick(plane, jnp.minimum(index, SEQS_IN - 1))
    came = yield [
        (part_of((z + step) % size), ("seq", [(i, (i + step) % size) for i in range(size)]))
        for step in range(1, size)
    ]
    return total(part_of(z), *came)


def share_attn(flat, slots):
    packed = jnp.stack(slots).astype(BF16)
    came = [lax.ppermute(packed, "tok", pairs) for pairs in flat.attn_rounds()]
    return [values.astype(F32) for values in came]


def regroup(rows):
    (came,) = yield [(rows, "home")]
    return came


def tie(*values):
    leaves, tree = jax.tree.flatten(values)
    return jax.tree.unflatten(tree, lax.optimization_barrier(leaves))


class Moving:
    def __init__(self, chain):
        self.chain = chain
        self.result = None
        self.wanted = next(chain)

    def send(self, operands):
        moved = []
        for operand, (_, way) in zip(operands, self.wanted):
            if way in ("sum", "sum seq"):
                axis = "tok" if way == "sum" else "seq"
                moved.append(lax.psum_scatter(operand, axis, scatter_dimension=0, tiled=True))
            elif way == "chips":
                cores = [[2 * chip + core for chip in range(TOK // 2)] for core in range(2)]
                moved.append(
                    lax.all_to_all(
                        operand, "tok", split_axis=0, concat_axis=0, tiled=True, axis_index_groups=cores
                    )
                )
            elif way == "home":
                moved.append(lax.all_to_all(operand, "tok", split_axis=0, concat_axis=0, tiled=True))
            else:
                moved.append(lax.ppermute(operand, *way))
        return moved

    def take(self, moved):
        try:
            self.wanted = self.chain.send(moved)
        except StopIteration as end:
            self.wanted, self.result = None, end.value

    def finish(self):
        while self.wanted is not None:
            self.take(self.send([operand for operand, _ in self.wanted]))
        return self.result


def beside(work, inputs, moving, loose=()):
    chains = [*moving, *loose]
    operands = [[operand for operand, _ in chain.wanted] for chain in chains]
    inputs, operands = tie(inputs, operands)
    moved = [chain.send(operand) for chain, operand in zip(chains, operands)]
    done = work(*inputs)
    done, moved[: len(moving)] = tie(done, moved[: len(moving)])
    for chain, values in zip(chains, moved):
        chain.take(values)
    return done


def own_slice(flat, device, early, late, passed):
    width = flat.width

    def assemble(d, early, late, passed):
        z, place = divmod(d, TOK)
        first, end = flat.first(d), flat.first(d) + flat.rows
        pieces = []
        if first < 1:
            pieces.append((early[SLOT - 1] + late[-1][:, SLOT - 1].reshape(-1))[None])
        if first < flat.bias_at:
            columns = [slots[s] for s in range(3) for slots in late]
            columns += [early[c * SLOT : (c + 1) * SLOT] for c in range(flat.chunks)]
            base = 1 + flat.per_row * flat.input_row(d)
            rows = jnp.concatenate(columns, axis=1).reshape(-1, width)
            pieces.append(rows[max(first, 1) - base : min(end, flat.bias_at) - base])
        if first < flat.attn_at and end > flat.bias_at:
            at = 4 * SLOT
            pieces += [early[at + 16 * c][None] for c in range(flat.chunks)]
            for s in range(2):
                row = [slots[s, GAINS_ROW] for slots in late]
                pieces.append(jnp.concatenate(row)[None])
        if z == 2:
            for part, holder, at, count in flat.attn_pieces(place):
                source = late
                if holder != place:
                    pairs = flat.attn_rounds()
                    source = next(c for c, p in zip(passed, pairs) if (holder, place) in p)
                rows = source[part][:, at : at + count]
                pieces.append(jnp.concatenate([rows[s] for s in range(3)], axis=1))
        if end > flat.down_at:
            low = max(first, flat.down_at)
            start = flat.down_at + flat.down_start(d)
            pieces.append(early[low - start : end - start])
        rows = jnp.concatenate(pieces)
        skip = flat.skip(d)
        return rows.reshape(-1)[skip : skip + flat.total * width // flat.devices]

    branches = [partial(assemble, d) for d in range(flat.devices)]
    return lax.switch(device, branches, early, late, passed)


def sequence_device(
    layer_input,
    norm_gain,
    weight_in,
    bias_in,
    query_gain,
    key_gain,
    weight_attn,
    weight_down,
    bias_down,
    image_ids,
    cotangent,
):
    seqs, slots, width = layer_input.shape
    tok, z = lax.axis_index("tok"), lax.axis_index("seq")
    flat = Flat(width, weight_down.shape[0], lax.axis_size("seq") * TOK)
    features = jnp.array(flat.features(), jnp.int32)[:, None]

    def homeward(rows):
        return Moving(regroup(rows.reshape(seqs, slots, -1)))

    gain = norm_gain[None]
    gains = (query_gain[None], key_gain[None])
    marks = jnp.pad(image_ids.astype(BF16)[:, None], ((0, 0), (0, 15), (0, width - slots)))
    rows = layer_input.reshape(seqs * slots, width)
    grads = cotangent.reshape(seqs * slots, width)
    moving = Moving(regroup(jnp.concatenate([layer_input, cotangent, marks], axis=1)))
    part_out, dn, payload = beside(
        partial(mlp, flat),
        (rows, grads, gain, weight_in, bias_in[None], weight_down, features),
        [moving],
    )
    came = moving.result
    early = Moving(share_mlp(payload))
    plane_sums = early.send([operand for operand, _ in early.wanted])
    query, key, value, grad_att, raw, perm, ids = heads(
        came, gain, weight_in, weight_attn, *gains, features
    )
    dn_heads = jnp.zeros((8, 128), F32)
    core = (tok % 2).astype(jnp.int32)[None]
    att = jnp.zeros((8, 128), BF16)

    def run(part, dn_heads, att, chains):
        return beside(
            partial(attend_part, flat, part),
            (core, query, key, value, grad_att, ids, gains, raw, perm, weight_in, dn_heads, came, att),
            chains,
        )

    dn_heads, att, *grads_0 = run(0, dn_heads, att, [])
    home, core_0 = homeward(att), Moving(share_heads_core(*grads_0))
    dn_heads, att, *grads_1 = run(1, dn_heads, att, [home, core_0])
    first = home.result.reshape(seqs * slots, -1)
    plane_0, core_1 = Moving(share_heads_plane(core_0.result)), Moving(share_heads_core(*grads_1))
    last, *grads_2 = run(2, dn_heads, att, [plane_0, core_1])
    last, grads_2, plane_sums = tie(last, grads_2, plane_sums)
    core_2 = Moving(share_heads_core(*grads_2))
    core_came = core_2.send([operand for operand, _ in core_2.wanted])
    early.take(plane_sums)
    ((operand, way),) = early.wanted
    core_came, operand = tie(core_came, operand)
    core_2.take(core_came)
    early.wanted = [(operand, way)]
    early.take(early.send([operand]))
    shape = (SEQS_IN, 3, SLOT, -1)
    both = jnp.concatenate([core_1.result, core_2.result], axis=1)
    both = Moving(share_heads_plane(both))
    before = Moving(share_heads_seq(plane_0.result.reshape(shape)))
    operands = [operand for operand, _ in before.wanted]
    chips, operands = tie(both.wanted[0][0], operands)
    both.take(both.send([chips]))
    moved = before.send(operands)
    both, moved, last = tie(both.result, moved, last)
    before.take(moved)
    home = homeward(last)
    planes = [plane.reshape(shape) for plane in jnp.split(both, 2)]
    late = Moving(share_heads_seq(jnp.stack(planes, axis=1))).finish()
    late = [before.result, late[0], late[1]]
    passed = share_attn(flat, late)
    last = home.finish().reshape(seqs * slots, -1)
    out, grad_input = close(
        rows, grads, gain, weight_attn, part_out, bias_down[None], dn, first, last
    )
    out, grad_input, late, passed = tie(out, grad_input, late, passed)
    grad_weights = own_slice(flat, z * TOK + tok, early.finish(), late, passed)
    shape = (seqs, slots, width)
    return (out.reshape(shape), grad_input.reshape(shape), grad_weights)


def per_device(layer_input, *rest):
    seqs, slots, _ = layer_input.shape
    if lax.axis_size("tok") == seqs == 8 and lax.axis_size("seq") == 4 and slots % 16 == 0:
        return sequence_device(layer_input, *rest)
    return units_device(layer_input, *rest)


def solution(mesh):
    placed = (
        P("seq", "tok", None),
        P(),
        P(),
        P(),
        P(),
        P(),
        P(),
        P(),
        P(),
        P("seq", "tok"),
        P("seq", "tok", None),
    )
    return jax.shard_map(
        per_device,
        mesh=mesh,
        in_specs=placed,
        out_specs=(P("seq", "tok", None), P("seq", "tok", None), P(("seq", "tok"))),
        check_vma=False,
    )
```

```python
from functools import partial

import jax
import jax.numpy as jnp
from jax import lax
from jax.experimental import pallas as pl
from jax.experimental.pallas import tpu as pltpu
from jax.sharding import PartitionSpec as P

HEADS = 12


EPS = 1e-06
NEG = -1e30

F32 = jnp.float32
BF16 = jnp.bfloat16
ROWS = 256
HEAD_DIM = 64
PAIR = 2 * HEAD_DIM
FAR = 192.0
VMEM_LIMIT = 60 * 1024 * 1024


def layer_norm(values, scaling):
    average = jnp.mean(values, axis=-1, keepdims=True)
    shifted = values - average
    spread = jnp.mean(shifted * shifted, axis=-1, keepdims=True)
    return shifted * lax.rsqrt(spread + EPS) * scaling


def head_norms(query_raw, key_raw, gain_query, gain_key):
    return (layer_norm(query_raw, gain_query), layer_norm(key_raw, gain_key))


def to_units(row_values, seq_count, head_count):
    part_len = row_values.shape[0] // seq_count
    shaped = row_values.reshape(seq_count, part_len, head_count, -1).transpose(0, 2, 3, 1)
    return shaped.reshape(seq_count * head_count, -1, part_len)


def from_units(unit_values, seq_count, head_count):
    part_len = unit_values.shape[2]
    shaped = unit_values.reshape(seq_count, head_count, -1, part_len).transpose(0, 3, 1, 2)
    return shaped.reshape(seq_count * part_len, -1)


def block_scores(query_block, key_unit, image_block, slot_ids, score_scale):
    scores = (
        lax.dot_general(
            query_block, key_unit, (((0,), (0,)), ((), ())), preferred_element_type=jnp.float32
        )
        * score_scale
    )
    allowed = image_block[:, None] == slot_ids[None, :]
    return (scores, allowed)


def split_blocks(unit_values, block_len):
    head_dim, length = unit_values.shape
    return unit_values.reshape(head_dim, length // block_len, block_len).transpose(1, 0, 2)


def attend_unit(packed, score_scale):
    query_unit, key_unit, value_unit, slot_ids = packed
    head_dim, length = query_unit.shape
    block_len = min(512, length)
    query_blocks = split_blocks(query_unit, block_len)
    image_blocks = slot_ids.reshape(length // block_len, block_len)

    def one_block(inputs):
        query_block, image_block = inputs
        scores, allowed = block_scores(query_block, key_unit, image_block, slot_ids, score_scale)
        scores = jnp.where(allowed, scores, NEG)
        row_max = jnp.max(scores, axis=-1, keepdims=True)
        shifted = jnp.exp(scores - row_max)
        row_total = jnp.sum(shifted, axis=-1, keepdims=True)
        weights = (shifted / row_total).astype(jnp.bfloat16)
        outputs = lax.dot_general(
            value_unit, weights, (((1,), (1,)), ((), ())), preferred_element_type=jnp.float32
        )
        return (outputs, row_max[:, 0] + jnp.log(row_total[:, 0]))

    outputs, log_total = lax.map(one_block, (query_blocks, image_blocks))
    return (outputs.transpose(1, 0, 2).reshape(head_dim, length), log_total.reshape(length))


def attend_back(packed, score_scale):
    query_unit, key_unit, value_unit, grad_unit, log_total, slot_ids = packed
    head_dim, length = query_unit.shape
    block_len = min(512, length)
    query_blocks = split_blocks(query_unit, block_len)
    grad_blocks = split_blocks(grad_unit, block_len)
    total_blocks = log_total.reshape(length // block_len, block_len)
    image_blocks = slot_ids.reshape(length // block_len, block_len)

    def one_block(carried, inputs):
        grad_key, grad_value = carried
        query_block, grad_block, total_block, image_block = inputs
        scores, allowed = block_scores(query_block, key_unit, image_block, slot_ids, score_scale)
        weights = jnp.where(allowed, jnp.exp(scores - total_block[:, None]), 0.0)
        weights_low = weights.astype(jnp.bfloat16)
        grad_weights = lax.dot_general(
            grad_block, value_unit, (((0,), (0,)), ((), ())), preferred_element_type=jnp.float32
        )
        inner = jnp.sum(weights * grad_weights, axis=-1, keepdims=True)
        grad_scores = (weights * (grad_weights - inner)).astype(jnp.bfloat16)
        grad_query = score_scale * lax.dot_general(
            key_unit, grad_scores, (((1,), (1,)), ((), ())), preferred_element_type=jnp.float32
        )
        grad_key = grad_key + score_scale * lax.dot_general(
            query_block, grad_scores, (((1,), (0,)), ((), ())), preferred_element_type=jnp.float32
        )
        grad_value = grad_value + lax.dot_general(
            grad_block, weights_low, (((1,), (0,)), ((), ())), preferred_element_type=jnp.float32
        )
        return ((grad_key, grad_value), grad_query)

    blank = jnp.zeros((head_dim, length), jnp.float32)
    (grad_key, grad_value), grad_query = lax.scan(
        one_block, (blank, blank), (query_blocks, grad_blocks, total_blocks, image_blocks)
    )
    return (grad_query.transpose(1, 0, 2).reshape(head_dim, length), grad_key, grad_value)


def reduce_grads(flat_grad):
    return lax.psum_scatter(flat_grad, ("seq", "tok"), scatter_dimension=0, tiled=True)


def units_device(
    layer_input,
    norm_gain,
    weight_in,
    bias_in,
    query_gain,
    key_gain,
    weight_attn,
    weight_down,
    bias_down,
    image_ids,
    cotangent,
):
    seq_count, part_len, model_width = layer_input.shape
    row_count = seq_count * part_len
    head_count = HEADS
    head_dim = model_width // head_count
    score_scale = head_dim ** (-0.5)
    whole_ids = lax.all_gather(image_ids, "tok", axis=1, tiled=True)
    unit_count = seq_count * head_count // lax.axis_size("tok")
    first_unit = lax.axis_index("tok") * unit_count
    unit_seq = (first_unit + jnp.arange(unit_count, dtype=jnp.int32)) // head_count
    unit_ids = jnp.take(whole_ids, unit_seq, axis=0)
    input_rows = layer_input.reshape(row_count, model_width).astype(jnp.float32)
    normalized_rows, input_back = jax.vjp(layer_norm, input_rows, norm_gain)
    normed_low = normalized_rows.astype(jnp.bfloat16)
    projected_rows = jnp.dot(normed_low, weight_in, preferred_element_type=jnp.float32)
    query_raw = projected_rows[:, :model_width].reshape(row_count, head_count, head_dim)
    key_raw = projected_rows[:, model_width : 2 * model_width].reshape(
        row_count, head_count, head_dim
    )
    value_low = projected_rows[:, 2 * model_width : 3 * model_width].astype(jnp.bfloat16)
    hidden_in = projected_rows[:, 3 * model_width :] + bias_in
    gain_query = query_gain.reshape(head_count, head_dim)
    gain_key = key_gain.reshape(head_count, head_dim)
    (query_normed, key_normed), heads_back = jax.vjp(
        head_norms, query_raw, key_raw, gain_query, gain_key
    )
    outgoing = (
        to_units(
            query_normed.reshape(row_count, model_width).astype(jnp.bfloat16), seq_count, head_count
        ),
        to_units(
            key_normed.reshape(row_count, model_width).astype(jnp.bfloat16), seq_count, head_count
        ),
        to_units(value_low, seq_count, head_count),
    )
    query_units, key_units, value_units = (
        lax.all_to_all(outgoing[0], "tok", split_axis=0, concat_axis=2, tiled=True),
        lax.all_to_all(outgoing[1], "tok", split_axis=0, concat_axis=2, tiled=True),
        lax.all_to_all(outgoing[2], "tok", split_axis=0, concat_axis=2, tiled=True),
    )
    attention_output, log_total = lax.map(
        partial(attend_unit, score_scale=score_scale),
        (query_units, key_units, value_units, unit_ids),
    )
    returned = lax.all_to_all(
        attention_output.astype(jnp.bfloat16), "tok", split_axis=2, concat_axis=0, tiled=True
    )
    attn_rows = from_units(returned, seq_count, head_count)
    activation, gelu_back = jax.vjp(partial(jax.nn.gelu, approximate=False), hidden_in)
    act_low = activation.astype(jnp.bfloat16)
    result_rows = input_rows + jnp.dot(attn_rows, weight_attn, preferred_element_type=jnp.float32)
    result_rows = (
        result_rows + jnp.dot(act_low, weight_down, preferred_element_type=jnp.float32) + bias_down
    )
    layer_output = result_rows.astype(jnp.bfloat16).reshape(seq_count, part_len, model_width)
    grad_rows = cotangent.reshape(row_count, model_width)
    grad_full = grad_rows.astype(jnp.float32)
    contract_rows = (((0,), (0,)), ((), ()))
    contract_cols = (((1,), (1,)), ((), ()))
    grad_bias_down = jnp.sum(grad_full, axis=0)
    grad_weight_down = lax.dot_general(
        act_low, grad_rows, contract_rows, preferred_element_type=jnp.float32
    )
    grad_weight_attn = lax.dot_general(
        attn_rows, grad_rows, contract_rows, preferred_element_type=jnp.float32
    )
    grad_activation = lax.dot_general(
        grad_rows, weight_down, contract_cols, preferred_element_type=jnp.float32
    )
    grad_hidden = gelu_back(grad_activation)[0]
    grad_bias_in = jnp.sum(grad_hidden, axis=0)
    grad_attended = lax.dot_general(
        grad_rows, weight_attn, contract_cols, preferred_element_type=jnp.float32
    )
    grad_units = lax.all_to_all(
        to_units(grad_attended.astype(jnp.bfloat16), seq_count, head_count),
        "tok",
        split_axis=0,
        concat_axis=2,
        tiled=True,
    )
    grad_query_u, grad_key_u, grad_value_u = lax.map(
        partial(attend_back, score_scale=score_scale),
        (query_units, key_units, value_units, grad_units, log_total, unit_ids),
    )
    back_query, back_key, back_value = (
        lax.all_to_all(
            grad_query_u.astype(jnp.bfloat16), "tok", split_axis=2, concat_axis=0, tiled=True
        ),
        lax.all_to_all(
            grad_key_u.astype(jnp.bfloat16), "tok", split_axis=2, concat_axis=0, tiled=True
        ),
        lax.all_to_all(
            grad_value_u.astype(jnp.bfloat16), "tok", split_axis=2, concat_axis=0, tiled=True
        ),
    )
    grad_query_n = (
        from_units(back_query, seq_count, head_count)
        .astype(jnp.float32)
        .reshape(row_count, head_count, head_dim)
    )
    grad_key_n = (
        from_units(back_key, seq_count, head_count)
        .astype(jnp.float32)
        .reshape(row_count, head_count, head_dim)
    )
    grad_value_rows = from_units(back_value, seq_count, head_count).astype(jnp.float32)
    grad_query_raw, grad_key_raw, grad_gain_query, grad_gain_key = heads_back(
        (grad_query_n, grad_key_n)
    )
    grad_projected = jnp.concatenate(
        [
            grad_query_raw.reshape(row_count, model_width),
            grad_key_raw.reshape(row_count, model_width),
            grad_value_rows,
            grad_hidden,
        ],
        axis=1,
    ).astype(jnp.bfloat16)
    grad_weight_in = lax.dot_general(
        normed_low, grad_projected, contract_rows, preferred_element_type=jnp.float32
    )
    grad_normed = lax.dot_general(
        grad_projected, weight_in, contract_cols, preferred_element_type=jnp.float32
    )
    grad_input_rows, grad_norm_gain = input_back(grad_normed)
    grad_input = (grad_full + grad_input_rows).reshape(seq_count, part_len, model_width)
    pieces = [
        grad_norm_gain,
        grad_weight_in,
        grad_bias_in,
        grad_gain_query,
        grad_gain_key,
        grad_weight_attn,
        grad_weight_down,
        grad_bias_down,
    ]
    flat_grad = jnp.concatenate([tensor.reshape(-1) for tensor in pieces])
    grad_weights = reduce_grads(flat_grad)
    return (layer_output, grad_input, grad_weights)


SLOT = 48
HELD = 304
PARTS = ((0, 256), (256, 256), (512, 256))
TOK = 8
SEQS_IN = 3
GAINS_ROW = 28
PLACE_ROWS = 4 * SLOT * 2 + 2 * HELD
ATTN_BLOCKS = (
    ((0, 48, 6, 0), (48, 48, 7, 0), (96, 48, 3, 0), (144, 48, 4, 0), (192, 48, 5, 0), (240, 16, 2, 32)),
    ((0, 48, 3, 0), (48, 48, 5, 0), (96, 48, 7, 0), (144, 48, 4, 0), (192, 48, 6, 0), (240, 16, 2, 32)),
    ((0, 48, 4, 0), (48, 48, 6, 0), (96, 48, 7, 0), (144, 48, 5, 0), (192, 48, 3, 0), (240, 16, 2, 32)),
)


class Flat:
    def __init__(self, width, hidden, devices):
        self.width = width
        self.chunks = hidden // width
        self.per_row = 3 + self.chunks
        self.bias_at = 1 + self.per_row * width
        self.gains_at = self.bias_at + self.chunks
        self.attn_at = self.gains_at + 2
        self.down_at = self.attn_at + width
        self.total = self.down_at + hidden + 1
        self.devices = devices
        self.rows = self.total // devices + 1

    def first(self, device):
        return device * self.total // self.devices

    def skip(self, device):
        return (device * self.total) % self.devices * self.width // self.devices

    def input_row(self, device):
        return max(0, (self.first(device) - 1) // self.per_row)

    def slots(self):
        pairs = [(place, z) for place in range(TOK) for z in range(3)]
        return [(place, z) for place, z in pairs if self.first(z * TOK + place) < self.bias_at]

    def features(self):
        return [self.input_row(z * TOK + place) + i for place, z in self.slots() for i in range(SLOT)]

    def bias_place(self):
        return next(d for d in range(self.devices) if self.first(d + 1) > self.bias_at) % TOK

    def down_start(self, device):
        start = self.first(device) - self.down_at
        return None if start + self.rows <= 0 else max(0, start) // 16 * 16

    def attn_pieces(self, place):
        low = self.first(2 * TOK + place) - self.attn_at
        high = low + self.rows
        found = []
        for part, (base, _) in enumerate(PARTS):
            for start, rows, holder, at in ATTN_BLOCKS[part]:
                begin, end = max(base + start, low), min(base + start + rows, high)
                if begin < end:
                    found.append((part, holder, at + begin - base - start, end - begin))
        return found

    def attn_rounds(self):
        pairs = {(h, p) for p in range(TOK) for _, h, _, _ in self.attn_pieces(p) if h != p}
        degree = lambda pair: sum((pair[0] == h) + (pair[1] == p) for h, p in pairs)
        rounds = []
        for holder, place in sorted(pairs, key=lambda pair: (-degree(pair), pair)):
            for taken in rounds:
                if all(holder != h and place != p for h, p in taken):
                    taken.append((holder, place))
                    break
            else:
                rounds.append([(holder, place)])
        return rounds


def side_of(place, core):
    return core if place % 2 == 0 else 1 - core


def selection(features_ref, width):
    columns = lax.broadcasted_iota(jnp.int32, (features_ref.shape[0], width), 1)
    return jnp.where(columns == features_ref[...], 1.0, 0.0).astype(BF16)


def dot(left, right):
    return jnp.dot(left, right, preferred_element_type=F32)


def dot_nt(left, right):
    return lax.dot_general(left, right, (((1,), (1,)), ((), ())), preferred_element_type=F32)


def dot_tn(left, right):
    return lax.dot_general(left, right, (((0,), (0,)), ((), ())), preferred_element_type=F32)


def standardize(rows):
    shifted = rows - jnp.mean(rows, axis=-1, keepdims=True)
    scale = lax.rsqrt(jnp.mean(shifted * shifted, axis=-1, keepdims=True) + EPS)
    return shifted * scale, scale


def head_means(values):
    width = min(4 * HEAD_DIM, values.shape[1])
    row = lax.broadcasted_iota(jnp.int32, (width, width), 0)
    column = lax.broadcasted_iota(jnp.int32, (width, width), 1)
    ones = jnp.where((row >> 6) == (column >> 6), 1.0, 0.0).astype(BF16)
    values = values.astype(BF16)
    parts = [
        dot(values[:, start : start + width], ones) for start in range(0, values.shape[1], width)
    ]
    return jnp.concatenate(parts, axis=1) * (1.0 / HEAD_DIM)


def head_standardize(raw):
    shifted = raw - head_means(raw)
    scale = lax.rsqrt(head_means(shifted * shifted) + EPS)
    return shifted * scale, scale


def gelu_pair(pre):
    phi = 0.5 + 0.5 * lax.erf(pre * (0.5**0.5))
    density = jnp.exp(-0.5 * pre * pre) * 0.3989422804014327
    return pre * phi, phi + pre * density


def with_row(values, row, vector):
    index = lax.broadcasted_iota(jnp.int32, values.shape, 0)
    return jnp.where(index == row, vector, values)


def mlp_kernel(
    flat, x_ref, g_ref, gain_ref, wh_ref, bias_ref, wd_ref, features_ref,
    out_ref, dn_ref, payload_ref,
    norm_ref, perm_ref, act_ref, dh_ref, gbd_ref, buffer_ref, sems,
):
    step = pl.program_id(0)
    last = flat.chunks - 1
    width = flat.width
    count = x_ref.shape[0] // ROWS

    @pl.when(step == 0)
    def _():
        gbd_ref[...] = jnp.zeros_like(gbd_ref)
        buffer_ref[:, 8 * SLOT + HELD :] = jnp.zeros((TOK, HELD, width), BF16)

        def block(i, carry):
            rows = pl.ds(pl.multiple_of(i * ROWS, ROWS), ROWS)
            hat, _ = standardize(x_ref[rows].astype(F32))
            norm_ref[rows] = (hat * gain_ref[...][None]).astype(BF16)
            out_ref[rows] = jnp.zeros_like(out_ref[rows])
            dn_ref[rows] = jnp.zeros_like(dn_ref[rows])
            gbd_ref[...] += jnp.sum(g_ref[rows].astype(F32), axis=0, keepdims=True)
            return carry

        lax.fori_loop(0, count, block, 0)
        perm_ref[...] = dot_nt(selection(features_ref, width), norm_ref[...]).astype(BF16)

    def products(i):
        rows = slice(i * ROWS, (i + 1) * ROWS)
        pre = dot(norm_ref[rows], wh_ref[...]) + bias_ref[...]
        return pre, dot_nt(g_ref[rows], wd_ref[...])

    grad_bias = jnp.zeros((1, width), F32)
    ahead = products(0)
    for i in range(count):
        rows = slice(i * ROWS, (i + 1) * ROWS)
        pre, dh = ahead
        if i + 1 < count:
            ahead = products(i + 1)
        act, slope = gelu_pair(pre)
        act_low = act.astype(BF16)
        dh = dh * slope
        dh_low = dh.astype(BF16)
        act_ref[rows] = act_low
        dh_ref[rows] = dh_low
        out_ref[rows] += dot(act_low, wd_ref[...])
        dn_ref[rows] += dot_nt(dh_low, wh_ref[...])
        grad_bias += jnp.sum(dh, axis=0, keepdims=True)

    def store(index, row, rows, place=None):
        places = slice(None) if place is None else place
        return pltpu.make_async_copy(
            buffer_ref.at[places, pl.ds(row, rows)], payload_ref.at[places, pl.ds(row, rows)], sems.at[index]
        )

    mixed = 8 * SLOT + HELD
    inputs = lambda chunk: [store(2 * chunk + z, (4 * z + chunk) * SLOT, SLOT) for z in range(2)]
    done = [[] for _ in range(flat.chunks)]
    for place in range(TOK):
        start = flat.down_start(3 * TOK + place)
        chunk = min((start + HELD - 1) // width, last)
        done[chunk].append((2 * flat.chunks + place, 8 * SLOT, HELD, place))
        start = flat.down_start(2 * TOK + place)
        chunk = last if start is None else min((start + HELD - 1) // width, last)
        done[chunk].append((2 * flat.chunks + TOK + place, mixed, HELD, place))

    grad_down = dot_tn(act_ref[...], g_ref[...])
    grad_in = dot(perm_ref[...], dh_ref[...])
    shift = pl.multiple_of(step * SLOT, SLOT)
    for index, (place, z) in enumerate(flat.slots()):
        part = grad_in[index * SLOT : (index + 1) * SLOT]
        at = z * 4 * SLOT if z < 2 else mixed
        buffer_ref[place, pl.ds(at + shift, SLOT)] = part.astype(BF16)

    for chunk in range(flat.chunks):

        @pl.when(step == chunk)
        def _():
            low = chunk * width
            for device in range(2 * TOK, 4 * TOK):
                start = flat.down_start(device)
                if start is None:
                    continue
                place, at = device % TOK, 8 * SLOT if device >= 3 * TOK else mixed
                begin, end = max(start, low), min(start + HELD, low + width)
                if begin < end:
                    part = grad_down[begin - low : end - low].astype(BF16)
                    buffer_ref[place, at + begin - start : at + end - start] = part
                if chunk == last and start + HELD > low + width:
                    tail = with_row(jnp.zeros((16, width), F32), 0, gbd_ref[...])
                    row = at + low + width - start
                    buffer_ref[place, row : row + 16] = tail.astype(BF16)
            tail = with_row(jnp.zeros((16, width), F32), 0, grad_bias).astype(BF16)
            at = mixed + 4 * SLOT + 16 * chunk
            buffer_ref[flat.bias_place(), at : at + 16] = tail
            if chunk == 0:
                inputs(0)[1].start()
            else:
                for copy in inputs(chunk):
                    copy.start()
            for args in done[chunk]:
                store(*args).start()

    @pl.when(step == last)
    def _():
        def block(i, total):
            rows = pl.ds(pl.multiple_of(i * ROWS, ROWS), ROWS)
            hat, _ = standardize(x_ref[rows].astype(F32))
            return total + jnp.sum(dn_ref[rows] * hat, axis=0, keepdims=True)

        total = lax.fori_loop(0, count, block, jnp.zeros((1, width), F32))
        kept = buffer_ref[0, SLOT - 16 : SLOT].astype(F32)
        buffer_ref[0, SLOT - 16 : SLOT] = with_row(kept, 15, total).astype(BF16)
        inputs(0)[0].start()
        for chunk in range(flat.chunks):
            for copy in inputs(chunk):
                copy.wait()
            for args in done[chunk]:
                store(*args).wait()


def mlp(flat, rows, grads, norm_gain, weight_in, bias_in, weight_down, features):
    count, width = rows.shape
    chunks = flat.chunks
    whole = lambda i: (0, 0)
    once = pl.Buffered(1)
    full = pl.BlockSpec((count, width), whole, pipeline_mode=once)
    payload = jax.ShapeDtypeStruct((TOK, PLACE_ROWS, width), BF16)
    return pl.pallas_call(
        partial(mlp_kernel, flat),
        grid=(chunks,),
        in_specs=[
            full,
            full,
            pl.BlockSpec((width,), lambda i: (0,)),
            pl.BlockSpec((width, width), lambda i: (0, i + 3)),
            pl.BlockSpec((1, width), lambda i: (0, i)),
            pl.BlockSpec((width, width), lambda i: (i, 0)),
            pl.BlockSpec(features.shape, whole, pipeline_mode=once),
        ],
        out_specs=[
            pl.BlockSpec((count, width), whole),
            pl.BlockSpec((count, width), whole),
            pl.BlockSpec(memory_space=pl.ANY),
        ],
        out_shape=[
            jax.ShapeDtypeStruct((count, width), F32),
            jax.ShapeDtypeStruct((count, width), F32),
            payload,
        ],
        scratch_shapes=[
            pltpu.VMEM((count, width), BF16),
            pltpu.VMEM((features.shape[0], count), BF16),
            pltpu.VMEM((count, width), BF16),
            pltpu.VMEM((count, width), BF16),
            pltpu.VMEM((1, width), F32),
            pltpu.VMEM(payload.shape, BF16),
            pltpu.SemaphoreType.DMA((2 * chunks + 2 * TOK,)),
        ],
        compiler_params=pltpu.CompilerParams(vmem_limit_bytes=VMEM_LIMIT),
        cost_estimate=pl.CostEstimate(
            flops=12 * count * width * width * chunks, bytes_accessed=32 * 2**20, transcendentals=0
        ),
        name="mlp",
    )(rows, grads, norm_gain, weight_in, bias_in, weight_down, features)


def heads_kernel(
    x_ref, g_ref, gain_ref, wqkv_ref, wattn_ref, qgain_ref, kgain_ref, features_ref, marks_ref,
    q_ref, k_ref, v_ref, do_ref, raw_ref, perm_ref, ids_ref,
    pick_ref,
):
    width = x_ref.shape[2]

    @pl.when(pl.program_id(0) == 0)
    def _():
        pick_ref[...] = selection(features_ref, width)

    slots = x_ref.shape[1]
    for group in range(x_ref.shape[0]):
        ids = marks_ref[group, :1, :slots].astype(F32)
        ids_ref[group * slots : (group + 1) * slots] = jnp.broadcast_to(ids, (PAIR, slots)).T
    hat, _ = standardize(x_ref[...].reshape(ROWS, width).astype(F32))
    normed = (hat * gain_ref[...][None]).astype(BF16)
    grads = g_ref[...].reshape(ROWS, width)
    perm_ref[...] = dot_nt(pick_ref[...], normed).astype(BF16)
    q_raw = dot(normed, wqkv_ref[:, :width])
    raw_ref[:, :width] = q_raw
    q_ref[...] = (head_standardize(q_raw)[0] * qgain_ref[...][None]).astype(BF16)
    k_raw = dot(normed, wqkv_ref[:, width : 2 * width])
    raw_ref[:, width:] = k_raw
    k_ref[...] = (head_standardize(k_raw)[0] * kgain_ref[...][None]).astype(BF16)
    v_ref[...] = dot(normed, wqkv_ref[:, 2 * width :]).astype(BF16)
    do_ref[...] = dot_nt(grads, wattn_ref[...]).astype(BF16)


def heads(came, norm_gain, weight_in, weight_attn, query_gain, key_gain, features):
    seqs, held, width = came.shape
    slots = held // 2 // 16 * 16
    count = seqs * slots
    whole = lambda i: (0, 0)
    block = pl.BlockSpec((ROWS, width), lambda i: (i, 0))
    vec = pl.BlockSpec((width,), lambda i: (0,))
    low = jax.ShapeDtypeStruct((count, width), BF16)
    group = (ROWS // slots, slots, width)
    return pl.pallas_call(
        heads_kernel,
        grid=(count // ROWS,),
        in_specs=[
            pl.BlockSpec(group, lambda i: (i, 0, 0)),
            pl.BlockSpec(group, lambda i: (i, 1, 0)),
            vec,
            pl.BlockSpec((width, 3 * width), whole),
            pl.BlockSpec((width, width), whole),
            vec,
            vec,
            pl.BlockSpec(features.shape, whole),
            pl.BlockSpec((ROWS // slots, 16, width), lambda i: (i, 2 * slots // 16, 0)),
        ],
        out_specs=[block] * 4
        + [
            pl.BlockSpec((ROWS, 2 * width), lambda i: (i, 0)),
            pl.BlockSpec((features.shape[0], ROWS), lambda i: (0, i)),
            pl.BlockSpec((ROWS, PAIR), lambda i: (i, 0)),
        ],
        out_shape=[low] * 4
        + [
            jax.ShapeDtypeStruct((count, 2 * width), F32),
            jax.ShapeDtypeStruct((features.shape[0], count), BF16),
            jax.ShapeDtypeStruct((count, PAIR), F32),
        ],
        scratch_shapes=[pltpu.VMEM((features.shape[0], width), BF16)],
        compiler_params=pltpu.CompilerParams(vmem_limit_bytes=VMEM_LIMIT),
        cost_estimate=pl.CostEstimate(
            flops=10 * count * width * width, bytes_accessed=26 * 2**20, transcendentals=0
        ),
        name="heads",
    )(came, came, norm_gain, weight_in, weight_attn, query_gain, key_gain, features, came)


def part_kernel(
    flat, part, core_ref, q_ref, k_ref, v_ref, do_ref, ids_ref, qgain_ref, kgain_ref,
    raw_hbm, perm_hbm, win_hbm, dn_hbm, came_hbm, att_hbm,
    *rest,
):
    step = pl.program_id(0)
    length = q_ref.shape[0]
    width = flat.width
    base, size = PARTS[part]
    final = part == len(PARTS) - 1
    if final:
        home_hbm, mine_hbm, theirs_hbm, *rest = rest
        *rest, att_ref, before_ref, dn_out_ref = rest
    elif part:
        dn_hbm_out, att_hbm_out, mine_hbm, theirs_hbm, *rest = rest
        *rest, att_ref, dn_out_ref = rest
    else:
        dn_hbm_out, mine_hbm, theirs_hbm, *rest = rest
        *rest, att_ref, dn_out_ref = rest
    ka_ref, va_ref, kat_ref, vat_ref, p_ref, plow_ref, pairs_ref, d_ref, *rest = rest
    raw_ref, perm_ref, g_ref, w_ref, dn_ref, x_ref, buffer_ref, sems = rest

    core = core_ref[0]
    slots = length // TOK
    extra = 0 if part else slots
    loads = {
        "raw": [
            pltpu.make_async_copy(
                raw_hbm.at[:, pl.ds(s * width + base, size)],
                raw_ref.at[:, pl.ds(s * size, size)],
                sems.at[s],
            )
            for s in range(2)
        ],
        "w": [
            pltpu.make_async_copy(
                win_hbm.at[:, pl.ds(s * width + base, size)],
                w_ref.at[:, pl.ds(s * size, size)],
                sems.at[2 + s],
            )
            for s in range(3)
        ],
        "perm": [pltpu.make_async_copy(perm_hbm, perm_ref, sems.at[5])],
        "g": [pltpu.make_async_copy(came_hbm.at[:, pl.ds(slots, slots)], g_ref, sems.at[6])],
    }
    if part:
        loads["dn"] = [pltpu.make_async_copy(dn_hbm, dn_ref, sems.at[7])]
    if final:
        loads["x"] = [pltpu.make_async_copy(came_hbm.at[:, pl.ds(0, slots)], x_ref, sems.at[8])]
        loads["att"] = [pltpu.make_async_copy(att_hbm, before_ref, sems.at[9])]

    @pl.when(step == 0)
    def _():
        for group in loads.values():
            for copy in group:
                copy.start()

    def arrived(name):
        for copy in loads[name]:
            copy.wait()

    def lanes(count, head):
        lane = lax.broadcasted_iota(jnp.int32, (count, PAIR), 1)
        return (lane >> 6) == head, lane - (1 - head) * HEAD_DIM

    ids = ids_ref[...].astype(jnp.int32) + 1

    def widen(head):
        mine, spare = lanes(length, head)
        marks = jnp.where(spare == ids, 1.0, jnp.where(spare == 17, -FAR, 0.0))
        ka = jnp.where(mine, k_ref[...].astype(F32), marks)
        ka_ref[head] = ka.astype(BF16)
        kat_ref[head] = ka.T.astype(BF16)
        marks = jnp.where((spare == 0) | (spare == 1), 1.0, 0.0)
        va = jnp.where(mine, v_ref[...].astype(F32), marks)
        va_ref[head] = va.astype(BF16)
        vat_ref[head] = va.T.astype(BF16)
        marks = jnp.where(spare == ids, FAR, jnp.where(spare == 17, 1.0, 0.0))
        return jnp.where(mine, q_ref[...].astype(F32) * (HEAD_DIM**-0.5), marks).astype(BF16)

    def score(head, qa):
        grown = jnp.exp(dot_nt(ka_ref[head], qa))
        p_ref[head] = grown
        low = grown.astype(BF16)
        plow_ref[head] = low
        return dot(vat_ref[head], low)

    def middle(head, sums):
        mine, spare = lanes(length, head)
        grad = do_ref[...].astype(F32)
        out = sums.T
        first = (1 - head) * HEAD_DIM
        inverse = 1.0 / out[:, first : first + 1]
        out = out * inverse
        inner = jnp.sum(jnp.where(mine, grad * out, 0.0), axis=-1, keepdims=True)
        offset = -inner * inverse
        high = offset.astype(BF16).astype(F32)
        marks = jnp.where(spare == 0, high, jnp.where(spare == 1, offset - high, 0.0))
        return out, jnp.where(mine, grad * inverse, marks).astype(BF16)

    def gradients(head, qa, grad_a):
        ds = (p_ref[head] * dot_nt(va_ref[head], grad_a)).astype(BF16)
        dv = dot(plow_ref[head], grad_a)
        dk = dot(ds, qa)
        dq = dot(kat_ref[head], ds).T * (HEAD_DIM**-0.5)
        return dq, dk, dv

    def finish():
        both = lambda index: jnp.concatenate([pairs_ref[index, pair] for pair in range(2)], axis=1)
        att_ref[...] = both(0)
        if extra:
            for place in range(TOK):
                own = att_ref[place * slots : (place + 1) * slots]
                buffer_ref[side_of(place, core), place // 2, :slots] = own
        for side in range(3):
            d_ref[:, side * size : (side + 1) * size] = both(1 + side)
        arrived("raw")
        arrived("w")
        if part:
            arrived("dn")
        if final:
            arrived("x")
            group = ROWS // x_ref.shape[1]

        def block(i, totals):
            rows = pl.ds(pl.multiple_of(i * ROWS, ROWS), ROWS)
            totals = list(totals)
            for side, gain_ref in enumerate((qgain_ref, kgain_ref)):
                lane = slice(side * size, (side + 1) * size)
                hat, scale = head_standardize(raw_ref[rows, lane])
                grad = d_ref[rows, lane].astype(F32)
                totals[side] += jnp.sum(grad * hat, axis=0, keepdims=True)
                grad = grad * gain_ref[...][None]
                grad = scale * (grad - head_means(grad) - hat * head_means(grad * hat))
                d_ref[rows, lane] = grad.astype(BF16)
            dn = dot_nt(d_ref[rows], w_ref[...])
            if part:
                dn = dn + dn_ref[rows]
            if final:
                x = x_ref[pl.ds(i * group, group)].reshape(ROWS, width).astype(F32)
                totals[2] += jnp.sum(dn * standardize(x)[0], axis=0, keepdims=True)
            dn_out_ref[rows] = dn.astype(dn_out_ref.dtype)
            return tuple(totals)

        zero = jnp.zeros((1, size), F32)
        totals = lax.fori_loop(0, length // ROWS, block, (zero, zero, jnp.zeros((1, width), F32)))

        if final:
            arrived("att")
            homeward = [
                pltpu.make_async_copy(before_ref, home_hbm.at[:, pl.ds(width + size, size)], sems.at[8]),
                pltpu.make_async_copy(dn_out_ref, home_hbm.at[:, pl.ds(0, width)], sems.at[12]),
                pltpu.make_async_copy(att_ref, home_hbm.at[:, pl.ds(width, size)], sems.at[13]),
            ]
        else:
            homeward = [pltpu.make_async_copy(dn_out_ref, dn_hbm_out, sems.at[12])]
            if part:
                homeward.append(pltpu.make_async_copy(att_ref, att_hbm_out, sems.at[13]))
        for copy in homeward:
            copy.start()
        arrived("perm")
        arrived("g")
        def put_slot(place, z, values):
            for s in range(3):
                row = extra + (3 * z + s) * SLOT
                part = values[:, s * size : (s + 1) * size].astype(BF16)
                buffer_ref[side_of(place, core), place // 2, row : row + values.shape[0]] = part

        grad_in = dot(perm_ref[...], d_ref[...])
        grad_attn = dot_tn(att_ref[...], g_ref[...].reshape(length, width))
        gains = jnp.concatenate([totals[0], totals[1], zero], axis=1)
        for index, (place, z) in enumerate(flat.slots()):
            values = grad_in[index * SLOT : (index + 1) * SLOT]
            if (place, z) == (flat.bias_place(), 2):
                start, rows, _, at = ATTN_BLOCKS[part][-1]
                values = jnp.concatenate([values[:at], grad_attn[start : start + rows]])
                values = with_row(values, GAINS_ROW, gains)
            if final and (place, z) == (0, 0):
                values = with_row(values, SLOT - 1, totals[2])
            put_slot(place, z, values)
        for start, rows, place, at in ATTN_BLOCKS[part]:
            if at == 0:
                put_slot(place, 2, grad_attn[start : start + rows])
        stores = [
            pltpu.make_async_copy(buffer_ref.at[side], ref, sems.at[10 + side])
            for side, ref in enumerate((mine_hbm, theirs_hbm))
        ]
        for copy in stores:
            copy.start()
        for copy in [*stores, *homeward]:
            copy.wait()

    qa = [widen(head) for head in range(2)]
    sums = score(0, qa[0])
    out, grad_a = middle(0, sums)
    first = (out, *gradients(0, qa[0], grad_a))
    sums = score(1, qa[1])
    out, grad_a = middle(1, sums)
    second = (out, *gradients(1, qa[1], grad_a))
    mine, _ = lanes(length, 0)
    for index in range(4):
        pairs_ref[index, step] = jnp.where(mine, first[index], second[index]).astype(BF16)

    @pl.when(step == pl.num_programs(0) - 1)
    def _():
        finish()


def attend_part(
    flat, part, core, query, key, value, grad_att, ids, gains, raw, perm, weight_in, dn, came, att
):
    length, width = query.shape
    base, size = PARTS[part]
    final = part == len(PARTS) - 1
    block = pl.BlockSpec((length, PAIR), lambda i: (0, base // PAIR + i))
    vec = pl.BlockSpec((size,), lambda i: (base // size,))
    anywhere = pl.BlockSpec(memory_space=pl.ANY)
    rows = SEQS_IN * 3 * SLOT + (0 if part else length // TOK)
    payload = jax.ShapeDtypeStruct((TOK // 2, rows, size), BF16)
    att_shape = jax.ShapeDtypeStruct((length, size), BF16)
    scratch = [pltpu.VMEM((length, size), BF16)]
    if final:
        results = [jax.ShapeDtypeStruct((length, width + 2 * size), BF16)]
        scratch += [pltpu.VMEM((length, size), BF16), pltpu.VMEM((length, width), BF16)]
    else:
        results = [jax.ShapeDtypeStruct((length, width), F32)] + [att_shape] * min(part, 1)
        scratch += [pltpu.VMEM((length, width), F32)]
    specs = [anywhere] * len(results)
    slots = length // came.shape[0]
    return pl.pallas_call(
        partial(part_kernel, flat, part),
        grid=(size // PAIR,),
        in_specs=[pl.BlockSpec(memory_space=pltpu.SMEM)]
        + [block] * 4
        + [pl.BlockSpec((length, PAIR), lambda i: (0, 0)), vec, vec]
        + [anywhere] * 6,
        out_specs=[*specs, anywhere, anywhere],
        out_shape=[*results, payload, payload],
        scratch_shapes=[
            pltpu.VMEM((2, length, PAIR), BF16),
            pltpu.VMEM((2, length, PAIR), BF16),
            pltpu.VMEM((2, PAIR, length), BF16),
            pltpu.VMEM((2, PAIR, length), BF16),
            pltpu.VMEM((2, length, length), F32),
            pltpu.VMEM((2, length, length), BF16),
            pltpu.VMEM((4, size // PAIR, length, PAIR), BF16),
            pltpu.VMEM((length, 3 * size), BF16),
            pltpu.VMEM((length, 2 * size), F32),
            pltpu.VMEM(perm.shape, BF16),
            pltpu.VMEM((came.shape[0], slots, width), BF16),
            pltpu.VMEM((width, 3 * size), BF16),
            pltpu.VMEM((length, width), F32),
            pltpu.VMEM((came.shape[0], slots, width), BF16),
            pltpu.VMEM((2, *payload.shape), BF16),
            pltpu.SemaphoreType.DMA((14,)),
            *scratch,
        ],
        compiler_params=pltpu.CompilerParams(vmem_limit_bytes=VMEM_LIMIT),
        cost_estimate=pl.CostEstimate(
            flops=48 * length * length * size, bytes_accessed=24 * 2**20, transcendentals=0
        ),
        name=f"attend{part}",
    )(core, query, key, value, grad_att, ids, *gains, raw, perm, weight_in, dn, came, att)


def close_kernel(
    x_ref, g_ref, gain_ref, wattn_ref, part_ref, bias_ref, dn_ref, att0_ref, home_ref,
    out_ref, gin_ref,
):
    width = x_ref.shape[1]
    size = att0_ref.shape[2]
    rows = x_ref[...].astype(F32)
    this, before = home_ref[:, width : width + size], home_ref[:, width + size :]
    attended = jnp.concatenate([att0_ref[0], before, this], axis=1)
    out = rows + dot(attended, wattn_ref[...]) + part_ref[...] + bias_ref[...][None]
    out_ref[...] = out.astype(BF16)
    hat, scale = standardize(rows)
    grad = (dn_ref[...] + home_ref[:, :width].astype(F32)) * gain_ref[...][None]
    mean = jnp.mean(grad, axis=-1, keepdims=True)
    along = jnp.mean(grad * hat, axis=-1, keepdims=True)
    gin_ref[...] = g_ref[...].astype(F32) + scale * (grad - mean - hat * along)


def close(rows, grads, norm_gain, weight_attn, partial_out, bias_down, dn, first, home):
    count, width = rows.shape
    whole = lambda i: (0, 0)
    block = pl.BlockSpec((ROWS, width), lambda i: (i, 0))
    columns = lambda values: pl.BlockSpec((ROWS, values.shape[1]), lambda i: (i, 0))
    vec = pl.BlockSpec((width,), lambda i: (0,))
    square = pl.BlockSpec((width, width), whole)
    return pl.pallas_call(
        close_kernel,
        grid=(count // ROWS,),
        in_specs=[block, block, vec, square, block, vec, block, pl.BlockSpec((1, ROWS, first.shape[2]), lambda i: (i, 0, 0)), columns(home)],
        out_specs=[block, block],
        out_shape=[
            jax.ShapeDtypeStruct((count, width), BF16),
            jax.ShapeDtypeStruct((count, width), F32),
        ],
        compiler_params=pltpu.CompilerParams(vmem_limit_bytes=VMEM_LIMIT),
        cost_estimate=pl.CostEstimate(
            flops=2 * count * width * width, bytes_accessed=18 * 2**20, transcendentals=0
        ),
        name="close",
    )(rows, grads, norm_gain, weight_attn, partial_out, bias_down, dn, first, home)


def total(*values):
    return sum(value.astype(F32) for value in values)


def low(*values):
    return total(*values).astype(BF16)


def pick(values, bit, axis=0):
    return lax.dynamic_index_in_dim(values, bit, axis, keepdims=False)


def across(shift):
    return ("tok", [(i, i ^ shift) for i in range(TOK)])


def share_mlp(payload):
    (place,) = yield [(payload, "sum")]
    (own,) = yield [(by_seq(place[0]), "sum seq")]
    return own


def by_seq_kernel(place_ref, out_ref):
    fill = jnp.zeros((HELD - 4 * SLOT, place_ref.shape[1]), BF16)
    for z in range(2):
        out_ref[z * HELD : z * HELD + 4 * SLOT] = place_ref[z * 4 * SLOT : (z + 1) * 4 * SLOT]
        out_ref[z * HELD + 4 * SLOT : (z + 1) * HELD] = fill
    out_ref[2 * HELD : 3 * HELD] = place_ref[8 * SLOT + HELD :]
    out_ref[3 * HELD :] = place_ref[8 * SLOT : 8 * SLOT + HELD]


def by_seq(place):
    return pl.pallas_call(
        by_seq_kernel,
        out_shape=jax.ShapeDtypeStruct((4 * HELD, place.shape[1]), BF16),
        name="by_seq",
    )(place)


def chip_kernel(slots, core_ref, *refs):
    *refs, out_ref = refs
    parts = len(refs) // 2
    rows = refs[0].shape[1] - slots
    if slots:
        core = core_ref[0]
        for ref, index in ((refs[0], core), (refs[1], 1 - core)):
            out_ref[:, pl.ds(pl.multiple_of(index * slots, slots), slots)] = ref[:, :slots]
    for part in range(parts):
        start = 2 * slots + part * rows
        mine_ref, came_ref = refs[part], refs[parts + part]
        out_ref[:, start : start + rows] = low(mine_ref[:, slots:], came_ref[:, slots:])


def by_chip(slots, core, mine, came):
    chips, rows, size = mine[0].shape
    block = lambda count: pl.BlockSpec((chips // 2, count, size), lambda i: (i, 0, 0))
    count = len(mine) * rows + slots
    return pl.pallas_call(
        partial(chip_kernel, slots),
        grid=(2,),
        in_specs=[pl.BlockSpec(memory_space=pltpu.SMEM)] + [block(rows)] * (2 * len(mine)),
        out_specs=block(count),
        out_shape=jax.ShapeDtypeStruct((chips, count, size), BF16),
        compiler_params=pltpu.CompilerParams(vmem_limit_bytes=VMEM_LIMIT),
        name="by_chip",
    )(core, *mine, *came)


def share_heads_core(theirs):
    (came,) = yield [(theirs, across(1))]
    return came


def share_heads_plane(chips, skip=0):
    (came,) = yield [(chips, "chips")]
    return came, low(jnp.sum(came[:, skip:].astype(F32), axis=0))


def share_heads_seq(plane):
    z = lax.axis_index("seq")
    size = lax.axis_size("seq")
    part_of = lambda index: pick(plane, jnp.minimum(index, SEQS_IN - 1))
    came = yield [
        (part_of((z + step) % size), ("seq", [(i, (i + step) % size) for i in range(size)]))
        for step in range(1, size)
    ]
    return total(part_of(z), *came)


def share_attn(flat, slots):
    packed = jnp.stack(slots).astype(BF16)
    came = [lax.ppermute(packed, "tok", pairs) for pairs in flat.attn_rounds()]
    return came


def regroup(rows):
    (came,) = yield [(rows, "home")]
    return came


def tie(*values):
    leaves, tree = jax.tree.flatten(values)
    return jax.tree.unflatten(tree, lax.optimization_barrier(leaves))


class Moving:
    def __init__(self, chain):
        self.chain = chain
        self.result = None
        self.wanted = next(chain)

    def send(self, operands):
        moved = []
        for operand, (_, way) in zip(operands, self.wanted):
            if way in ("sum", "sum seq"):
                axis = "tok" if way == "sum" else "seq"
                moved.append(lax.psum_scatter(operand, axis, scatter_dimension=0, tiled=True))
            elif way == "chips":
                cores = [[2 * chip + core for chip in range(TOK // 2)] for core in range(2)]
                moved.append(
                    lax.all_to_all(
                        operand, "tok", split_axis=0, concat_axis=0, tiled=True, axis_index_groups=cores
                    )
                )
            elif way == "home":
                moved.append(lax.all_to_all(operand, "tok", split_axis=0, concat_axis=0, tiled=True))
            else:
                moved.append(lax.ppermute(operand, *way))
        return moved

    def take(self, moved):
        try:
            self.wanted = self.chain.send(moved)
        except StopIteration as end:
            self.wanted, self.result = None, end.value

    def finish(self):
        while self.wanted is not None:
            self.take(self.send([operand for operand, _ in self.wanted]))
        return self.result


def beside(work, inputs, moving, loose=()):
    chains = [*moving, *loose]
    operands = [[operand for operand, _ in chain.wanted] for chain in chains]
    inputs, operands = tie(inputs, operands)
    moved = [chain.send(operand) for chain, operand in zip(chains, operands)]
    done = work(*inputs)
    done, moved[: len(moving)] = tie(done, moved[: len(moving)])
    for chain, values in zip(chains, moved):
        chain.take(values)
    return done


def own_slice(flat, device, early, late, passed):
    width = flat.width

    def assemble(d, early, late, passed):
        early = early.astype(F32)
        passed = [values.astype(F32) for values in passed]
        z, place = divmod(d, TOK)
        first, end = flat.first(d), flat.first(d) + flat.rows
        pieces = []
        if first < 1:
            pieces.append((early[SLOT - 1] + late[-1][:, SLOT - 1].reshape(-1))[None])
        if first < flat.bias_at:
            columns = [slots[s] for s in range(3) for slots in late]
            columns += [early[c * SLOT : (c + 1) * SLOT] for c in range(flat.chunks)]
            base = 1 + flat.per_row * flat.input_row(d)
            rows = jnp.concatenate(columns, axis=1).reshape(-1, width)
            pieces.append(rows[max(first, 1) - base : min(end, flat.bias_at) - base])
        if first < flat.attn_at and end > flat.bias_at:
            at = 4 * SLOT
            pieces += [early[at + 16 * c][None] for c in range(flat.chunks)]
            for s in range(2):
                row = [slots[s, GAINS_ROW] for slots in late]
                pieces.append(jnp.concatenate(row)[None])
        if z == 2:
            for part, holder, at, count in flat.attn_pieces(place):
                source = late
                if holder != place:
                    pairs = flat.attn_rounds()
                    source = next(c for c, p in zip(passed, pairs) if (holder, place) in p)
                rows = source[part][:, at : at + count]
                pieces.append(jnp.concatenate([rows[s] for s in range(3)], axis=1))
        if end > flat.down_at:
            low = max(first, flat.down_at)
            start = flat.down_at + flat.down_start(d)
            pieces.append(early[low - start : end - start])
        rows = jnp.concatenate(pieces)
        skip = flat.skip(d)
        return rows.reshape(-1)[skip : skip + flat.total * width // flat.devices]

    branches = [partial(assemble, d) for d in range(flat.devices)]
    return lax.switch(device, branches, early, late, passed)


def sequence_device(
    layer_input,
    norm_gain,
    weight_in,
    bias_in,
    query_gain,
    key_gain,
    weight_attn,
    weight_down,
    bias_down,
    image_ids,
    cotangent,
):
    seqs, slots, width = layer_input.shape
    tok, z = lax.axis_index("tok"), lax.axis_index("seq")
    flat = Flat(width, weight_down.shape[0], lax.axis_size("seq") * TOK)
    features = jnp.array(flat.features(), jnp.int32)[:, None]

    def homeward(rows):
        return Moving(regroup(rows.reshape(seqs, slots, -1)))

    gain = norm_gain
    gains = (query_gain, key_gain)
    marks = jnp.pad(image_ids.astype(BF16)[:, None], ((0, 0), (0, 15), (0, width - slots)))
    rows = layer_input.reshape(seqs * slots, width)
    grads = cotangent.reshape(seqs * slots, width)
    moving = Moving(regroup(jnp.concatenate([layer_input, cotangent, marks], axis=1)))
    part_out, dn, payload = beside(
        partial(mlp, flat),
        (rows, grads, gain, weight_in, bias_in[None], weight_down, features),
        [moving],
    )
    came = moving.result
    early = Moving(share_mlp(payload))
    plane_sums = early.send([operand for operand, _ in early.wanted])
    query, key, value, grad_att, raw, perm, ids = heads(
        came, gain, weight_in, weight_attn, *gains, features
    )
    dn_heads = jnp.zeros((8, 128), F32)
    core = (tok % 2).astype(jnp.int32)[None]
    att = jnp.zeros((8, 128), BF16)

    def run(part, dn_heads, att, chains, loose=()):
        return beside(
            partial(attend_part, flat, part),
            (core, query, key, value, grad_att, ids, gains, raw, perm, weight_in, dn_heads, came, att),
            chains,
            loose,
        )

    dn_heads, mine_0, theirs_0 = run(0, dn_heads, att, [])
    core_0 = Moving(share_heads_core(theirs_0))
    dn_heads, att, mine_1, theirs_1 = run(1, dn_heads, att, [core_0])
    chips = by_chip(slots, core, [mine_0], [core_0.result])
    plane_0, core_1 = Moving(share_heads_plane(chips, 2 * slots)), Moving(share_heads_core(theirs_1))
    last, mine_2, theirs_2 = run(2, dn_heads, att, [core_1], [plane_0])
    first, plane_0 = plane_0.result
    core_2 = Moving(share_heads_core(theirs_2)).finish()
    both = by_chip(0, core, [mine_1, mine_2], [core_1.result, core_2])
    plane_sums, _ = tie(plane_sums, both)
    early.take(plane_sums)
    early.take(early.send([operand for operand, _ in early.wanted]))
    both = Moving(share_heads_plane(both))
    both.take(both.send([operand for operand, _ in both.wanted]))
    shape = (SEQS_IN, 3, SLOT, -1)
    before = Moving(share_heads_seq(plane_0.reshape(shape)))
    moved = before.send([operand for operand, _ in before.wanted])
    both, moved, last = tie(both.result[1], moved, last)
    before.take(moved)
    home = homeward(last)
    planes = [plane.reshape(shape) for plane in jnp.split(both, 2)]
    late = Moving(share_heads_seq(jnp.stack(planes, axis=1))).finish()
    late = [before.result, late[0], late[1]]
    passed = share_attn(flat, late)
    last = home.finish().reshape(seqs * slots, -1)
    out, grad_input = close(
        rows, grads, gain, weight_attn, part_out, bias_down, dn, first, last
    )
    out, grad_input, late, passed = tie(out, grad_input, late, passed)
    grad_weights = own_slice(flat, z * TOK + tok, early.finish(), late, passed)
    shape = (seqs, slots, width)
    return (out.reshape(shape), grad_input.reshape(shape), grad_weights)


def per_device(layer_input, *rest):
    seqs, slots, _ = layer_input.shape
    if lax.axis_size("tok") == seqs == 8 and lax.axis_size("seq") == 4 and slots % 16 == 0:
        return sequence_device(layer_input, *rest)
    return units_device(layer_input, *rest)


def solution(mesh):
    placed = (
        P("seq", "tok", None),
        P(),
        P(),
        P(),
        P(),
        P(),
        P(),
        P(),
        P(),
        P("seq", "tok"),
        P("seq", "tok", None),
    )
    return jax.shard_map(
        per_device,
        mesh=mesh,
        in_specs=placed,
        out_specs=(P("seq", "tok", None), P("seq", "tok", None), P(("seq", "tok"))),
        check_vma=False,
    )
```

```python
from functools import partial

import jax
import jax.numpy as jnp
from jax import lax
from jax.experimental import pallas as pl
from jax.experimental.pallas import tpu as pltpu
from jax.sharding import PartitionSpec as P

HEADS = 12


EPS = 1e-06
NEG = -1e30

F32 = jnp.float32
BF16 = jnp.bfloat16
ROWS = 256
HEAD_DIM = 64
PAIR = 2 * HEAD_DIM
FAR = 192.0
VMEM_LIMIT = 60 * 1024 * 1024


def layer_norm(values, scaling):
    average = jnp.mean(values, axis=-1, keepdims=True)
    shifted = values - average
    spread = jnp.mean(shifted * shifted, axis=-1, keepdims=True)
    return shifted * lax.rsqrt(spread + EPS) * scaling


def head_norms(query_raw, key_raw, gain_query, gain_key):
    return (layer_norm(query_raw, gain_query), layer_norm(key_raw, gain_key))


def to_units(row_values, seq_count, head_count):
    part_len = row_values.shape[0] // seq_count
    shaped = row_values.reshape(seq_count, part_len, head_count, -1).transpose(0, 2, 3, 1)
    return shaped.reshape(seq_count * head_count, -1, part_len)


def from_units(unit_values, seq_count, head_count):
    part_len = unit_values.shape[2]
    shaped = unit_values.reshape(seq_count, head_count, -1, part_len).transpose(0, 3, 1, 2)
    return shaped.reshape(seq_count * part_len, -1)


def block_scores(query_block, key_unit, image_block, slot_ids, score_scale):
    scores = (
        lax.dot_general(
            query_block, key_unit, (((0,), (0,)), ((), ())), preferred_element_type=jnp.float32
        )
        * score_scale
    )
    allowed = image_block[:, None] == slot_ids[None, :]
    return (scores, allowed)


def split_blocks(unit_values, block_len):
    head_dim, length = unit_values.shape
    return unit_values.reshape(head_dim, length // block_len, block_len).transpose(1, 0, 2)


def attend_unit(packed, score_scale):
    query_unit, key_unit, value_unit, slot_ids = packed
    head_dim, length = query_unit.shape
    block_len = min(512, length)
    query_blocks = split_blocks(query_unit, block_len)
    image_blocks = slot_ids.reshape(length // block_len, block_len)

    def one_block(inputs):
        query_block, image_block = inputs
        scores, allowed = block_scores(query_block, key_unit, image_block, slot_ids, score_scale)
        scores = jnp.where(allowed, scores, NEG)
        row_max = jnp.max(scores, axis=-1, keepdims=True)
        shifted = jnp.exp(scores - row_max)
        row_total = jnp.sum(shifted, axis=-1, keepdims=True)
        weights = (shifted / row_total).astype(jnp.bfloat16)
        outputs = lax.dot_general(
            value_unit, weights, (((1,), (1,)), ((), ())), preferred_element_type=jnp.float32
        )
        return (outputs, row_max[:, 0] + jnp.log(row_total[:, 0]))

    outputs, log_total = lax.map(one_block, (query_blocks, image_blocks))
    return (outputs.transpose(1, 0, 2).reshape(head_dim, length), log_total.reshape(length))


def attend_back(packed, score_scale):
    query_unit, key_unit, value_unit, grad_unit, log_total, slot_ids = packed
    head_dim, length = query_unit.shape
    block_len = min(512, length)
    query_blocks = split_blocks(query_unit, block_len)
    grad_blocks = split_blocks(grad_unit, block_len)
    total_blocks = log_total.reshape(length // block_len, block_len)
    image_blocks = slot_ids.reshape(length // block_len, block_len)

    def one_block(carried, inputs):
        grad_key, grad_value = carried
        query_block, grad_block, total_block, image_block = inputs
        scores, allowed = block_scores(query_block, key_unit, image_block, slot_ids, score_scale)
        weights = jnp.where(allowed, jnp.exp(scores - total_block[:, None]), 0.0)
        weights_low = weights.astype(jnp.bfloat16)
        grad_weights = lax.dot_general(
            grad_block, value_unit, (((0,), (0,)), ((), ())), preferred_element_type=jnp.float32
        )
        inner = jnp.sum(weights * grad_weights, axis=-1, keepdims=True)
        grad_scores = (weights * (grad_weights - inner)).astype(jnp.bfloat16)
        grad_query = score_scale * lax.dot_general(
            key_unit, grad_scores, (((1,), (1,)), ((), ())), preferred_element_type=jnp.float32
        )
        grad_key = grad_key + score_scale * lax.dot_general(
            query_block, grad_scores, (((1,), (0,)), ((), ())), preferred_element_type=jnp.float32
        )
        grad_value = grad_value + lax.dot_general(
            grad_block, weights_low, (((1,), (0,)), ((), ())), preferred_element_type=jnp.float32
        )
        return ((grad_key, grad_value), grad_query)

    blank = jnp.zeros((head_dim, length), jnp.float32)
    (grad_key, grad_value), grad_query = lax.scan(
        one_block, (blank, blank), (query_blocks, grad_blocks, total_blocks, image_blocks)
    )
    return (grad_query.transpose(1, 0, 2).reshape(head_dim, length), grad_key, grad_value)


def reduce_grads(flat_grad):
    return lax.psum_scatter(flat_grad, ("seq", "tok"), scatter_dimension=0, tiled=True)


def units_device(
    layer_input,
    norm_gain,
    weight_in,
    bias_in,
    query_gain,
    key_gain,
    weight_attn,
    weight_down,
    bias_down,
    image_ids,
    cotangent,
):
    seq_count, part_len, model_width = layer_input.shape
    row_count = seq_count * part_len
    head_count = HEADS
    head_dim = model_width // head_count
    score_scale = head_dim ** (-0.5)
    whole_ids = lax.all_gather(image_ids, "tok", axis=1, tiled=True)
    unit_count = seq_count * head_count // lax.axis_size("tok")
    first_unit = lax.axis_index("tok") * unit_count
    unit_seq = (first_unit + jnp.arange(unit_count, dtype=jnp.int32)) // head_count
    unit_ids = jnp.take(whole_ids, unit_seq, axis=0)
    input_rows = layer_input.reshape(row_count, model_width).astype(jnp.float32)
    normalized_rows, input_back = jax.vjp(layer_norm, input_rows, norm_gain)
    normed_low = normalized_rows.astype(jnp.bfloat16)
    projected_rows = jnp.dot(normed_low, weight_in, preferred_element_type=jnp.float32)
    query_raw = projected_rows[:, :model_width].reshape(row_count, head_count, head_dim)
    key_raw = projected_rows[:, model_width : 2 * model_width].reshape(
        row_count, head_count, head_dim
    )
    value_low = projected_rows[:, 2 * model_width : 3 * model_width].astype(jnp.bfloat16)
    hidden_in = projected_rows[:, 3 * model_width :] + bias_in
    gain_query = query_gain.reshape(head_count, head_dim)
    gain_key = key_gain.reshape(head_count, head_dim)
    (query_normed, key_normed), heads_back = jax.vjp(
        head_norms, query_raw, key_raw, gain_query, gain_key
    )
    outgoing = (
        to_units(
            query_normed.reshape(row_count, model_width).astype(jnp.bfloat16), seq_count, head_count
        ),
        to_units(
            key_normed.reshape(row_count, model_width).astype(jnp.bfloat16), seq_count, head_count
        ),
        to_units(value_low, seq_count, head_count),
    )
    query_units, key_units, value_units = (
        lax.all_to_all(outgoing[0], "tok", split_axis=0, concat_axis=2, tiled=True),
        lax.all_to_all(outgoing[1], "tok", split_axis=0, concat_axis=2, tiled=True),
        lax.all_to_all(outgoing[2], "tok", split_axis=0, concat_axis=2, tiled=True),
    )
    attention_output, log_total = lax.map(
        partial(attend_unit, score_scale=score_scale),
        (query_units, key_units, value_units, unit_ids),
    )
    returned = lax.all_to_all(
        attention_output.astype(jnp.bfloat16), "tok", split_axis=2, concat_axis=0, tiled=True
    )
    attn_rows = from_units(returned, seq_count, head_count)
    activation, gelu_back = jax.vjp(partial(jax.nn.gelu, approximate=False), hidden_in)
    act_low = activation.astype(jnp.bfloat16)
    result_rows = input_rows + jnp.dot(attn_rows, weight_attn, preferred_element_type=jnp.float32)
    result_rows = (
        result_rows + jnp.dot(act_low, weight_down, preferred_element_type=jnp.float32) + bias_down
    )
    layer_output = result_rows.astype(jnp.bfloat16).reshape(seq_count, part_len, model_width)
    grad_rows = cotangent.reshape(row_count, model_width)
    grad_full = grad_rows.astype(jnp.float32)
    contract_rows = (((0,), (0,)), ((), ()))
    contract_cols = (((1,), (1,)), ((), ()))
    grad_bias_down = jnp.sum(grad_full, axis=0)
    grad_weight_down = lax.dot_general(
        act_low, grad_rows, contract_rows, preferred_element_type=jnp.float32
    )
    grad_weight_attn = lax.dot_general(
        attn_rows, grad_rows, contract_rows, preferred_element_type=jnp.float32
    )
    grad_activation = lax.dot_general(
        grad_rows, weight_down, contract_cols, preferred_element_type=jnp.float32
    )
    grad_hidden = gelu_back(grad_activation)[0]
    grad_bias_in = jnp.sum(grad_hidden, axis=0)
    grad_attended = lax.dot_general(
        grad_rows, weight_attn, contract_cols, preferred_element_type=jnp.float32
    )
    grad_units = lax.all_to_all(
        to_units(grad_attended.astype(jnp.bfloat16), seq_count, head_count),
        "tok",
        split_axis=0,
        concat_axis=2,
        tiled=True,
    )
    grad_query_u, grad_key_u, grad_value_u = lax.map(
        partial(attend_back, score_scale=score_scale),
        (query_units, key_units, value_units, grad_units, log_total, unit_ids),
    )
    back_query, back_key, back_value = (
        lax.all_to_all(
            grad_query_u.astype(jnp.bfloat16), "tok", split_axis=2, concat_axis=0, tiled=True
        ),
        lax.all_to_all(
            grad_key_u.astype(jnp.bfloat16), "tok", split_axis=2, concat_axis=0, tiled=True
        ),
        lax.all_to_all(
            grad_value_u.astype(jnp.bfloat16), "tok", split_axis=2, concat_axis=0, tiled=True
        ),
    )
    grad_query_n = (
        from_units(back_query, seq_count, head_count)
        .astype(jnp.float32)
        .reshape(row_count, head_count, head_dim)
    )
    grad_key_n = (
        from_units(back_key, seq_count, head_count)
        .astype(jnp.float32)
        .reshape(row_count, head_count, head_dim)
    )
    grad_value_rows = from_units(back_value, seq_count, head_count).astype(jnp.float32)
    grad_query_raw, grad_key_raw, grad_gain_query, grad_gain_key = heads_back(
        (grad_query_n, grad_key_n)
    )
    grad_projected = jnp.concatenate(
        [
            grad_query_raw.reshape(row_count, model_width),
            grad_key_raw.reshape(row_count, model_width),
            grad_value_rows,
            grad_hidden,
        ],
        axis=1,
    ).astype(jnp.bfloat16)
    grad_weight_in = lax.dot_general(
        normed_low, grad_projected, contract_rows, preferred_element_type=jnp.float32
    )
    grad_normed = lax.dot_general(
        grad_projected, weight_in, contract_cols, preferred_element_type=jnp.float32
    )
    grad_input_rows, grad_norm_gain = input_back(grad_normed)
    grad_input = (grad_full + grad_input_rows).reshape(seq_count, part_len, model_width)
    pieces = [
        grad_norm_gain,
        grad_weight_in,
        grad_bias_in,
        grad_gain_query,
        grad_gain_key,
        grad_weight_attn,
        grad_weight_down,
        grad_bias_down,
    ]
    flat_grad = jnp.concatenate([tensor.reshape(-1) for tensor in pieces])
    grad_weights = reduce_grads(flat_grad)
    return (layer_output, grad_input, grad_weights)


SLOT = 48
HELD = 304
PARTS = ((0, 256), (256, 256), (512, 256))
TOK = 8
SEQS_IN = 3
GAINS_ROW = 28
PLACE_ROWS = 4 * SLOT * 2 + 2 * HELD
ATTN_BLOCKS = (
    ((0, 48, 6, 0), (48, 48, 7, 0), (96, 48, 3, 0), (144, 48, 4, 0), (192, 48, 5, 0), (240, 16, 2, 32)),
    ((0, 48, 3, 0), (48, 48, 5, 0), (96, 48, 7, 0), (144, 48, 4, 0), (192, 48, 6, 0), (240, 16, 2, 32)),
    ((0, 48, 4, 0), (48, 48, 6, 0), (96, 48, 7, 0), (144, 48, 5, 0), (192, 48, 3, 0), (240, 16, 2, 32)),
)


class Flat:
    def __init__(self, width, hidden, devices):
        self.width = width
        self.chunks = hidden // width
        self.per_row = 3 + self.chunks
        self.bias_at = 1 + self.per_row * width
        self.gains_at = self.bias_at + self.chunks
        self.attn_at = self.gains_at + 2
        self.down_at = self.attn_at + width
        self.total = self.down_at + hidden + 1
        self.devices = devices
        self.rows = self.total // devices + 1

    def first(self, device):
        return device * self.total // self.devices

    def skip(self, device):
        return (device * self.total) % self.devices * self.width // self.devices

    def input_row(self, device):
        return max(0, (self.first(device) - 1) // self.per_row)

    def slots(self):
        pairs = [(place, z) for place in range(TOK) for z in range(3)]
        return [(place, z) for place, z in pairs if self.first(z * TOK + place) < self.bias_at]

    def features(self):
        return [self.input_row(z * TOK + place) + i for place, z in self.slots() for i in range(SLOT)]

    def bias_place(self):
        return next(d for d in range(self.devices) if self.first(d + 1) > self.bias_at) % TOK

    def down_start(self, device):
        start = self.first(device) - self.down_at
        return None if start + self.rows <= 0 else max(0, start) // 16 * 16

    def attn_pieces(self, place):
        low = self.first(2 * TOK + place) - self.attn_at
        high = low + self.rows
        found = []
        for part, (base, _) in enumerate(PARTS):
            for start, rows, holder, at in ATTN_BLOCKS[part]:
                begin, end = max(base + start, low), min(base + start + rows, high)
                if begin < end:
                    found.append((part, holder, at + begin - base - start, end - begin))
        return found

    def attn_rounds(self):
        pairs = {(h, p) for p in range(TOK) for _, h, _, _ in self.attn_pieces(p) if h != p}
        degree = lambda pair: sum((pair[0] == h) + (pair[1] == p) for h, p in pairs)
        rounds = []
        for holder, place in sorted(pairs, key=lambda pair: (-degree(pair), pair)):
            for taken in rounds:
                if all(holder != h and place != p for h, p in taken):
                    taken.append((holder, place))
                    break
            else:
                rounds.append([(holder, place)])
        return rounds


def side_of(place, core):
    return core if place % 2 == 0 else 1 - core


def selection(features_ref, width):
    columns = lax.broadcasted_iota(jnp.int32, (features_ref.shape[0], width), 1)
    return jnp.where(columns == features_ref[...], 1.0, 0.0).astype(BF16)


def dot(left, right):
    return jnp.dot(left, right, preferred_element_type=F32)


def dot_nt(left, right):
    return lax.dot_general(left, right, (((1,), (1,)), ((), ())), preferred_element_type=F32)


def dot_tn(left, right):
    return lax.dot_general(left, right, (((0,), (0,)), ((), ())), preferred_element_type=F32)


def standardize(rows):
    shifted = rows - jnp.mean(rows, axis=-1, keepdims=True)
    scale = lax.rsqrt(jnp.mean(shifted * shifted, axis=-1, keepdims=True) + EPS)
    return shifted * scale, scale


def head_means(values):
    width = min(4 * HEAD_DIM, values.shape[1])
    row = lax.broadcasted_iota(jnp.int32, (width, width), 0)
    column = lax.broadcasted_iota(jnp.int32, (width, width), 1)
    ones = jnp.where((row >> 6) == (column >> 6), 1.0, 0.0).astype(BF16)
    values = values.astype(BF16)
    parts = [
        dot(values[:, start : start + width], ones) for start in range(0, values.shape[1], width)
    ]
    return jnp.concatenate(parts, axis=1) * (1.0 / HEAD_DIM)


def head_standardize(raw):
    shifted = raw - head_means(raw)
    scale = lax.rsqrt(head_means(shifted * shifted) + EPS)
    return shifted * scale, scale


def gelu_pair(pre):
    phi = 0.5 + 0.5 * lax.erf(pre * (0.5**0.5))
    density = jnp.exp(-0.5 * pre * pre) * 0.3989422804014327
    return pre * phi, phi + pre * density


def with_row(values, row, vector):
    index = lax.broadcasted_iota(jnp.int32, values.shape, 0)
    return jnp.where(index == row, vector, values)


def mlp_kernel(
    flat, x_ref, g_ref, gain_ref, wh_ref, bias_ref, wd_ref, features_ref,
    out_ref, dn_ref, payload_ref,
    norm_ref, perm_ref, act_ref, dh_ref, gbd_ref, buffer_ref, sems,
):
    step = pl.program_id(0)
    last = flat.chunks - 1
    width = flat.width
    count = x_ref.shape[0] // ROWS

    @pl.when(step == 0)
    def _():
        gbd_ref[...] = jnp.zeros_like(gbd_ref)
        buffer_ref[:, 8 * SLOT + HELD :] = jnp.zeros((TOK, HELD, width), BF16)

        def block(i, carry):
            rows = pl.ds(pl.multiple_of(i * ROWS, ROWS), ROWS)
            hat, _ = standardize(x_ref[rows].astype(F32))
            norm_ref[rows] = (hat * gain_ref[...][None]).astype(BF16)
            out_ref[rows] = jnp.zeros_like(out_ref[rows])
            dn_ref[rows] = jnp.zeros_like(dn_ref[rows])
            gbd_ref[...] += jnp.sum(g_ref[rows].astype(F32), axis=0, keepdims=True)
            return carry

        lax.fori_loop(0, count, block, 0)
        perm_ref[...] = dot_nt(selection(features_ref, width), norm_ref[...]).astype(BF16)

    def products(i):
        rows = slice(i * ROWS, (i + 1) * ROWS)
        pre = dot(norm_ref[rows], wh_ref[...]) + bias_ref[...]
        return pre, dot_nt(g_ref[rows], wd_ref[...])

    grad_bias = jnp.zeros((1, width), F32)
    ahead = products(0)
    for i in range(count):
        rows = slice(i * ROWS, (i + 1) * ROWS)
        pre, dh = ahead
        if i + 1 < count:
            ahead = products(i + 1)
        act, slope = gelu_pair(pre)
        act_low = act.astype(BF16)
        dh = dh * slope
        dh_low = dh.astype(BF16)
        act_ref[rows] = act_low
        dh_ref[rows] = dh_low
        out_ref[rows] += dot(act_low, wd_ref[...])
        dn_ref[rows] += dot_nt(dh_low, wh_ref[...])
        grad_bias += jnp.sum(dh, axis=0, keepdims=True)

    def store(index, row, rows, place=None):
        places = slice(None) if place is None else place
        return pltpu.make_async_copy(
            buffer_ref.at[places, pl.ds(row, rows)], payload_ref.at[places, pl.ds(row, rows)], sems.at[index]
        )

    mixed = 8 * SLOT + HELD
    inputs = lambda chunk: [store(2 * chunk + z, (4 * z + chunk) * SLOT, SLOT) for z in range(2)]
    done = [[] for _ in range(flat.chunks)]
    for place in range(TOK):
        start = flat.down_start(3 * TOK + place)
        chunk = min((start + HELD - 1) // width, last)
        done[chunk].append((2 * flat.chunks + place, 8 * SLOT, HELD, place))
        start = flat.down_start(2 * TOK + place)
        chunk = last if start is None else min((start + HELD - 1) // width, last)
        done[chunk].append((2 * flat.chunks + TOK + place, mixed, HELD, place))

    grad_down = dot_tn(act_ref[...], g_ref[...])
    grad_in = dot(perm_ref[...], dh_ref[...])
    shift = pl.multiple_of(step * SLOT, SLOT)
    for index, (place, z) in enumerate(flat.slots()):
        part = grad_in[index * SLOT : (index + 1) * SLOT]
        at = z * 4 * SLOT if z < 2 else mixed
        buffer_ref[place, pl.ds(at + shift, SLOT)] = part.astype(BF16)

    for chunk in range(flat.chunks):

        @pl.when(step == chunk)
        def _():
            low = chunk * width
            for device in range(2 * TOK, 4 * TOK):
                start = flat.down_start(device)
                if start is None:
                    continue
                place, at = device % TOK, 8 * SLOT if device >= 3 * TOK else mixed
                begin, end = max(start, low), min(start + HELD, low + width)
                if begin < end:
                    part = grad_down[begin - low : end - low].astype(BF16)
                    buffer_ref[place, at + begin - start : at + end - start] = part
                if chunk == last and start + HELD > low + width:
                    tail = with_row(jnp.zeros((16, width), F32), 0, gbd_ref[...])
                    row = at + low + width - start
                    buffer_ref[place, row : row + 16] = tail.astype(BF16)
            tail = with_row(jnp.zeros((16, width), F32), 0, grad_bias).astype(BF16)
            at = mixed + 4 * SLOT + 16 * chunk
            buffer_ref[flat.bias_place(), at : at + 16] = tail
            if chunk == 0:
                inputs(0)[1].start()
            else:
                for copy in inputs(chunk):
                    copy.start()
            for args in done[chunk]:
                store(*args).start()

    @pl.when(step == last)
    def _():
        def block(i, total):
            rows = pl.ds(pl.multiple_of(i * ROWS, ROWS), ROWS)
            hat, _ = standardize(x_ref[rows].astype(F32))
            return total + jnp.sum(dn_ref[rows] * hat, axis=0, keepdims=True)

        total = lax.fori_loop(0, count, block, jnp.zeros((1, width), F32))
        kept = buffer_ref[0, SLOT - 16 : SLOT].astype(F32)
        buffer_ref[0, SLOT - 16 : SLOT] = with_row(kept, 15, total).astype(BF16)
        inputs(0)[0].start()
        for chunk in range(flat.chunks):
            for copy in inputs(chunk):
                copy.wait()
            for args in done[chunk]:
                store(*args).wait()


def mlp(flat, rows, grads, norm_gain, weight_in, bias_in, weight_down, features):
    count, width = rows.shape
    chunks = flat.chunks
    whole = lambda i: (0, 0)
    once = pl.Buffered(1)
    full = pl.BlockSpec((count, width), whole, pipeline_mode=once)
    payload = jax.ShapeDtypeStruct((TOK, PLACE_ROWS, width), BF16)
    return pl.pallas_call(
        partial(mlp_kernel, flat),
        grid=(chunks,),
        in_specs=[
            full,
            full,
            pl.BlockSpec((width,), lambda i: (0,)),
            pl.BlockSpec((width, width), lambda i: (0, i + 3)),
            pl.BlockSpec((1, width), lambda i: (0, i)),
            pl.BlockSpec((width, width), lambda i: (i, 0)),
            pl.BlockSpec(features.shape, whole, pipeline_mode=once),
        ],
        out_specs=[
            pl.BlockSpec((count, width), whole),
            pl.BlockSpec((count, width), whole),
            pl.BlockSpec(memory_space=pl.ANY),
        ],
        out_shape=[
            jax.ShapeDtypeStruct((count, width), F32),
            jax.ShapeDtypeStruct((count, width), F32),
            payload,
        ],
        scratch_shapes=[
            pltpu.VMEM((count, width), BF16),
            pltpu.VMEM((features.shape[0], count), BF16),
            pltpu.VMEM((count, width), BF16),
            pltpu.VMEM((count, width), BF16),
            pltpu.VMEM((1, width), F32),
            pltpu.VMEM(payload.shape, BF16),
            pltpu.SemaphoreType.DMA((2 * chunks + 2 * TOK,)),
        ],
        compiler_params=pltpu.CompilerParams(vmem_limit_bytes=VMEM_LIMIT),
        cost_estimate=pl.CostEstimate(
            flops=12 * count * width * width * chunks, bytes_accessed=32 * 2**20, transcendentals=0
        ),
        name="mlp",
    )(rows, grads, norm_gain, weight_in, bias_in, weight_down, features)


def heads_kernel(
    x_ref, g_ref, gain_ref, wqkv_ref, wattn_ref, qgain_ref, kgain_ref, features_ref, marks_ref,
    q_ref, k_ref, v_ref, do_ref, raw_ref, perm_ref, ids_ref,
    pick_ref,
):
    width = x_ref.shape[2]

    @pl.when(pl.program_id(0) == 0)
    def _():
        pick_ref[...] = selection(features_ref, width)

    slots = x_ref.shape[1]
    for group in range(x_ref.shape[0]):
        ids = marks_ref[group, :1, :slots].astype(F32)
        ids_ref[group * slots : (group + 1) * slots] = jnp.broadcast_to(ids, (PAIR, slots)).T
    hat, _ = standardize(x_ref[...].reshape(ROWS, width).astype(F32))
    normed = (hat * gain_ref[...][None]).astype(BF16)
    grads = g_ref[...].reshape(ROWS, width)
    perm_ref[...] = dot_nt(pick_ref[...], normed).astype(BF16)
    q_raw = dot(normed, wqkv_ref[:, :width])
    raw_ref[:, :width] = q_raw
    q_ref[...] = (head_standardize(q_raw)[0] * qgain_ref[...][None]).astype(BF16)
    k_raw = dot(normed, wqkv_ref[:, width : 2 * width])
    raw_ref[:, width:] = k_raw
    k_ref[...] = (head_standardize(k_raw)[0] * kgain_ref[...][None]).astype(BF16)
    v_ref[...] = dot(normed, wqkv_ref[:, 2 * width :]).astype(BF16)
    do_ref[...] = dot_nt(grads, wattn_ref[...]).astype(BF16)


def heads(came, norm_gain, weight_in, weight_attn, query_gain, key_gain, features):
    seqs, held, width = came.shape
    slots = held // 2 // 16 * 16
    count = seqs * slots
    whole = lambda i: (0, 0)
    block = pl.BlockSpec((ROWS, width), lambda i: (i, 0))
    vec = pl.BlockSpec((width,), lambda i: (0,))
    low = jax.ShapeDtypeStruct((count, width), BF16)
    group = (ROWS // slots, slots, width)
    return pl.pallas_call(
        heads_kernel,
        grid=(count // ROWS,),
        in_specs=[
            pl.BlockSpec(group, lambda i: (i, 0, 0)),
            pl.BlockSpec(group, lambda i: (i, 1, 0)),
            vec,
            pl.BlockSpec((width, 3 * width), whole),
            pl.BlockSpec((width, width), whole),
            vec,
            vec,
            pl.BlockSpec(features.shape, whole),
            pl.BlockSpec((ROWS // slots, 16, width), lambda i: (i, 2 * slots // 16, 0)),
        ],
        out_specs=[block] * 4
        + [
            pl.BlockSpec((ROWS, 2 * width), lambda i: (i, 0)),
            pl.BlockSpec((features.shape[0], ROWS), lambda i: (0, i)),
            pl.BlockSpec((ROWS, PAIR), lambda i: (i, 0)),
        ],
        out_shape=[low] * 4
        + [
            jax.ShapeDtypeStruct((count, 2 * width), F32),
            jax.ShapeDtypeStruct((features.shape[0], count), BF16),
            jax.ShapeDtypeStruct((count, PAIR), F32),
        ],
        scratch_shapes=[pltpu.VMEM((features.shape[0], width), BF16)],
        compiler_params=pltpu.CompilerParams(vmem_limit_bytes=VMEM_LIMIT),
        cost_estimate=pl.CostEstimate(
            flops=10 * count * width * width, bytes_accessed=26 * 2**20, transcendentals=0
        ),
        name="heads",
    )(came, came, norm_gain, weight_in, weight_attn, query_gain, key_gain, features, came)


def part_kernel(
    flat, part, core_ref, q_ref, k_ref, v_ref, do_ref, ids_ref, qgain_ref, kgain_ref,
    raw_hbm, perm_hbm, win_hbm, dn_hbm, came_hbm, att_hbm,
    *rest,
):
    step = pl.program_id(0)
    length = q_ref.shape[0]
    width = flat.width
    base, size = PARTS[part]
    final = part == len(PARTS) - 1
    if final:
        home_hbm, mine_hbm, theirs_hbm, *rest = rest
        *rest, att_ref, before_ref, dn_out_ref = rest
    elif part:
        dn_hbm_out, att_hbm_out, mine_hbm, theirs_hbm, *rest = rest
        *rest, att_ref, dn_out_ref = rest
    else:
        dn_hbm_out, mine_hbm, theirs_hbm, *rest = rest
        *rest, att_ref, dn_out_ref = rest
    ka_ref, va_ref, kat_ref, vat_ref, p_ref, plow_ref, pairs_ref, d_ref, *rest = rest
    raw_ref, perm_ref, g_ref, w_ref, dn_ref, x_ref, buffer_ref, sems = rest

    core = core_ref[0]
    slots = length // TOK
    extra = 0 if part else slots
    loads = {
        "raw": [
            pltpu.make_async_copy(
                raw_hbm.at[:, pl.ds(s * width + base, size)],
                raw_ref.at[:, pl.ds(s * size, size)],
                sems.at[s],
            )
            for s in range(2)
        ],
        "w": [
            pltpu.make_async_copy(
                win_hbm.at[:, pl.ds(s * width + base, size)],
                w_ref.at[:, pl.ds(s * size, size)],
                sems.at[2 + s],
            )
            for s in range(3)
        ],
        "perm": [pltpu.make_async_copy(perm_hbm, perm_ref, sems.at[5])],
        "g": [pltpu.make_async_copy(came_hbm.at[:, pl.ds(slots, slots)], g_ref, sems.at[6])],
    }
    if part:
        loads["dn"] = [pltpu.make_async_copy(dn_hbm, dn_ref, sems.at[7])]
    if final:
        loads["x"] = [pltpu.make_async_copy(came_hbm.at[:, pl.ds(0, slots)], x_ref, sems.at[8])]
        loads["att"] = [pltpu.make_async_copy(att_hbm, before_ref, sems.at[9])]

    @pl.when(step == 0)
    def _():
        for group in loads.values():
            for copy in group:
                copy.start()

    def arrived(name):
        for copy in loads[name]:
            copy.wait()

    def lanes(count, head):
        lane = lax.broadcasted_iota(jnp.int32, (count, PAIR), 1)
        return (lane >> 6) == head, lane - (1 - head) * HEAD_DIM

    ids = ids_ref[...].astype(jnp.int32) + 1

    def widen(head):
        mine, spare = lanes(length, head)
        marks = jnp.where(spare == ids, 1.0, jnp.where(spare == 17, -FAR, 0.0))
        ka = jnp.where(mine, k_ref[...].astype(F32), marks)
        ka_ref[head] = ka.astype(BF16)
        kat_ref[head] = ka.T.astype(BF16)
        marks = jnp.where((spare == 0) | (spare == 1), 1.0, 0.0)
        va = jnp.where(mine, v_ref[...].astype(F32), marks)
        va_ref[head] = va.astype(BF16)
        vat_ref[head] = va.T.astype(BF16)
        marks = jnp.where(spare == ids, FAR, jnp.where(spare == 17, 1.0, 0.0))
        return jnp.where(mine, q_ref[...].astype(F32) * (HEAD_DIM**-0.5), marks).astype(BF16)

    def score(head, qa):
        grown = jnp.exp(dot_nt(ka_ref[head], qa))
        p_ref[head] = grown
        low = grown.astype(BF16)
        plow_ref[head] = low
        return dot(vat_ref[head], low)

    def middle(head, sums):
        mine, spare = lanes(length, head)
        grad = do_ref[...].astype(F32)
        out = sums.T
        first = (1 - head) * HEAD_DIM
        inverse = 1.0 / out[:, first : first + 1]
        out = out * inverse
        inner = jnp.sum(jnp.where(mine, grad * out, 0.0), axis=-1, keepdims=True)
        offset = -inner * inverse
        high = offset.astype(BF16).astype(F32)
        marks = jnp.where(spare == 0, high, jnp.where(spare == 1, offset - high, 0.0))
        return out, jnp.where(mine, grad * inverse, marks).astype(BF16)

    def gradients(head, qa, grad_a):
        ds = (p_ref[head] * dot_nt(va_ref[head], grad_a)).astype(BF16)
        dv = dot(plow_ref[head], grad_a)
        dk = dot(ds, qa)
        dq = dot(kat_ref[head], ds).T * (HEAD_DIM**-0.5)
        return dq, dk, dv

    def finish():
        both = lambda index: jnp.concatenate([pairs_ref[index, pair] for pair in range(2)], axis=1)
        att_ref[...] = both(0)
        if extra:
            for place in range(TOK):
                own = att_ref[place * slots : (place + 1) * slots]
                buffer_ref[side_of(place, core), place // 2, :slots] = own
        for side in range(3):
            d_ref[:, side * size : (side + 1) * size] = both(1 + side)
        arrived("raw")
        arrived("w")
        if part:
            arrived("dn")
        if final:
            arrived("x")
            group = ROWS // x_ref.shape[1]

        def block(i, totals):
            rows = pl.ds(pl.multiple_of(i * ROWS, ROWS), ROWS)
            totals = list(totals)
            for side, gain_ref in enumerate((qgain_ref, kgain_ref)):
                lane = slice(side * size, (side + 1) * size)
                hat, scale = head_standardize(raw_ref[rows, lane])
                grad = d_ref[rows, lane].astype(F32)
                totals[side] += jnp.sum(grad * hat, axis=0, keepdims=True)
                grad = grad * gain_ref[...][None]
                grad = scale * (grad - head_means(grad) - hat * head_means(grad * hat))
                d_ref[rows, lane] = grad.astype(BF16)
            dn = dot_nt(d_ref[rows], w_ref[...])
            if part:
                dn = dn + dn_ref[rows]
            if final:
                x = x_ref[pl.ds(i * group, group)].reshape(ROWS, width).astype(F32)
                totals[2] += jnp.sum(dn * standardize(x)[0], axis=0, keepdims=True)
            dn_out_ref[rows] = dn.astype(dn_out_ref.dtype)
            return tuple(totals)

        zero = jnp.zeros((1, size), F32)
        totals = lax.fori_loop(0, length // ROWS, block, (zero, zero, jnp.zeros((1, width), F32)))

        if final:
            arrived("att")
            homeward = [
                pltpu.make_async_copy(before_ref, home_hbm.at[:, pl.ds(width + size, size)], sems.at[8]),
                pltpu.make_async_copy(dn_out_ref, home_hbm.at[:, pl.ds(0, width)], sems.at[12]),
                pltpu.make_async_copy(att_ref, home_hbm.at[:, pl.ds(width, size)], sems.at[13]),
            ]
        else:
            homeward = [pltpu.make_async_copy(dn_out_ref, dn_hbm_out, sems.at[12])]
            if part:
                homeward.append(pltpu.make_async_copy(att_ref, att_hbm_out, sems.at[13]))
        for copy in homeward:
            copy.start()
        arrived("perm")
        arrived("g")
        def put_slot(place, z, values):
            for s in range(3):
                row = extra + (3 * z + s) * SLOT
                part = values[:, s * size : (s + 1) * size].astype(BF16)
                buffer_ref[side_of(place, core), place // 2, row : row + values.shape[0]] = part

        grad_in = dot(perm_ref[...], d_ref[...])
        grad_attn = dot_tn(att_ref[...], g_ref[...].reshape(length, width))
        gains = jnp.concatenate([totals[0], totals[1], zero], axis=1)
        for index, (place, z) in enumerate(flat.slots()):
            values = grad_in[index * SLOT : (index + 1) * SLOT]
            if (place, z) == (flat.bias_place(), 2):
                start, rows, _, at = ATTN_BLOCKS[part][-1]
                values = jnp.concatenate([values[:at], grad_attn[start : start + rows]])
                values = with_row(values, GAINS_ROW, gains)
            if final and (place, z) == (0, 0):
                values = with_row(values, SLOT - 1, totals[2])
            put_slot(place, z, values)
        for start, rows, place, at in ATTN_BLOCKS[part]:
            if at == 0:
                put_slot(place, 2, grad_attn[start : start + rows])
        stores = [
            pltpu.make_async_copy(buffer_ref.at[side], ref, sems.at[10 + side])
            for side, ref in enumerate((mine_hbm, theirs_hbm))
        ]
        for copy in stores:
            copy.start()
        for copy in [*stores, *homeward]:
            copy.wait()

    qa = [widen(head) for head in range(2)]
    sums = score(0, qa[0])
    out, grad_a = middle(0, sums)
    first = (out, *gradients(0, qa[0], grad_a))
    sums = score(1, qa[1])
    out, grad_a = middle(1, sums)
    second = (out, *gradients(1, qa[1], grad_a))
    mine, _ = lanes(length, 0)
    for index in range(4):
        pairs_ref[index, step] = jnp.where(mine, first[index], second[index]).astype(BF16)

    @pl.when(step == pl.num_programs(0) - 1)
    def _():
        finish()


def attend_part(
    flat, part, core, query, key, value, grad_att, ids, gains, raw, perm, weight_in, dn, came, att
):
    length, width = query.shape
    base, size = PARTS[part]
    final = part == len(PARTS) - 1
    block = pl.BlockSpec((length, PAIR), lambda i: (0, base // PAIR + i))
    vec = pl.BlockSpec((size,), lambda i: (base // size,))
    anywhere = pl.BlockSpec(memory_space=pl.ANY)
    rows = SEQS_IN * 3 * SLOT + (0 if part else length // TOK)
    payload = jax.ShapeDtypeStruct((TOK // 2, rows, size), BF16)
    att_shape = jax.ShapeDtypeStruct((length, size), BF16)
    scratch = [pltpu.VMEM((length, size), BF16)]
    if final:
        results = [jax.ShapeDtypeStruct((length, width + 2 * size), BF16)]
        scratch += [pltpu.VMEM((length, size), BF16), pltpu.VMEM((length, width), BF16)]
    else:
        results = [jax.ShapeDtypeStruct((length, width), F32)] + [att_shape] * min(part, 1)
        scratch += [pltpu.VMEM((length, width), F32)]
    specs = [anywhere] * len(results)
    slots = length // came.shape[0]
    return pl.pallas_call(
        partial(part_kernel, flat, part),
        grid=(size // PAIR,),
        in_specs=[pl.BlockSpec(memory_space=pltpu.SMEM)]
        + [block] * 4
        + [pl.BlockSpec((length, PAIR), lambda i: (0, 0)), vec, vec]
        + [anywhere] * 6,
        out_specs=[*specs, anywhere, anywhere],
        out_shape=[*results, payload, payload],
        scratch_shapes=[
            pltpu.VMEM((2, length, PAIR), BF16),
            pltpu.VMEM((2, length, PAIR), BF16),
            pltpu.VMEM((2, PAIR, length), BF16),
            pltpu.VMEM((2, PAIR, length), BF16),
            pltpu.VMEM((2, length, length), F32),
            pltpu.VMEM((2, length, length), BF16),
            pltpu.VMEM((4, size // PAIR, length, PAIR), BF16),
            pltpu.VMEM((length, 3 * size), BF16),
            pltpu.VMEM((length, 2 * size), F32),
            pltpu.VMEM(perm.shape, BF16),
            pltpu.VMEM((came.shape[0], slots, width), BF16),
            pltpu.VMEM((width, 3 * size), BF16),
            pltpu.VMEM((length, width), F32),
            pltpu.VMEM((came.shape[0], slots, width), BF16),
            pltpu.VMEM((2, *payload.shape), BF16),
            pltpu.SemaphoreType.DMA((14,)),
            *scratch,
        ],
        compiler_params=pltpu.CompilerParams(vmem_limit_bytes=VMEM_LIMIT),
        cost_estimate=pl.CostEstimate(
            flops=48 * length * length * size, bytes_accessed=24 * 2**20, transcendentals=0
        ),
        name=f"attend{part}",
    )(core, query, key, value, grad_att, ids, *gains, raw, perm, weight_in, dn, came, att)


def close_kernel(
    x_ref, g_ref, gain_ref, wattn_ref, part_ref, bias_ref, dn_ref, att0_ref, home_ref,
    out_ref, gin_ref,
):
    width = x_ref.shape[1]
    size = att0_ref.shape[2]
    rows = x_ref[...].astype(F32)
    this, before = home_ref[:, width : width + size], home_ref[:, width + size :]
    attended = jnp.concatenate([att0_ref[0], before, this], axis=1)
    out = rows + dot(attended, wattn_ref[...]) + part_ref[...] + bias_ref[...][None]
    out_ref[...] = out.astype(BF16)
    hat, scale = standardize(rows)
    grad = (dn_ref[...] + home_ref[:, :width].astype(F32)) * gain_ref[...][None]
    mean = jnp.mean(grad, axis=-1, keepdims=True)
    along = jnp.mean(grad * hat, axis=-1, keepdims=True)
    gin_ref[...] = g_ref[...].astype(F32) + scale * (grad - mean - hat * along)


def close(rows, grads, norm_gain, weight_attn, partial_out, bias_down, dn, first, home):
    count, width = rows.shape
    whole = lambda i: (0, 0)
    block = pl.BlockSpec((ROWS, width), lambda i: (i, 0))
    columns = lambda values: pl.BlockSpec((ROWS, values.shape[1]), lambda i: (i, 0))
    vec = pl.BlockSpec((width,), lambda i: (0,))
    square = pl.BlockSpec((width, width), whole)
    return pl.pallas_call(
        close_kernel,
        grid=(count // ROWS,),
        in_specs=[block, block, vec, square, block, vec, block, pl.BlockSpec((1, ROWS, first.shape[2]), lambda i: (i, 0, 0)), columns(home)],
        out_specs=[block, block],
        out_shape=[
            jax.ShapeDtypeStruct((count, width), BF16),
            jax.ShapeDtypeStruct((count, width), F32),
        ],
        compiler_params=pltpu.CompilerParams(vmem_limit_bytes=52 * 2**20),
        cost_estimate=pl.CostEstimate(
            flops=2 * count * width * width, bytes_accessed=18 * 2**20, transcendentals=0
        ),
        name="close",
    )(rows, grads, norm_gain, weight_attn, partial_out, bias_down, dn, first, home)


def total(*values):
    return sum(value.astype(F32) for value in values)


def low(*values):
    return total(*values).astype(BF16)


def pick(values, bit, axis=0):
    return lax.dynamic_index_in_dim(values, bit, axis, keepdims=False)


def across(shift):
    return ("tok", [(i, i ^ shift) for i in range(TOK)])


def share_mlp(payload):
    (place,) = yield [(payload, "sum")]
    (own,) = yield [(by_seq(place[0]), "sum seq")]
    return own


def by_seq_kernel(place_ref, out_ref):
    fill = jnp.zeros((HELD - 4 * SLOT, place_ref.shape[1]), BF16)
    for z in range(2):
        out_ref[z * HELD : z * HELD + 4 * SLOT] = place_ref[z * 4 * SLOT : (z + 1) * 4 * SLOT]
        out_ref[z * HELD + 4 * SLOT : (z + 1) * HELD] = fill
    out_ref[2 * HELD : 3 * HELD] = place_ref[8 * SLOT + HELD :]
    out_ref[3 * HELD :] = place_ref[8 * SLOT : 8 * SLOT + HELD]


def by_seq(place):
    return pl.pallas_call(
        by_seq_kernel,
        out_shape=jax.ShapeDtypeStruct((4 * HELD, place.shape[1]), BF16),
        name="by_seq",
    )(place)


def chip_kernel(slots, core_ref, *refs):
    *refs, out_ref = refs
    parts = len(refs) // 2
    rows = refs[0].shape[1] - slots
    if slots:
        core = core_ref[0]
        for ref, index in ((refs[0], core), (refs[1], 1 - core)):
            out_ref[:, pl.ds(pl.multiple_of(index * slots, slots), slots)] = ref[:, :slots]
    for part in range(parts):
        start = 2 * slots + part * rows
        mine_ref, came_ref = refs[part], refs[parts + part]
        out_ref[:, start : start + rows] = low(mine_ref[:, slots:], came_ref[:, slots:])


def by_chip(slots, core, mine, came):
    chips, rows, size = mine[0].shape
    block = lambda count: pl.BlockSpec((chips // 2, count, size), lambda i: (i, 0, 0))
    count = len(mine) * rows + slots
    return pl.pallas_call(
        partial(chip_kernel, slots),
        grid=(2,),
        in_specs=[pl.BlockSpec(memory_space=pltpu.SMEM)] + [block(rows)] * (2 * len(mine)),
        out_specs=block(count),
        out_shape=jax.ShapeDtypeStruct((chips, count, size), BF16),
        compiler_params=pltpu.CompilerParams(vmem_limit_bytes=16 * 2**20),
        name="by_chip",
    )(core, *mine, *came)


def share_heads_core(theirs):
    (came,) = yield [(theirs, across(1))]
    return came


def share_heads_plane(chips, skip=0):
    (came,) = yield [(chips, "chips")]
    return came, low(jnp.sum(came[:, skip:].astype(F32), axis=0))


def share_heads_seq(plane):
    z = lax.axis_index("seq")
    size = lax.axis_size("seq")
    part_of = lambda index: pick(plane, jnp.minimum(index, SEQS_IN - 1))
    came = yield [
        (part_of((z + step) % size), ("seq", [(i, (i + step) % size) for i in range(size)]))
        for step in range(1, size)
    ]
    return total(part_of(z), *came)


def share_attn(flat, slots):
    packed = jnp.stack(slots).astype(BF16)
    came = [lax.ppermute(packed, "tok", pairs) for pairs in flat.attn_rounds()]
    return came


def regroup(rows):
    (came,) = yield [(rows, "home")]
    return came


def tie(*values):
    leaves, tree = jax.tree.flatten(values)
    return jax.tree.unflatten(tree, lax.optimization_barrier(leaves))


class Moving:
    def __init__(self, chain):
        self.chain = chain
        self.result = None
        self.wanted = next(chain)

    def send(self, operands):
        moved = []
        for operand, (_, way) in zip(operands, self.wanted):
            if way in ("sum", "sum seq"):
                axis = "tok" if way == "sum" else "seq"
                moved.append(lax.psum_scatter(operand, axis, scatter_dimension=0, tiled=True))
            elif way == "chips":
                cores = [[2 * chip + core for chip in range(TOK // 2)] for core in range(2)]
                moved.append(
                    lax.all_to_all(
                        operand, "tok", split_axis=0, concat_axis=0, tiled=True, axis_index_groups=cores
                    )
                )
            elif way == "home":
                moved.append(lax.all_to_all(operand, "tok", split_axis=0, concat_axis=0, tiled=True))
            else:
                moved.append(lax.ppermute(operand, *way))
        return moved

    def take(self, moved):
        try:
            self.wanted = self.chain.send(moved)
        except StopIteration as end:
            self.wanted, self.result = None, end.value

    def finish(self):
        while self.wanted is not None:
            self.take(self.send([operand for operand, _ in self.wanted]))
        return self.result


def beside(work, inputs, moving, loose=()):
    chains = [*moving, *loose]
    operands = [[operand for operand, _ in chain.wanted] for chain in chains]
    inputs, operands = tie(inputs, operands)
    moved = [chain.send(operand) for chain, operand in zip(chains, operands)]
    done = work(*inputs)
    done, moved[: len(moving)] = tie(done, moved[: len(moving)])
    for chain, values in zip(chains, moved):
        chain.take(values)
    return done


def own_slice(flat, device, early, late, passed):
    width = flat.width

    def assemble(d, early, late, passed):
        early = early.astype(F32)
        passed = [values.astype(F32) for values in passed]
        z, place = divmod(d, TOK)
        first, end = flat.first(d), flat.first(d) + flat.rows
        pieces = []
        if first < 1:
            pieces.append((early[SLOT - 1] + late[-1][:, SLOT - 1].reshape(-1))[None])
        if first < flat.bias_at:
            columns = [slots[s] for s in range(3) for slots in late]
            columns += [early[c * SLOT : (c + 1) * SLOT] for c in range(flat.chunks)]
            base = 1 + flat.per_row * flat.input_row(d)
            rows = jnp.concatenate(columns, axis=1).reshape(-1, width)
            pieces.append(rows[max(first, 1) - base : min(end, flat.bias_at) - base])
        if first < flat.attn_at and end > flat.bias_at:
            at = 4 * SLOT
            pieces += [early[at + 16 * c][None] for c in range(flat.chunks)]
            for s in range(2):
                row = [slots[s, GAINS_ROW] for slots in late]
                pieces.append(jnp.concatenate(row)[None])
        if z == 2:
            for part, holder, at, count in flat.attn_pieces(place):
                source = late
                if holder != place:
                    pairs = flat.attn_rounds()
                    source = next(c for c, p in zip(passed, pairs) if (holder, place) in p)
                rows = source[part][:, at : at + count]
                pieces.append(jnp.concatenate([rows[s] for s in range(3)], axis=1))
        if end > flat.down_at:
            low = max(first, flat.down_at)
            start = flat.down_at + flat.down_start(d)
            pieces.append(early[low - start : end - start])
        rows = jnp.concatenate(pieces)
        skip = flat.skip(d)
        return rows.reshape(-1)[skip : skip + flat.total * width // flat.devices]

    branches = [partial(assemble, d) for d in range(flat.devices)]
    return lax.switch(device, branches, early, late, passed)


def sequence_device(
    layer_input,
    norm_gain,
    weight_in,
    bias_in,
    query_gain,
    key_gain,
    weight_attn,
    weight_down,
    bias_down,
    image_ids,
    cotangent,
):
    seqs, slots, width = layer_input.shape
    tok, z = lax.axis_index("tok"), lax.axis_index("seq")
    flat = Flat(width, weight_down.shape[0], lax.axis_size("seq") * TOK)
    features = jnp.array(flat.features(), jnp.int32)[:, None]

    def homeward(rows):
        return Moving(regroup(rows.reshape(seqs, slots, -1)))

    gain = norm_gain
    gains = (query_gain, key_gain)
    marks = jnp.pad(image_ids.astype(BF16)[:, None], ((0, 0), (0, 15), (0, width - slots)))
    rows = layer_input.reshape(seqs * slots, width)
    grads = cotangent.reshape(seqs * slots, width)
    moving = Moving(regroup(jnp.concatenate([layer_input, cotangent, marks], axis=1)))
    part_out, dn, payload = beside(
        partial(mlp, flat),
        (rows, grads, gain, weight_in, bias_in[None], weight_down, features),
        [moving],
    )
    came = moving.result
    early = Moving(share_mlp(payload))
    plane_sums = early.send([operand for operand, _ in early.wanted])
    query, key, value, grad_att, raw, perm, ids = heads(
        came, gain, weight_in, weight_attn, *gains, features
    )
    dn_heads = jnp.zeros((8, 128), F32)
    core = (tok % 2).astype(jnp.int32)[None]
    att = jnp.zeros((8, 128), BF16)

    def run(part, dn_heads, att, chains, loose=()):
        return beside(
            partial(attend_part, flat, part),
            (core, query, key, value, grad_att, ids, gains, raw, perm, weight_in, dn_heads, came, att),
            chains,
            loose,
        )

    dn_heads, mine_0, theirs_0 = run(0, dn_heads, att, [])
    core_0 = Moving(share_heads_core(theirs_0))
    dn_heads, att, mine_1, theirs_1 = run(1, dn_heads, att, [core_0])
    chips = by_chip(slots, core, [mine_0], [core_0.result])
    plane_0, core_1 = Moving(share_heads_plane(chips, 2 * slots)), Moving(share_heads_core(theirs_1))
    last, mine_2, theirs_2 = run(2, dn_heads, att, [core_1], [plane_0])
    first, plane_0 = plane_0.result
    core_2 = Moving(share_heads_core(theirs_2)).finish()
    both = by_chip(0, core, [mine_1, mine_2], [core_1.result, core_2])
    plane_sums, _ = tie(plane_sums, both)
    early.take(plane_sums)
    early.take(early.send([operand for operand, _ in early.wanted]))
    both = Moving(share_heads_plane(both))
    both.take(both.send([operand for operand, _ in both.wanted]))
    shape = (SEQS_IN, 3, SLOT, -1)
    before = Moving(share_heads_seq(plane_0.reshape(shape)))
    moved = before.send([operand for operand, _ in before.wanted])
    both, moved, last = tie(both.result[1], moved, last)
    before.take(moved)
    home = homeward(last)
    planes = [plane.reshape(shape) for plane in jnp.split(both, 2)]
    late = Moving(share_heads_seq(jnp.stack(planes, axis=1))).finish()
    late = [before.result, late[0], late[1]]
    passed = share_attn(flat, late)
    last = home.finish().reshape(seqs * slots, -1)
    out, grad_input = close(
        rows, grads, gain, weight_attn, part_out, bias_down, dn, first, last
    )
    out, grad_input, late, passed = tie(out, grad_input, late, passed)
    grad_weights = own_slice(flat, z * TOK + tok, early.finish(), late, passed)
    shape = (seqs, slots, width)
    return (out.reshape(shape), grad_input.reshape(shape), grad_weights)


def per_device(layer_input, *rest):
    seqs, slots, _ = layer_input.shape
    if lax.axis_size("tok") == seqs == 8 and lax.axis_size("seq") == 4 and slots % 16 == 0:
        return sequence_device(layer_input, *rest)
    return units_device(layer_input, *rest)


def solution(mesh):
    placed = (
        P("seq", "tok", None),
        P(),
        P(),
        P(),
        P(),
        P(),
        P(),
        P(),
        P(),
        P("seq", "tok"),
        P("seq", "tok", None),
    )
    return jax.shard_map(
        per_device,
        mesh=mesh,
        in_specs=placed,
        out_specs=(P("seq", "tok", None), P("seq", "tok", None), P(("seq", "tok"))),
        check_vma=False,
    )
```

```python
from functools import partial

import jax
import jax.numpy as jnp
from jax import lax
from jax.experimental import pallas as pl
from jax.experimental.pallas import tpu as pltpu
from jax.sharding import PartitionSpec as P

HEADS = 12


EPS = 1e-06
NEG = -1e30

F32 = jnp.float32
BF16 = jnp.bfloat16
ROWS = 256
HEAD_DIM = 64
PAIR = 2 * HEAD_DIM
FAR = 192.0
VMEM_LIMIT = 60 * 1024 * 1024


def layer_norm(values, scaling):
    average = jnp.mean(values, axis=-1, keepdims=True)
    shifted = values - average
    spread = jnp.mean(shifted * shifted, axis=-1, keepdims=True)
    return shifted * lax.rsqrt(spread + EPS) * scaling


def head_norms(query_raw, key_raw, gain_query, gain_key):
    return (layer_norm(query_raw, gain_query), layer_norm(key_raw, gain_key))


def to_units(row_values, seq_count, head_count):
    part_len = row_values.shape[0] // seq_count
    shaped = row_values.reshape(seq_count, part_len, head_count, -1).transpose(0, 2, 3, 1)
    return shaped.reshape(seq_count * head_count, -1, part_len)


def from_units(unit_values, seq_count, head_count):
    part_len = unit_values.shape[2]
    shaped = unit_values.reshape(seq_count, head_count, -1, part_len).transpose(0, 3, 1, 2)
    return shaped.reshape(seq_count * part_len, -1)


def block_scores(query_block, key_unit, image_block, slot_ids, score_scale):
    scores = (
        lax.dot_general(
            query_block, key_unit, (((0,), (0,)), ((), ())), preferred_element_type=jnp.float32
        )
        * score_scale
    )
    allowed = image_block[:, None] == slot_ids[None, :]
    return (scores, allowed)


def split_blocks(unit_values, block_len):
    head_dim, length = unit_values.shape
    return unit_values.reshape(head_dim, length // block_len, block_len).transpose(1, 0, 2)


def attend_unit(packed, score_scale):
    query_unit, key_unit, value_unit, slot_ids = packed
    head_dim, length = query_unit.shape
    block_len = min(512, length)
    query_blocks = split_blocks(query_unit, block_len)
    image_blocks = slot_ids.reshape(length // block_len, block_len)

    def one_block(inputs):
        query_block, image_block = inputs
        scores, allowed = block_scores(query_block, key_unit, image_block, slot_ids, score_scale)
        scores = jnp.where(allowed, scores, NEG)
        row_max = jnp.max(scores, axis=-1, keepdims=True)
        shifted = jnp.exp(scores - row_max)
        row_total = jnp.sum(shifted, axis=-1, keepdims=True)
        weights = (shifted / row_total).astype(jnp.bfloat16)
        outputs = lax.dot_general(
            value_unit, weights, (((1,), (1,)), ((), ())), preferred_element_type=jnp.float32
        )
        return (outputs, row_max[:, 0] + jnp.log(row_total[:, 0]))

    outputs, log_total = lax.map(one_block, (query_blocks, image_blocks))
    return (outputs.transpose(1, 0, 2).reshape(head_dim, length), log_total.reshape(length))


def attend_back(packed, score_scale):
    query_unit, key_unit, value_unit, grad_unit, log_total, slot_ids = packed
    head_dim, length = query_unit.shape
    block_len = min(512, length)
    query_blocks = split_blocks(query_unit, block_len)
    grad_blocks = split_blocks(grad_unit, block_len)
    total_blocks = log_total.reshape(length // block_len, block_len)
    image_blocks = slot_ids.reshape(length // block_len, block_len)

    def one_block(carried, inputs):
        grad_key, grad_value = carried
        query_block, grad_block, total_block, image_block = inputs
        scores, allowed = block_scores(query_block, key_unit, image_block, slot_ids, score_scale)
        weights = jnp.where(allowed, jnp.exp(scores - total_block[:, None]), 0.0)
        weights_low = weights.astype(jnp.bfloat16)
        grad_weights = lax.dot_general(
            grad_block, value_unit, (((0,), (0,)), ((), ())), preferred_element_type=jnp.float32
        )
        inner = jnp.sum(weights * grad_weights, axis=-1, keepdims=True)
        grad_scores = (weights * (grad_weights - inner)).astype(jnp.bfloat16)
        grad_query = score_scale * lax.dot_general(
            key_unit, grad_scores, (((1,), (1,)), ((), ())), preferred_element_type=jnp.float32
        )
        grad_key = grad_key + score_scale * lax.dot_general(
            query_block, grad_scores, (((1,), (0,)), ((), ())), preferred_element_type=jnp.float32
        )
        grad_value = grad_value + lax.dot_general(
            grad_block, weights_low, (((1,), (0,)), ((), ())), preferred_element_type=jnp.float32
        )
        return ((grad_key, grad_value), grad_query)

    blank = jnp.zeros((head_dim, length), jnp.float32)
    (grad_key, grad_value), grad_query = lax.scan(
        one_block, (blank, blank), (query_blocks, grad_blocks, total_blocks, image_blocks)
    )
    return (grad_query.transpose(1, 0, 2).reshape(head_dim, length), grad_key, grad_value)


def reduce_grads(flat_grad):
    return lax.psum_scatter(flat_grad, ("seq", "tok"), scatter_dimension=0, tiled=True)


def units_device(
    layer_input,
    norm_gain,
    weight_in,
    bias_in,
    query_gain,
    key_gain,
    weight_attn,
    weight_down,
    bias_down,
    image_ids,
    cotangent,
):
    seq_count, part_len, model_width = layer_input.shape
    row_count = seq_count * part_len
    head_count = HEADS
    head_dim = model_width // head_count
    score_scale = head_dim ** (-0.5)
    whole_ids = lax.all_gather(image_ids, "tok", axis=1, tiled=True)
    unit_count = seq_count * head_count // lax.axis_size("tok")
    first_unit = lax.axis_index("tok") * unit_count
    unit_seq = (first_unit + jnp.arange(unit_count, dtype=jnp.int32)) // head_count
    unit_ids = jnp.take(whole_ids, unit_seq, axis=0)
    input_rows = layer_input.reshape(row_count, model_width).astype(jnp.float32)
    normalized_rows, input_back = jax.vjp(layer_norm, input_rows, norm_gain)
    normed_low = normalized_rows.astype(jnp.bfloat16)
    projected_rows = jnp.dot(normed_low, weight_in, preferred_element_type=jnp.float32)
    query_raw = projected_rows[:, :model_width].reshape(row_count, head_count, head_dim)
    key_raw = projected_rows[:, model_width : 2 * model_width].reshape(
        row_count, head_count, head_dim
    )
    value_low = projected_rows[:, 2 * model_width : 3 * model_width].astype(jnp.bfloat16)
    hidden_in = projected_rows[:, 3 * model_width :] + bias_in
    gain_query = query_gain.reshape(head_count, head_dim)
    gain_key = key_gain.reshape(head_count, head_dim)
    (query_normed, key_normed), heads_back = jax.vjp(
        head_norms, query_raw, key_raw, gain_query, gain_key
    )
    outgoing = (
        to_units(
            query_normed.reshape(row_count, model_width).astype(jnp.bfloat16), seq_count, head_count
        ),
        to_units(
            key_normed.reshape(row_count, model_width).astype(jnp.bfloat16), seq_count, head_count
        ),
        to_units(value_low, seq_count, head_count),
    )
    query_units, key_units, value_units = (
        lax.all_to_all(outgoing[0], "tok", split_axis=0, concat_axis=2, tiled=True),
        lax.all_to_all(outgoing[1], "tok", split_axis=0, concat_axis=2, tiled=True),
        lax.all_to_all(outgoing[2], "tok", split_axis=0, concat_axis=2, tiled=True),
    )
    attention_output, log_total = lax.map(
        partial(attend_unit, score_scale=score_scale),
        (query_units, key_units, value_units, unit_ids),
    )
    returned = lax.all_to_all(
        attention_output.astype(jnp.bfloat16), "tok", split_axis=2, concat_axis=0, tiled=True
    )
    attn_rows = from_units(returned, seq_count, head_count)
    activation, gelu_back = jax.vjp(partial(jax.nn.gelu, approximate=False), hidden_in)
    act_low = activation.astype(jnp.bfloat16)
    result_rows = input_rows + jnp.dot(attn_rows, weight_attn, preferred_element_type=jnp.float32)
    result_rows = (
        result_rows + jnp.dot(act_low, weight_down, preferred_element_type=jnp.float32) + bias_down
    )
    layer_output = result_rows.astype(jnp.bfloat16).reshape(seq_count, part_len, model_width)
    grad_rows = cotangent.reshape(row_count, model_width)
    grad_full = grad_rows.astype(jnp.float32)
    contract_rows = (((0,), (0,)), ((), ()))
    contract_cols = (((1,), (1,)), ((), ()))
    grad_bias_down = jnp.sum(grad_full, axis=0)
    grad_weight_down = lax.dot_general(
        act_low, grad_rows, contract_rows, preferred_element_type=jnp.float32
    )
    grad_weight_attn = lax.dot_general(
        attn_rows, grad_rows, contract_rows, preferred_element_type=jnp.float32
    )
    grad_activation = lax.dot_general(
        grad_rows, weight_down, contract_cols, preferred_element_type=jnp.float32
    )
    grad_hidden = gelu_back(grad_activation)[0]
    grad_bias_in = jnp.sum(grad_hidden, axis=0)
    grad_attended = lax.dot_general(
        grad_rows, weight_attn, contract_cols, preferred_element_type=jnp.float32
    )
    grad_units = lax.all_to_all(
        to_units(grad_attended.astype(jnp.bfloat16), seq_count, head_count),
        "tok",
        split_axis=0,
        concat_axis=2,
        tiled=True,
    )
    grad_query_u, grad_key_u, grad_value_u = lax.map(
        partial(attend_back, score_scale=score_scale),
        (query_units, key_units, value_units, grad_units, log_total, unit_ids),
    )
    back_query, back_key, back_value = (
        lax.all_to_all(
            grad_query_u.astype(jnp.bfloat16), "tok", split_axis=2, concat_axis=0, tiled=True
        ),
        lax.all_to_all(
            grad_key_u.astype(jnp.bfloat16), "tok", split_axis=2, concat_axis=0, tiled=True
        ),
        lax.all_to_all(
            grad_value_u.astype(jnp.bfloat16), "tok", split_axis=2, concat_axis=0, tiled=True
        ),
    )
    grad_query_n = (
        from_units(back_query, seq_count, head_count)
        .astype(jnp.float32)
        .reshape(row_count, head_count, head_dim)
    )
    grad_key_n = (
        from_units(back_key, seq_count, head_count)
        .astype(jnp.float32)
        .reshape(row_count, head_count, head_dim)
    )
    grad_value_rows = from_units(back_value, seq_count, head_count).astype(jnp.float32)
    grad_query_raw, grad_key_raw, grad_gain_query, grad_gain_key = heads_back(
        (grad_query_n, grad_key_n)
    )
    grad_projected = jnp.concatenate(
        [
            grad_query_raw.reshape(row_count, model_width),
            grad_key_raw.reshape(row_count, model_width),
            grad_value_rows,
            grad_hidden,
        ],
        axis=1,
    ).astype(jnp.bfloat16)
    grad_weight_in = lax.dot_general(
        normed_low, grad_projected, contract_rows, preferred_element_type=jnp.float32
    )
    grad_normed = lax.dot_general(
        grad_projected, weight_in, contract_cols, preferred_element_type=jnp.float32
    )
    grad_input_rows, grad_norm_gain = input_back(grad_normed)
    grad_input = (grad_full + grad_input_rows).reshape(seq_count, part_len, model_width)
    pieces = [
        grad_norm_gain,
        grad_weight_in,
        grad_bias_in,
        grad_gain_query,
        grad_gain_key,
        grad_weight_attn,
        grad_weight_down,
        grad_bias_down,
    ]
    flat_grad = jnp.concatenate([tensor.reshape(-1) for tensor in pieces])
    grad_weights = reduce_grads(flat_grad)
    return (layer_output, grad_input, grad_weights)


SLOT = 48
HELD = 304
PARTS = ((0, 256), (256, 256), (512, 256))
TOK = 8
SEQS_IN = 3
GAINS_ROW = 28
PLACE_ROWS = 4 * SLOT * 2 + 2 * HELD
ATTN_BLOCKS = (
    ((0, 48, 6, 0), (48, 48, 7, 0), (96, 48, 3, 0), (144, 48, 4, 0), (192, 48, 5, 0), (240, 16, 2, 32)),
    ((0, 48, 3, 0), (48, 48, 5, 0), (96, 48, 7, 0), (144, 48, 4, 0), (192, 48, 6, 0), (240, 16, 2, 32)),
    ((0, 48, 4, 0), (48, 48, 6, 0), (96, 48, 7, 0), (144, 48, 5, 0), (192, 48, 3, 0), (240, 16, 2, 32)),
)


class Flat:
    def __init__(self, width, hidden, devices):
        self.width = width
        self.chunks = hidden // width
        self.per_row = 3 + self.chunks
        self.bias_at = 1 + self.per_row * width
        self.gains_at = self.bias_at + self.chunks
        self.attn_at = self.gains_at + 2
        self.down_at = self.attn_at + width
        self.total = self.down_at + hidden + 1
        self.devices = devices
        self.rows = self.total // devices + 1

    def first(self, device):
        return device * self.total // self.devices

    def skip(self, device):
        return (device * self.total) % self.devices * self.width // self.devices

    def input_row(self, device):
        return max(0, (self.first(device) - 1) // self.per_row)

    def slots(self):
        pairs = [(place, z) for place in range(TOK) for z in range(3)]
        return [(place, z) for place, z in pairs if self.first(z * TOK + place) < self.bias_at]

    def features(self):
        return [self.input_row(z * TOK + place) + i for place, z in self.slots() for i in range(SLOT)]

    def bias_place(self):
        return next(d for d in range(self.devices) if self.first(d + 1) > self.bias_at) % TOK

    def down_start(self, device):
        start = self.first(device) - self.down_at
        return None if start + self.rows <= 0 else max(0, start) // 16 * 16

    def attn_pieces(self, place):
        low = self.first(2 * TOK + place) - self.attn_at
        high = low + self.rows
        found = []
        for part, (base, _) in enumerate(PARTS):
            for start, rows, holder, at in ATTN_BLOCKS[part]:
                begin, end = max(base + start, low), min(base + start + rows, high)
                if begin < end:
                    found.append((part, holder, at + begin - base - start, end - begin))
        return found

    def attn_rounds(self):
        pairs = {(h, p) for p in range(TOK) for _, h, _, _ in self.attn_pieces(p) if h != p}
        degree = lambda pair: sum((pair[0] == h) + (pair[1] == p) for h, p in pairs)
        rounds = []
        for holder, place in sorted(pairs, key=lambda pair: (-degree(pair), pair)):
            for taken in rounds:
                if all(holder != h and place != p for h, p in taken):
                    taken.append((holder, place))
                    break
            else:
                rounds.append([(holder, place)])
        return rounds


def side_of(place, core):
    return core if place % 2 == 0 else 1 - core


def selection(features_ref, width):
    columns = lax.broadcasted_iota(jnp.int32, (features_ref.shape[0], width), 1)
    return jnp.where(columns == features_ref[...], 1.0, 0.0).astype(BF16)


def dot(left, right):
    return jnp.dot(left, right, preferred_element_type=F32)


def dot_nt(left, right):
    return lax.dot_general(left, right, (((1,), (1,)), ((), ())), preferred_element_type=F32)


def dot_tn(left, right):
    return lax.dot_general(left, right, (((0,), (0,)), ((), ())), preferred_element_type=F32)


def standardize(rows):
    shifted = rows - jnp.mean(rows, axis=-1, keepdims=True)
    scale = lax.rsqrt(jnp.mean(shifted * shifted, axis=-1, keepdims=True) + EPS)
    return shifted * scale, scale


def head_means(values):
    width = min(4 * HEAD_DIM, values.shape[1])
    row = lax.broadcasted_iota(jnp.int32, (width, width), 0)
    column = lax.broadcasted_iota(jnp.int32, (width, width), 1)
    ones = jnp.where((row >> 6) == (column >> 6), 1.0, 0.0).astype(BF16)
    values = values.astype(BF16)
    parts = [
        dot(values[:, start : start + width], ones) for start in range(0, values.shape[1], width)
    ]
    return jnp.concatenate(parts, axis=1) * (1.0 / HEAD_DIM)


def head_standardize(raw):
    shifted = raw - head_means(raw)
    scale = lax.rsqrt(head_means(shifted * shifted) + EPS)
    return shifted * scale, scale


def gelu_pair(pre):
    phi = 0.5 + 0.5 * lax.erf(pre * (0.5**0.5))
    density = jnp.exp(-0.5 * pre * pre) * 0.3989422804014327
    return pre * phi, phi + pre * density


def with_row(values, row, vector):
    index = lax.broadcasted_iota(jnp.int32, values.shape, 0)
    return jnp.where(index == row, vector, values)


def mlp_kernel(
    flat, x_ref, g_ref, gain_ref, wh_ref, bias_ref, wd_ref, features_ref,
    out_low_ref, dn_low_ref, payload_ref,
    out_ref, dn_ref, norm_ref, perm_ref, act_ref, dh_ref, gbd_ref, buffer_ref, sems,
):
    step = pl.program_id(0)
    last = flat.chunks - 1
    width = flat.width
    count = x_ref.shape[0] // ROWS

    @pl.when(step == 0)
    def _():
        gbd_ref[...] = jnp.zeros_like(gbd_ref)
        buffer_ref[:, 8 * SLOT + HELD :] = jnp.zeros((TOK, HELD, width), BF16)

        def block(i, carry):
            rows = pl.ds(pl.multiple_of(i * ROWS, ROWS), ROWS)
            hat, _ = standardize(x_ref[rows].astype(F32))
            norm_ref[rows] = (hat * gain_ref[...][None]).astype(BF16)
            out_ref[rows] = jnp.zeros_like(out_ref[rows])
            dn_ref[rows] = jnp.zeros_like(dn_ref[rows])
            gbd_ref[...] += jnp.sum(g_ref[rows].astype(F32), axis=0, keepdims=True)
            return carry

        lax.fori_loop(0, count, block, 0)
        perm_ref[...] = dot_nt(selection(features_ref, width), norm_ref[...]).astype(BF16)

    def products(i):
        rows = slice(i * ROWS, (i + 1) * ROWS)
        pre = dot(norm_ref[rows], wh_ref[...]) + bias_ref[...]
        return pre, dot_nt(g_ref[rows], wd_ref[...])

    grad_bias = jnp.zeros((1, width), F32)
    ahead = products(0)
    for i in range(count):
        rows = slice(i * ROWS, (i + 1) * ROWS)
        pre, dh = ahead
        if i + 1 < count:
            ahead = products(i + 1)
        act, slope = gelu_pair(pre)
        act_low = act.astype(BF16)
        dh = dh * slope
        dh_low = dh.astype(BF16)
        act_ref[rows] = act_low
        dh_ref[rows] = dh_low
        out_ref[rows] += dot(act_low, wd_ref[...])
        dn_ref[rows] += dot_nt(dh_low, wh_ref[...])
        grad_bias += jnp.sum(dh, axis=0, keepdims=True)

    def store(index, row, rows, place=None):
        places = slice(None) if place is None else place
        return pltpu.make_async_copy(
            buffer_ref.at[places, pl.ds(row, rows)], payload_ref.at[places, pl.ds(row, rows)], sems.at[index]
        )

    mixed = 8 * SLOT + HELD
    inputs = lambda chunk: [store(2 * chunk + z, (4 * z + chunk) * SLOT, SLOT) for z in range(2)]
    done = [[] for _ in range(flat.chunks)]
    for place in range(TOK):
        start = flat.down_start(3 * TOK + place)
        chunk = min((start + HELD - 1) // width, last)
        done[chunk].append((2 * flat.chunks + place, 8 * SLOT, HELD, place))
        start = flat.down_start(2 * TOK + place)
        chunk = last if start is None else min((start + HELD - 1) // width, last)
        done[chunk].append((2 * flat.chunks + TOK + place, mixed, HELD, place))

    grad_down = dot_tn(act_ref[...], g_ref[...])
    grad_in = dot(perm_ref[...], dh_ref[...])
    shift = pl.multiple_of(step * SLOT, SLOT)
    for index, (place, z) in enumerate(flat.slots()):
        part = grad_in[index * SLOT : (index + 1) * SLOT]
        at = z * 4 * SLOT if z < 2 else mixed
        buffer_ref[place, pl.ds(at + shift, SLOT)] = part.astype(BF16)

    for chunk in range(flat.chunks):

        @pl.when(step == chunk)
        def _():
            low = chunk * width
            for device in range(2 * TOK, 4 * TOK):
                start = flat.down_start(device)
                if start is None:
                    continue
                place, at = device % TOK, 8 * SLOT if device >= 3 * TOK else mixed
                begin, end = max(start, low), min(start + HELD, low + width)
                if begin < end:
                    part = grad_down[begin - low : end - low].astype(BF16)
                    buffer_ref[place, at + begin - start : at + end - start] = part
                if chunk == last and start + HELD > low + width:
                    tail = with_row(jnp.zeros((16, width), F32), 0, gbd_ref[...])
                    row = at + low + width - start
                    buffer_ref[place, row : row + 16] = tail.astype(BF16)
            tail = with_row(jnp.zeros((16, width), F32), 0, grad_bias).astype(BF16)
            at = mixed + 4 * SLOT + 16 * chunk
            buffer_ref[flat.bias_place(), at : at + 16] = tail
            if chunk == 0:
                inputs(0)[1].start()
            else:
                for copy in inputs(chunk):
                    copy.start()
            for args in done[chunk]:
                store(*args).start()

    @pl.when(step == last)
    def _():
        def block(i, total):
            rows = pl.ds(pl.multiple_of(i * ROWS, ROWS), ROWS)
            hat, _ = standardize(x_ref[rows].astype(F32))
            return total + jnp.sum(dn_ref[rows] * hat, axis=0, keepdims=True)

        total = lax.fori_loop(0, count, block, jnp.zeros((1, width), F32))
        out_low_ref[...] = out_ref[...].astype(BF16)
        dn_low_ref[...] = dn_ref[...].astype(BF16)
        kept = buffer_ref[0, SLOT - 16 : SLOT].astype(F32)
        buffer_ref[0, SLOT - 16 : SLOT] = with_row(kept, 15, total).astype(BF16)
        inputs(0)[0].start()
        for chunk in range(flat.chunks):
            for copy in inputs(chunk):
                copy.wait()
            for args in done[chunk]:
                store(*args).wait()


def mlp(flat, rows, grads, norm_gain, weight_in, bias_in, weight_down, features):
    count, width = rows.shape
    chunks = flat.chunks
    whole = lambda i: (0, 0)
    once = pl.Buffered(1)
    full = pl.BlockSpec((count, width), whole, pipeline_mode=once)
    payload = jax.ShapeDtypeStruct((TOK, PLACE_ROWS, width), BF16)
    return pl.pallas_call(
        partial(mlp_kernel, flat),
        grid=(chunks,),
        in_specs=[
            full,
            full,
            pl.BlockSpec((width,), lambda i: (0,)),
            pl.BlockSpec((width, width), lambda i: (0, i + 3)),
            pl.BlockSpec((1, width), lambda i: (0, i)),
            pl.BlockSpec((width, width), lambda i: (i, 0)),
            pl.BlockSpec(features.shape, whole, pipeline_mode=once),
        ],
        out_specs=[
            pl.BlockSpec((count, width), whole),
            pl.BlockSpec((count, width), whole),
            pl.BlockSpec(memory_space=pl.ANY),
        ],
        out_shape=[
            jax.ShapeDtypeStruct((count, width), BF16),
            jax.ShapeDtypeStruct((count, width), BF16),
            payload,
        ],
        scratch_shapes=[
            pltpu.VMEM((count, width), F32),
            pltpu.VMEM((count, width), F32),
            pltpu.VMEM((count, width), BF16),
            pltpu.VMEM((features.shape[0], count), BF16),
            pltpu.VMEM((count, width), BF16),
            pltpu.VMEM((count, width), BF16),
            pltpu.VMEM((1, width), F32),
            pltpu.VMEM(payload.shape, BF16),
            pltpu.SemaphoreType.DMA((2 * chunks + 2 * TOK,)),
        ],
        compiler_params=pltpu.CompilerParams(vmem_limit_bytes=VMEM_LIMIT),
        cost_estimate=pl.CostEstimate(
            flops=12 * count * width * width * chunks, bytes_accessed=32 * 2**20, transcendentals=0
        ),
        name="mlp",
    )(rows, grads, norm_gain, weight_in, bias_in, weight_down, features)


def heads_kernel(
    x_ref, g_ref, gain_ref, wqkv_ref, wattn_ref, qgain_ref, kgain_ref, features_ref, marks_ref,
    q_ref, k_ref, v_ref, do_ref, raw_ref, perm_ref, ids_ref,
    pick_ref,
):
    width = x_ref.shape[2]

    @pl.when(pl.program_id(0) == 0)
    def _():
        pick_ref[...] = selection(features_ref, width)

    slots = x_ref.shape[1]
    for group in range(x_ref.shape[0]):
        ids = marks_ref[group, :1, :slots].astype(F32)
        ids_ref[group * slots : (group + 1) * slots] = jnp.broadcast_to(ids, (PAIR, slots)).T
    hat, _ = standardize(x_ref[...].reshape(ROWS, width).astype(F32))
    normed = (hat * gain_ref[...][None]).astype(BF16)
    grads = g_ref[...].reshape(ROWS, width)
    perm_ref[...] = dot_nt(pick_ref[...], normed).astype(BF16)
    q_raw = dot(normed, wqkv_ref[:, :width])
    raw_ref[:, :width] = q_raw
    q_ref[...] = (head_standardize(q_raw)[0] * qgain_ref[...][None]).astype(BF16)
    k_raw = dot(normed, wqkv_ref[:, width : 2 * width])
    raw_ref[:, width:] = k_raw
    k_ref[...] = (head_standardize(k_raw)[0] * kgain_ref[...][None]).astype(BF16)
    v_ref[...] = dot(normed, wqkv_ref[:, 2 * width :]).astype(BF16)
    do_ref[...] = dot_nt(grads, wattn_ref[...]).astype(BF16)


def heads(came, norm_gain, weight_in, weight_attn, query_gain, key_gain, features):
    seqs, held, width = came.shape
    slots = held // 2 // 16 * 16
    count = seqs * slots
    whole = lambda i: (0, 0)
    block = pl.BlockSpec((ROWS, width), lambda i: (i, 0))
    vec = pl.BlockSpec((width,), lambda i: (0,))
    low = jax.ShapeDtypeStruct((count, width), BF16)
    group = (ROWS // slots, slots, width)
    return pl.pallas_call(
        heads_kernel,
        grid=(count // ROWS,),
        in_specs=[
            pl.BlockSpec(group, lambda i: (i, 0, 0)),
            pl.BlockSpec(group, lambda i: (i, 1, 0)),
            vec,
            pl.BlockSpec((width, 3 * width), whole),
            pl.BlockSpec((width, width), whole),
            vec,
            vec,
            pl.BlockSpec(features.shape, whole),
            pl.BlockSpec((ROWS // slots, 16, width), lambda i: (i, 2 * slots // 16, 0)),
        ],
        out_specs=[block] * 4
        + [
            pl.BlockSpec((ROWS, 2 * width), lambda i: (i, 0)),
            pl.BlockSpec((features.shape[0], ROWS), lambda i: (0, i)),
            pl.BlockSpec((ROWS, PAIR), lambda i: (i, 0)),
        ],
        out_shape=[low] * 4
        + [
            jax.ShapeDtypeStruct((count, 2 * width), F32),
            jax.ShapeDtypeStruct((features.shape[0], count), BF16),
            jax.ShapeDtypeStruct((count, PAIR), F32),
        ],
        scratch_shapes=[pltpu.VMEM((features.shape[0], width), BF16)],
        compiler_params=pltpu.CompilerParams(vmem_limit_bytes=VMEM_LIMIT),
        cost_estimate=pl.CostEstimate(
            flops=10 * count * width * width, bytes_accessed=26 * 2**20, transcendentals=0
        ),
        name="heads",
    )(came, came, norm_gain, weight_in, weight_attn, query_gain, key_gain, features, came)


def part_kernel(
    flat, part, core_ref, q_ref, k_ref, v_ref, do_ref, ids_ref, qgain_ref, kgain_ref,
    raw_hbm, perm_hbm, win_hbm, dn_hbm, came_hbm, att_hbm,
    *rest,
):
    step = pl.program_id(0)
    length = q_ref.shape[0]
    width = flat.width
    base, size = PARTS[part]
    final = part == len(PARTS) - 1
    if final:
        home_hbm, mine_hbm, theirs_hbm, *rest = rest
        *rest, att_ref, before_ref, dn_out_ref = rest
    elif part:
        dn_hbm_out, att_hbm_out, mine_hbm, theirs_hbm, *rest = rest
        *rest, att_ref, dn_out_ref = rest
    else:
        dn_hbm_out, mine_hbm, theirs_hbm, *rest = rest
        *rest, att_ref, dn_out_ref = rest
    ka_ref, va_ref, kat_ref, vat_ref, p_ref, plow_ref, pairs_ref, d_ref, *rest = rest
    raw_ref, perm_ref, g_ref, w_ref, dn_ref, x_ref, buffer_ref, sems = rest

    core = core_ref[0]
    slots = length // TOK
    extra = 0 if part else slots
    loads = {
        "raw": [
            pltpu.make_async_copy(
                raw_hbm.at[:, pl.ds(s * width + base, size)],
                raw_ref.at[:, pl.ds(s * size, size)],
                sems.at[s],
            )
            for s in range(2)
        ],
        "w": [
            pltpu.make_async_copy(
                win_hbm.at[:, pl.ds(s * width + base, size)],
                w_ref.at[:, pl.ds(s * size, size)],
                sems.at[2 + s],
            )
            for s in range(3)
        ],
        "perm": [pltpu.make_async_copy(perm_hbm, perm_ref, sems.at[5])],
        "g": [pltpu.make_async_copy(came_hbm.at[:, pl.ds(slots, slots)], g_ref, sems.at[6])],
    }
    if part:
        loads["dn"] = [pltpu.make_async_copy(dn_hbm, dn_ref, sems.at[7])]
    if final:
        loads["x"] = [pltpu.make_async_copy(came_hbm.at[:, pl.ds(0, slots)], x_ref, sems.at[8])]
        loads["att"] = [pltpu.make_async_copy(att_hbm, before_ref, sems.at[9])]

    @pl.when(step == 0)
    def _():
        for group in loads.values():
            for copy in group:
                copy.start()

    def arrived(name):
        for copy in loads[name]:
            copy.wait()

    def lanes(count, head):
        lane = lax.broadcasted_iota(jnp.int32, (count, PAIR), 1)
        return (lane >> 6) == head, lane - (1 - head) * HEAD_DIM

    ids = ids_ref[...].astype(jnp.int32) + 1

    def widen(head):
        mine, spare = lanes(length, head)
        marks = jnp.where(spare == ids, 1.0, jnp.where(spare == 17, -FAR, 0.0))
        ka = jnp.where(mine, k_ref[...].astype(F32), marks)
        ka_ref[head] = ka.astype(BF16)
        kat_ref[head] = ka.T.astype(BF16)
        marks = jnp.where((spare == 0) | (spare == 1), 1.0, 0.0)
        va = jnp.where(mine, v_ref[...].astype(F32), marks)
        va_ref[head] = va.astype(BF16)
        vat_ref[head] = va.T.astype(BF16)
        marks = jnp.where(spare == ids, FAR, jnp.where(spare == 17, 1.0, 0.0))
        return jnp.where(mine, q_ref[...].astype(F32) * (HEAD_DIM**-0.5), marks).astype(BF16)

    def score(head, qa):
        grown = jnp.exp(dot_nt(ka_ref[head], qa))
        p_ref[head] = grown
        low = grown.astype(BF16)
        plow_ref[head] = low
        return dot(vat_ref[head], low)

    def middle(head, sums):
        mine, spare = lanes(length, head)
        grad = do_ref[...].astype(F32)
        out = sums.T
        first = (1 - head) * HEAD_DIM
        inverse = 1.0 / out[:, first : first + 1]
        out = out * inverse
        inner = jnp.sum(jnp.where(mine, grad * out, 0.0), axis=-1, keepdims=True)
        offset = -inner * inverse
        high = offset.astype(BF16).astype(F32)
        marks = jnp.where(spare == 0, high, jnp.where(spare == 1, offset - high, 0.0))
        return out, jnp.where(mine, grad * inverse, marks).astype(BF16)

    def gradients(head, qa, grad_a):
        ds = (p_ref[head] * dot_nt(va_ref[head], grad_a)).astype(BF16)
        dv = dot(plow_ref[head], grad_a)
        dk = dot(ds, qa)
        dq = dot(kat_ref[head], ds).T * (HEAD_DIM**-0.5)
        return dq, dk, dv

    def finish():
        both = lambda index: jnp.concatenate([pairs_ref[index, pair] for pair in range(2)], axis=1)
        att_ref[...] = both(0)
        if extra:
            for place in range(TOK):
                own = att_ref[place * slots : (place + 1) * slots]
                buffer_ref[side_of(place, core), place // 2, :slots] = own
        for side in range(3):
            d_ref[:, side * size : (side + 1) * size] = both(1 + side)
        arrived("raw")
        arrived("w")
        if part:
            arrived("dn")
        if final:
            arrived("x")
            group = ROWS // x_ref.shape[1]

        def block(i, totals):
            rows = pl.ds(pl.multiple_of(i * ROWS, ROWS), ROWS)
            totals = list(totals)
            for side, gain_ref in enumerate((qgain_ref, kgain_ref)):
                lane = slice(side * size, (side + 1) * size)
                hat, scale = head_standardize(raw_ref[rows, lane])
                grad = d_ref[rows, lane].astype(F32)
                totals[side] += jnp.sum(grad * hat, axis=0, keepdims=True)
                grad = grad * gain_ref[...][None]
                grad = scale * (grad - head_means(grad) - hat * head_means(grad * hat))
                d_ref[rows, lane] = grad.astype(BF16)
            dn = dot_nt(d_ref[rows], w_ref[...])
            if part:
                dn = dn + dn_ref[rows]
            if final:
                x = x_ref[pl.ds(i * group, group)].reshape(ROWS, width).astype(F32)
                totals[2] += jnp.sum(dn * standardize(x)[0], axis=0, keepdims=True)
            dn_out_ref[rows] = dn.astype(dn_out_ref.dtype)
            return tuple(totals)

        zero = jnp.zeros((1, size), F32)
        totals = lax.fori_loop(0, length // ROWS, block, (zero, zero, jnp.zeros((1, width), F32)))

        if final:
            arrived("att")
            homeward = [
                pltpu.make_async_copy(before_ref, home_hbm.at[:, pl.ds(width + size, size)], sems.at[8]),
                pltpu.make_async_copy(dn_out_ref, home_hbm.at[:, pl.ds(0, width)], sems.at[12]),
                pltpu.make_async_copy(att_ref, home_hbm.at[:, pl.ds(width, size)], sems.at[13]),
            ]
        else:
            homeward = [pltpu.make_async_copy(dn_out_ref, dn_hbm_out, sems.at[12])]
            if part:
                homeward.append(pltpu.make_async_copy(att_ref, att_hbm_out, sems.at[13]))
        for copy in homeward:
            copy.start()
        arrived("perm")
        arrived("g")
        def put_slot(place, z, values):
            for s in range(3):
                row = extra + (3 * z + s) * SLOT
                part = values[:, s * size : (s + 1) * size].astype(BF16)
                buffer_ref[side_of(place, core), place // 2, row : row + values.shape[0]] = part

        grad_in = dot(perm_ref[...], d_ref[...])
        grad_attn = dot_tn(att_ref[...], g_ref[...].reshape(length, width))
        gains = jnp.concatenate([totals[0], totals[1], zero], axis=1)
        for index, (place, z) in enumerate(flat.slots()):
            values = grad_in[index * SLOT : (index + 1) * SLOT]
            if (place, z) == (flat.bias_place(), 2):
                start, rows, _, at = ATTN_BLOCKS[part][-1]
                values = jnp.concatenate([values[:at], grad_attn[start : start + rows]])
                values = with_row(values, GAINS_ROW, gains)
            if final and (place, z) == (0, 0):
                values = with_row(values, SLOT - 1, totals[2])
            put_slot(place, z, values)
        for start, rows, place, at in ATTN_BLOCKS[part]:
            if at == 0:
                put_slot(place, 2, grad_attn[start : start + rows])
        stores = [
            pltpu.make_async_copy(buffer_ref.at[side], ref, sems.at[10 + side])
            for side, ref in enumerate((mine_hbm, theirs_hbm))
        ]
        for copy in stores:
            copy.start()
        for copy in [*stores, *homeward]:
            copy.wait()

    qa = [widen(head) for head in range(2)]
    sums = score(0, qa[0])
    out, grad_a = middle(0, sums)
    first = (out, *gradients(0, qa[0], grad_a))
    sums = score(1, qa[1])
    out, grad_a = middle(1, sums)
    second = (out, *gradients(1, qa[1], grad_a))
    mine, _ = lanes(length, 0)
    for index in range(4):
        pairs_ref[index, step] = jnp.where(mine, first[index], second[index]).astype(BF16)

    @pl.when(step == pl.num_programs(0) - 1)
    def _():
        finish()


def attend_part(
    flat, part, core, query, key, value, grad_att, ids, gains, raw, perm, weight_in, dn, came, att
):
    length, width = query.shape
    base, size = PARTS[part]
    final = part == len(PARTS) - 1
    block = pl.BlockSpec((length, PAIR), lambda i: (0, base // PAIR + i))
    vec = pl.BlockSpec((size,), lambda i: (base // size,))
    anywhere = pl.BlockSpec(memory_space=pl.ANY)
    rows = SEQS_IN * 3 * SLOT + (0 if part else length // TOK)
    payload = jax.ShapeDtypeStruct((TOK // 2, rows, size), BF16)
    att_shape = jax.ShapeDtypeStruct((length, size), BF16)
    scratch = [pltpu.VMEM((length, size), BF16)]
    if final:
        results = [jax.ShapeDtypeStruct((length, width + 2 * size), BF16)]
        scratch += [pltpu.VMEM((length, size), BF16), pltpu.VMEM((length, width), BF16)]
    else:
        results = [jax.ShapeDtypeStruct((length, width), F32)] + [att_shape] * min(part, 1)
        scratch += [pltpu.VMEM((length, width), F32)]
    specs = [anywhere] * len(results)
    slots = length // came.shape[0]
    return pl.pallas_call(
        partial(part_kernel, flat, part),
        grid=(size // PAIR,),
        in_specs=[pl.BlockSpec(memory_space=pltpu.SMEM)]
        + [block] * 4
        + [pl.BlockSpec((length, PAIR), lambda i: (0, 0)), vec, vec]
        + [anywhere] * 6,
        out_specs=[*specs, anywhere, anywhere],
        out_shape=[*results, payload, payload],
        scratch_shapes=[
            pltpu.VMEM((2, length, PAIR), BF16),
            pltpu.VMEM((2, length, PAIR), BF16),
            pltpu.VMEM((2, PAIR, length), BF16),
            pltpu.VMEM((2, PAIR, length), BF16),
            pltpu.VMEM((2, length, length), F32),
            pltpu.VMEM((2, length, length), BF16),
            pltpu.VMEM((4, size // PAIR, length, PAIR), BF16),
            pltpu.VMEM((length, 3 * size), BF16),
            pltpu.VMEM((length, 2 * size), F32),
            pltpu.VMEM(perm.shape, BF16),
            pltpu.VMEM((came.shape[0], slots, width), BF16),
            pltpu.VMEM((width, 3 * size), BF16),
            pltpu.VMEM((length, width), F32),
            pltpu.VMEM((came.shape[0], slots, width), BF16),
            pltpu.VMEM((2, *payload.shape), BF16),
            pltpu.SemaphoreType.DMA((14,)),
            *scratch,
        ],
        compiler_params=pltpu.CompilerParams(vmem_limit_bytes=VMEM_LIMIT),
        cost_estimate=pl.CostEstimate(
            flops=48 * length * length * size, bytes_accessed=24 * 2**20, transcendentals=0
        ),
        name=f"attend{part}",
    )(core, query, key, value, grad_att, ids, *gains, raw, perm, weight_in, dn, came, att)


def close_kernel(
    x_ref, g_ref, gain_ref, wattn_ref, part_ref, bias_ref, dn_ref, att0_ref, home_ref,
    out_ref, gin_ref,
):
    width = x_ref.shape[1]
    size = att0_ref.shape[2]
    rows = x_ref[...].astype(F32)
    this, before = home_ref[:, width : width + size], home_ref[:, width + size :]
    attended = jnp.concatenate([att0_ref[0], before, this], axis=1)
    out = rows + dot(attended, wattn_ref[...]) + part_ref[...] + bias_ref[...][None]
    out_ref[...] = out.astype(BF16)
    hat, scale = standardize(rows)
    grad = (dn_ref[...] + home_ref[:, :width].astype(F32)) * gain_ref[...][None]
    mean = jnp.mean(grad, axis=-1, keepdims=True)
    along = jnp.mean(grad * hat, axis=-1, keepdims=True)
    gin_ref[...] = g_ref[...].astype(F32) + scale * (grad - mean - hat * along)


def close(rows, grads, norm_gain, weight_attn, partial_out, bias_down, dn, first, home):
    count, width = rows.shape
    whole = lambda i: (0, 0)
    block = pl.BlockSpec((ROWS, width), lambda i: (i, 0))
    columns = lambda values: pl.BlockSpec((ROWS, values.shape[1]), lambda i: (i, 0))
    vec = pl.BlockSpec((width,), lambda i: (0,))
    square = pl.BlockSpec((width, width), whole)
    return pl.pallas_call(
        close_kernel,
        grid=(count // ROWS,),
        in_specs=[block, block, vec, square, block, vec, block, pl.BlockSpec((1, ROWS, first.shape[2]), lambda i: (i, 0, 0)), columns(home)],
        out_specs=[block, block],
        out_shape=[
            jax.ShapeDtypeStruct((count, width), BF16),
            jax.ShapeDtypeStruct((count, width), F32),
        ],
        compiler_params=pltpu.CompilerParams(vmem_limit_bytes=52 * 2**20),
        cost_estimate=pl.CostEstimate(
            flops=2 * count * width * width, bytes_accessed=18 * 2**20, transcendentals=0
        ),
        name="close",
    )(rows, grads, norm_gain, weight_attn, partial_out, bias_down, dn, first, home)


def total(*values):
    return sum(value.astype(F32) for value in values)


def low(*values):
    return total(*values).astype(BF16)


def pick(values, bit, axis=0):
    return lax.dynamic_index_in_dim(values, bit, axis, keepdims=False)


def across(shift):
    return ("tok", [(i, i ^ shift) for i in range(TOK)])


def share_mlp(payload):
    (place,) = yield [(payload, "sum")]
    (own,) = yield [(by_seq(place[0]), "sum seq")]
    return own


def by_seq_kernel(place_ref, out_ref):
    fill = jnp.zeros((HELD - 4 * SLOT, place_ref.shape[1]), BF16)
    for z in range(2):
        out_ref[z * HELD : z * HELD + 4 * SLOT] = place_ref[z * 4 * SLOT : (z + 1) * 4 * SLOT]
        out_ref[z * HELD + 4 * SLOT : (z + 1) * HELD] = fill
    out_ref[2 * HELD : 3 * HELD] = place_ref[8 * SLOT + HELD :]
    out_ref[3 * HELD :] = place_ref[8 * SLOT : 8 * SLOT + HELD]


def by_seq(place):
    return pl.pallas_call(
        by_seq_kernel,
        out_shape=jax.ShapeDtypeStruct((4 * HELD, place.shape[1]), BF16),
        name="by_seq",
    )(place)


def chip_kernel(slots, core_ref, *refs):
    *refs, out_ref = refs
    parts = len(refs) // 2
    rows = refs[0].shape[1] - slots
    if slots:
        core = core_ref[0]
        for ref, index in ((refs[0], core), (refs[1], 1 - core)):
            out_ref[:, pl.ds(pl.multiple_of(index * slots, slots), slots)] = ref[:, :slots]
    for part in range(parts):
        start = 2 * slots + part * rows
        mine_ref, came_ref = refs[part], refs[parts + part]
        out_ref[:, start : start + rows] = low(mine_ref[:, slots:], came_ref[:, slots:])


def by_chip(slots, core, mine, came):
    chips, rows, size = mine[0].shape
    block = lambda count: pl.BlockSpec((chips // 2, count, size), lambda i: (i, 0, 0))
    count = len(mine) * rows + slots
    return pl.pallas_call(
        partial(chip_kernel, slots),
        grid=(2,),
        in_specs=[pl.BlockSpec(memory_space=pltpu.SMEM)] + [block(rows)] * (2 * len(mine)),
        out_specs=block(count),
        out_shape=jax.ShapeDtypeStruct((chips, count, size), BF16),
        compiler_params=pltpu.CompilerParams(vmem_limit_bytes=16 * 2**20),
        name="by_chip",
    )(core, *mine, *came)


def share_heads_core(theirs):
    (came,) = yield [(theirs, across(1))]
    return came


def share_heads_plane(chips, skip=0):
    (came,) = yield [(chips, "chips")]
    return came, low(jnp.sum(came[:, skip:].astype(F32), axis=0))


def share_heads_seq(plane):
    z = lax.axis_index("seq")
    size = lax.axis_size("seq")
    part_of = lambda index: pick(plane, jnp.minimum(index, SEQS_IN - 1))
    came = yield [
        (part_of((z + step) % size), ("seq", [(i, (i + step) % size) for i in range(size)]))
        for step in range(1, size)
    ]
    return total(part_of(z), *came)


def share_attn(flat, slots):
    packed = jnp.stack(slots).astype(BF16)
    came = [lax.ppermute(packed, "tok", pairs) for pairs in flat.attn_rounds()]
    return came


def regroup(rows):
    (came,) = yield [(rows, "home")]
    return came


def tie(*values):
    leaves, tree = jax.tree.flatten(values)
    return jax.tree.unflatten(tree, lax.optimization_barrier(leaves))


class Moving:
    def __init__(self, chain):
        self.chain = chain
        self.result = None
        self.wanted = next(chain)

    def send(self, operands):
        moved = []
        for operand, (_, way) in zip(operands, self.wanted):
            if way in ("sum", "sum seq"):
                axis = "tok" if way == "sum" else "seq"
                moved.append(lax.psum_scatter(operand, axis, scatter_dimension=0, tiled=True))
            elif way == "chips":
                cores = [[2 * chip + core for chip in range(TOK // 2)] for core in range(2)]
                moved.append(
                    lax.all_to_all(
                        operand, "tok", split_axis=0, concat_axis=0, tiled=True, axis_index_groups=cores
                    )
                )
            elif way == "home":
                moved.append(lax.all_to_all(operand, "tok", split_axis=0, concat_axis=0, tiled=True))
            else:
                moved.append(lax.ppermute(operand, *way))
        return moved

    def take(self, moved):
        try:
            self.wanted = self.chain.send(moved)
        except StopIteration as end:
            self.wanted, self.result = None, end.value

    def finish(self):
        while self.wanted is not None:
            self.take(self.send([operand for operand, _ in self.wanted]))
        return self.result


def beside(work, inputs, moving, loose=()):
    chains = [*moving, *loose]
    operands = [[operand for operand, _ in chain.wanted] for chain in chains]
    inputs, operands = tie(inputs, operands)
    moved = [chain.send(operand) for chain, operand in zip(chains, operands)]
    done = work(*inputs)
    done, moved[: len(moving)] = tie(done, moved[: len(moving)])
    for chain, values in zip(chains, moved):
        chain.take(values)
    return done


def own_slice(flat, device, early, late, passed):
    width = flat.width

    def assemble(d, early, late, passed):
        early = early.astype(F32)
        passed = [values.astype(F32) for values in passed]
        z, place = divmod(d, TOK)
        first, end = flat.first(d), flat.first(d) + flat.rows
        pieces = []
        if first < 1:
            pieces.append((early[SLOT - 1] + late[-1][:, SLOT - 1].reshape(-1))[None])
        if first < flat.bias_at:
            columns = [slots[s] for s in range(3) for slots in late]
            columns += [early[c * SLOT : (c + 1) * SLOT] for c in range(flat.chunks)]
            base = 1 + flat.per_row * flat.input_row(d)
            rows = jnp.concatenate(columns, axis=1).reshape(-1, width)
            pieces.append(rows[max(first, 1) - base : min(end, flat.bias_at) - base])
        if first < flat.attn_at and end > flat.bias_at:
            at = 4 * SLOT
            pieces += [early[at + 16 * c][None] for c in range(flat.chunks)]
            for s in range(2):
                row = [slots[s, GAINS_ROW] for slots in late]
                pieces.append(jnp.concatenate(row)[None])
        if z == 2:
            for part, holder, at, count in flat.attn_pieces(place):
                source = late
                if holder != place:
                    pairs = flat.attn_rounds()
                    source = next(c for c, p in zip(passed, pairs) if (holder, place) in p)
                rows = source[part][:, at : at + count]
                pieces.append(jnp.concatenate([rows[s] for s in range(3)], axis=1))
        if end > flat.down_at:
            low = max(first, flat.down_at)
            start = flat.down_at + flat.down_start(d)
            pieces.append(early[low - start : end - start])
        rows = jnp.concatenate(pieces)
        skip = flat.skip(d)
        return rows.reshape(-1)[skip : skip + flat.total * width // flat.devices]

    branches = [partial(assemble, d) for d in range(flat.devices)]
    return lax.switch(device, branches, early, late, passed)


def sequence_device(
    layer_input,
    norm_gain,
    weight_in,
    bias_in,
    query_gain,
    key_gain,
    weight_attn,
    weight_down,
    bias_down,
    image_ids,
    cotangent,
):
    seqs, slots, width = layer_input.shape
    tok, z = lax.axis_index("tok"), lax.axis_index("seq")
    flat = Flat(width, weight_down.shape[0], lax.axis_size("seq") * TOK)
    features = jnp.array(flat.features(), jnp.int32)[:, None]

    def homeward(rows):
        return Moving(regroup(rows.reshape(seqs, slots, -1)))

    gain = norm_gain
    gains = (query_gain, key_gain)
    marks = jnp.pad(image_ids.astype(BF16)[:, None], ((0, 0), (0, 15), (0, width - slots)))
    rows = layer_input.reshape(seqs * slots, width)
    grads = cotangent.reshape(seqs * slots, width)
    moving = Moving(regroup(jnp.concatenate([layer_input, cotangent, marks], axis=1)))
    part_out, dn, payload = beside(
        partial(mlp, flat),
        (rows, grads, gain, weight_in, bias_in[None], weight_down, features),
        [moving],
    )
    came = moving.result
    early = Moving(share_mlp(payload))
    plane_sums = early.send([operand for operand, _ in early.wanted])
    query, key, value, grad_att, raw, perm, ids = heads(
        came, gain, weight_in, weight_attn, *gains, features
    )
    dn_heads = jnp.zeros((8, 128), F32)
    core = (tok % 2).astype(jnp.int32)[None]
    att = jnp.zeros((8, 128), BF16)

    def run(part, dn_heads, att, chains, loose=()):
        return beside(
            partial(attend_part, flat, part),
            (core, query, key, value, grad_att, ids, gains, raw, perm, weight_in, dn_heads, came, att),
            chains,
            loose,
        )

    dn_heads, mine_0, theirs_0 = run(0, dn_heads, att, [])
    core_0 = Moving(share_heads_core(theirs_0))
    dn_heads, att, mine_1, theirs_1 = run(1, dn_heads, att, [core_0])
    chips = by_chip(slots, core, [mine_0], [core_0.result])
    plane_0, core_1 = Moving(share_heads_plane(chips, 2 * slots)), Moving(share_heads_core(theirs_1))
    last, mine_2, theirs_2 = run(2, dn_heads, att, [core_1], [plane_0])
    first, plane_0 = plane_0.result
    core_2 = Moving(share_heads_core(theirs_2)).finish()
    both = by_chip(0, core, [mine_1, mine_2], [core_1.result, core_2])
    plane_sums, _ = tie(plane_sums, both)
    early.take(plane_sums)
    early.take(early.send([operand for operand, _ in early.wanted]))
    both = Moving(share_heads_plane(both))
    both.take(both.send([operand for operand, _ in both.wanted]))
    shape = (SEQS_IN, 3, SLOT, -1)
    before = Moving(share_heads_seq(plane_0.reshape(shape)))
    moved = before.send([operand for operand, _ in before.wanted])
    both, moved, last = tie(both.result[1], moved, last)
    before.take(moved)
    home = homeward(last)
    planes = [plane.reshape(shape) for plane in jnp.split(both, 2)]
    late = Moving(share_heads_seq(jnp.stack(planes, axis=1))).finish()
    late = [before.result, late[0], late[1]]
    passed = share_attn(flat, late)
    last = home.finish().reshape(seqs * slots, -1)
    out, grad_input = close(
        rows, grads, gain, weight_attn, part_out, bias_down, dn, first, last
    )
    out, grad_input, late, passed = tie(out, grad_input, late, passed)
    grad_weights = own_slice(flat, z * TOK + tok, early.finish(), late, passed)
    shape = (seqs, slots, width)
    return (out.reshape(shape), grad_input.reshape(shape), grad_weights)


def per_device(layer_input, *rest):
    seqs, slots, _ = layer_input.shape
    if lax.axis_size("tok") == seqs == 8 and lax.axis_size("seq") == 4 and slots % 16 == 0:
        return sequence_device(layer_input, *rest)
    return units_device(layer_input, *rest)


def solution(mesh):
    placed = (
        P("seq", "tok", None),
        P(),
        P(),
        P(),
        P(),
        P(),
        P(),
        P(),
        P(),
        P("seq", "tok"),
        P("seq", "tok", None),
    )
    return jax.shard_map(
        per_device,
        mesh=mesh,
        in_specs=placed,
        out_specs=(P("seq", "tok", None), P("seq", "tok", None), P(("seq", "tok"))),
        check_vma=False,
    )
```
